32 devices in a mesh: seq: 4 (over z), tensor: 8 (over y, x, core).
Axes of the slice: x: 2, y: 2, z: 4, core: 2. Of those that a mesh axis runs over, the one named last changes fastest.
Arguments:
- tokens: bfloat16 [4096, 1536], P(('seq', 'tensor')), may hold values from -6 to 6
- segment_ids: int32 [4096], P(('seq', 'tensor')), may hold values from 0 to 15, never falling along the last dimension, each value on 1 to 1024 neighbouring positions
- page_table: int32 [4, 64], P('seq'), may hold values from 0 to 63, each once within a row
- attn_gain: float32 [1536], replicated, may hold values from 0.6 to 6
- w_qkv: bfloat16 [1536, 2048], P(None, 'tensor'), may hold values from -0.15625 to 0.15625
- w_out: bfloat16 [1536, 1536], P(None, 'tensor'), may hold values from -0.15625 to 0.15625
- moe_gain: float32 [1536], replicated, may hold values from 0.25 to 1.75
- route_ids: int32 [4096, 4], P(('seq', 'tensor')), may hold values from 0 to 7, all different within a row; in each aligned block of 128 rows (0 to 127, 128 to 255, ...) at most 96 rows name the same one
- route_weight: float32 [4096, 4], P(('seq', 'tensor')), may hold values from 0.05 to 1
- w_gate: bfloat16 [8, 1536, 768], P('tensor'), may hold values from -0.15625 to 0.15625
- w_up: bfloat16 [8, 1536, 768], P('tensor'), may hold values from -0.15625 to 0.15625
- w_down: bfloat16 [8, 768, 1536], P('tensor'), may hold values from -0.21875 to 0.21875
Outputs:
- mixed: bfloat16 [4096, 1536], P(('seq', 'tensor'))
- cache: bfloat16 [256, 16, 512], P(('seq', 'tensor'))
The draws below stay inside these ranges and needn't reach their ends.
Inputs may be any that keep to these rules, and one draw needn't show every extreme that they name: `segment_ids`: segment numbers never fall along the tokens; every prompt spans 1 to 1024 tokens and one spans exactly 1024. `page_table`: each row is a permutation of the slots of one block. `route_ids`: each token names 4 different experts; among the rows of one device no expert is named more than 96 times, a bound that some block reaches.
All inputs are finite; a program needn't handle non-finite values.
Results may differ from the reference program's by a relative error of at most 0.012.
The reference program's roundings to bfloat16 on the way count: a program that leaves them out, or rounds other values in their place, can miss the bound.
Values may be sent and summed in bfloat16 or wider, within the bound.
No kernel may reach another device: no remote copies, remote signals or barrier semaphores. Data moves between devices by JAX's collectives and lax.ppermute only.
A program may use at most 128 MiB of HBM per device.

```python
import math
import jax
import jax.numpy as jnp
import numpy as np
from jax import lax

D = 1536
HEADS = 12
KV_HEADS = 2
HEAD = 128
EXP_HID = 768
TOP = 4
PAGE = 16
TOK_DEV = 128
EXPERTS = 8
TOK_SEQ = 1024
TOKENS = 4096
SEG_MOST = 1024
SEGS = 16
CAP = 96
QKVW = 2048
PAGES_SEQ = 64
PAGES = 256
N_SEQ = 4
N_TENSOR = 8


def draw_attn_gain(key, part):
    return jax.random.uniform(key, (D,), jnp.float32, 0.6, 1.6)


def block_scale(rng, shape, split, smallest, high):
    gain = 1.0
    for dim, shards_of in split:
        heights = jax.random.uniform(jax.random.fold_in(jax.random.fold_in(rng, 6), dim), (shards_of,), jnp.float32, smallest / len(split), high / len(split))
        gain = gain * jnp.repeat(jnp.exp(heights), shape[dim] // shards_of).reshape((-1,) + (1,) * (len(shape) - 1 - dim))
    return gain


def split_up(count, total, most, lean):
    loads = [(1 << 20) // math.isqrt(standing ** lean) + 1 for standing in range(2, count + 1)]
    rest, counts = total - most - (count - 1), [1] * (count - 1)
    while rest > 0:
        candidates = [i for i in range(count - 1) if counts[i] < most]
        pool, budget = sum([loads[i] for i in candidates]), rest
        for i in candidates:
            addition = min(most - counts[i], max(1, budget * loads[i] // pool), rest)
            counts[i] = counts[i] + addition
            rest = rest - addition
    return np.array([most] + counts)


def ragged(stream_key, number_of, total, limit, slope):
    if number_of == 2:
        one = jax.random.randint(stream_key, (), max(1, total - limit), min(limit, total - 1) + 1)
        return jnp.stack([one, total - one])
    sizes = jnp.asarray(split_up(number_of, total, limit, slope), jnp.int32)
    twos = (number_of - 1) // 2
    source_of, receiver = sizes[1:1 + 2 * twos:2], sizes[2:2 + 2 * twos:2]
    slack = jnp.minimum(source_of - 1, limit - receiver)
    passed = jax.random.randint(jax.random.fold_in(stream_key, 1), (twos,), 0, 1 << 20) % (slack + 1)
    sizes = sizes.at[1:1 + 2 * twos:2].set(source_of - passed).at[2:2 + 2 * twos:2].set(receiver + passed)
    return sizes[jax.random.permutation(jax.random.fold_in(stream_key, 2), number_of)]


def shared_out(stream_key, own, number, rows, count, top, limit, skew):
    sequence = jax.random.permutation(stream_key, count)
    heavy_load, common = portions_of(count, rows * top, limit, skew, True), portions_of(count, rows * top, limit, skew, False)
    places = jnp.arange(count)

    def named(sizes, offset_by):
        used = int((sizes > 0).sum())
        fixed = max(1, used // 4)
        passed = fixed + (places - fixed + offset_by * (used - fixed)) % max(1, count - fixed)
        return jnp.zeros((count,), jnp.int32).at[sequence[jnp.where(places < fixed, places, passed)]].set(jnp.asarray(sizes, jnp.int32))

    sizes = jnp.where(number % 4 == 0, named(heavy_load, number // 4), named(common, number - number // 4 - 1))
    mixed = jax.random.permutation(jax.random.fold_in(own, 3), count)
    giver, receiver = mixed[0:count // 2 * 2:2], mixed[1:count // 2 * 2:2]
    slack = jnp.minimum(sizes[giver] - 1, limit - sizes[receiver]) // 2
    slack = jnp.where((giver == sequence[0]) | (receiver == sequence[0]) | (sizes[receiver] == 0), 0, jnp.maximum(slack, 0))
    passed = jax.random.randint(jax.random.fold_in(own, 4), (count // 2,), 0, 1 << 20) % (slack + 1)
    sizes = sizes.at[giver].add(-passed).at[receiver].add(passed)
    items = jnp.searchsorted(jnp.cumsum(sizes), jnp.arange(rows * top), side="right").astype(jnp.int32)
    grid = items.reshape(top, rows).T
    grid = grid[jax.random.permutation(jax.random.fold_in(own, 1), rows)]
    offset_by = jax.random.randint(jax.random.fold_in(own, 2), (rows, 1), 0, top)
    return jnp.take_along_axis(grid, (jnp.arange(top)[None, :] + offset_by) % top, axis=1)


def portions_of(count, total, reach, skew, full):
    weights = [(1 << 20) // math.isqrt(rank ** skew) + 1 for rank in range(1, count + 1)]
    largest = reach if full else min(reach, max(-(-total // count), total * weights[0] // sum(weights)))
    least = 1 if total - largest >= count - 1 else 0
    holding, surplus = [largest] + [least] * (count - 1), total - largest - least * (count - 1)
    while surplus > 0:
        movable = [i for i in range(1, count) if holding[i] < largest] or [i for i in range(1, count) if holding[i] < reach]
        pool, remaining = sum([weights[i] for i in movable]), surplus
        for i in movable:
            addition = min(reach - holding[i], max(1, remaining * weights[i] // pool), surplus)
            holding[i] = holding[i] + addition
            surplus = surplus - addition
    return np.array(holding)


def gaussian(stream_key, shape, width, reach, shards=(), kind=jnp.bfloat16):
    factor_of = block_scale(stream_key, shape, shards, -0.22, 0.18) if shards else 1.0
    result = jax.random.normal(stream_key, shape, jnp.float32) * width * factor_of
    return jnp.minimum(jnp.maximum(result, -reach), reach).astype(kind)


def setup_inputs(seed: int = 0) -> dict:
    keys = jax.random.split(jax.random.key(seed), 13)
    tokens = gaussian(keys[0], (TOKENS, D), 1.0, 6.0, ((0, 32),))
    segment_ids = jnp.searchsorted(jnp.cumsum(ragged(keys[1], SEGS, TOKENS, SEG_MOST, 2)), jnp.arange(TOKENS), side="right").astype(jnp.int32)
    page_table = jax.vmap(lambda own: jax.random.permutation(own, PAGES_SEQ))(jax.random.split(keys[2], N_SEQ)).reshape((N_SEQ, PAGES_SEQ)).astype(jnp.int32)
    attn_gain = draw_attn_gain(jax.random.fold_in(keys[12], 71), 0)
    w_qkv = gaussian(keys[4], (D, QKVW), D ** -0.5, 0.15625, ((1, 8),))
    w_out = gaussian(keys[5], (HEADS * HEAD, D), (HEADS * HEAD) ** -0.5, 0.15625, ((1, 8),))
    moe_gain = jnp.clip(1.0 + 0.15 * jax.random.normal(keys[6], (D,), jnp.float32), 0.25, 1.75)
    route_ids_keys = jax.random.split(jax.random.fold_in(keys[7], 1), TOKENS // TOK_DEV)
    route_ids_turns = jax.random.permutation(jax.random.fold_in(keys[7], 3), TOKENS // TOK_DEV)
    route_ids = jax.vmap(lambda own, number: shared_out(jax.random.fold_in(keys[7], 2), own, number, TOK_DEV, EXPERTS, TOP, CAP, 2))(route_ids_keys, route_ids_turns).reshape((TOKENS, TOP))
    route_weight = jnp.clip(jnp.exp(math.log(1.0) - 2.9957323 * jax.random.uniform(keys[8], (TOKENS, TOP), jnp.float32) ** block_scale(keys[8], (TOKENS, TOP), ((0, 32),), -0.2, 0.2)), 0.05, 1.0)
    w_gate = gaussian(keys[9], (EXPERTS, D, EXP_HID), D ** -0.5, 0.15625, ((0, 8),))
    w_up = gaussian(keys[10], (EXPERTS, D, EXP_HID), D ** -0.5, 0.15625, ((0, 8),))
    w_down = gaussian(keys[11], (EXPERTS, EXP_HID, D), EXP_HID ** -0.5, 0.21875, ((0, 8),))
    return dict(tokens=tokens, segment_ids=segment_ids, page_table=page_table, attn_gain=attn_gain, w_qkv=w_qkv, w_out=w_out, moe_gain=moe_gain, route_ids=route_ids, route_weight=route_weight, w_gate=w_gate, w_up=w_up, w_down=w_down)


epsilon = 1e-06

def rms_scaled(values, scales):
    wide = values.astype(jnp.float32)
    mean_sq = lax.optimization_barrier(jnp.mean(wide * wide, axis=-1, keepdims=True))
    return (wide * lax.rsqrt(mean_sq + epsilon) * scales).astype(jnp.bfloat16)

def attend(queries, keys_window, values_window, allowed):
    scores = jnp.einsum('qhd,kd->hqk', queries.astype(jnp.float32), keys_window.astype(jnp.float32)) / math.sqrt(HEAD)
    scores = jnp.where(allowed[None], scores, -jnp.inf)
    highest = lax.optimization_barrier(jnp.max(scores, axis=-1, keepdims=True))
    weights = jnp.exp(scores - highest)
    totals = lax.optimization_barrier(jnp.sum(weights, axis=-1, keepdims=True))
    shares = (weights / totals).astype(jnp.bfloat16)
    return jnp.einsum('hqk,kd->qhd', shares.astype(jnp.float32), values_window.astype(jnp.float32))

def reference(tokens, segment_ids, page_table, attn_gain, w_qkv, w_out, moe_gain, route_ids, route_weight, w_gate, w_up, w_down):
    normed = rms_scaled(tokens, attn_gain)
    projected = jnp.dot(normed, w_qkv, preferred_element_type=jnp.float32).astype(jnp.bfloat16)
    query_width = HEADS * HEAD
    queries = projected[:, :query_width]
    all_kv = projected[:, query_width:]
    kv_width = all_kv.shape[1]
    pages = all_kv.reshape(N_SEQ, PAGES_SEQ, PAGE, kv_width)
    inverse = jnp.argsort(page_table, axis=1).astype(jnp.int32)
    cache = jnp.take_along_axis(pages, inverse[:, :, None, None], axis=1).reshape(PAGES, PAGE, kv_width)
    padded_kv = jnp.concatenate([jnp.zeros((TOK_SEQ, kv_width), jnp.bfloat16), all_kv], axis=0)
    padded_segs = jnp.concatenate([jnp.full((TOK_SEQ,), -1, jnp.int32), segment_ids], axis=0)
    window = TOK_SEQ + TOK_DEV
    per_group = HEADS // KV_HEADS

    def one_block(block_index):
        first_row = (block_index * TOK_DEV).astype(jnp.int32)
        keys_window = lax.dynamic_slice_in_dim(padded_kv, first_row, window, 0)
        segs_window = lax.dynamic_slice_in_dim(padded_segs, first_row, window, 0)
        query_rows = lax.dynamic_slice_in_dim(queries, first_row, TOK_DEV, 0).reshape(TOK_DEV, HEADS, HEAD)
        query_segs = lax.dynamic_slice_in_dim(segment_ids, first_row, TOK_DEV, 0)
        key_pos = first_row - TOK_SEQ + jnp.arange(window, dtype=jnp.int32)
        query_pos = first_row + jnp.arange(TOK_DEV, dtype=jnp.int32)
        allowed = (segs_window[None, :] == query_segs[:, None]) & (key_pos[None, :] <= query_pos[:, None])
        contexts = []
        for kv_group in range(KV_HEADS):
            key_cols = keys_window[:, kv_group * HEAD:(kv_group + 1) * HEAD]
            value_cols = keys_window[:, (KV_HEADS + kv_group) * HEAD:(KV_HEADS + kv_group + 1) * HEAD]
            contexts.append(attend(query_rows[:, kv_group * per_group:(kv_group + 1) * per_group], key_cols, value_cols, allowed))
        return jnp.concatenate(contexts, axis=1).reshape(TOK_DEV, query_width).astype(jnp.bfloat16)
    context = lax.map(one_block, jnp.arange(TOKENS // TOK_DEV, dtype=jnp.int32)).reshape(TOKENS, query_width)
    residual = (tokens.astype(jnp.float32) + jnp.dot(context, w_out, preferred_element_type=jnp.float32)).astype(jnp.bfloat16)
    expert_input = rms_scaled(residual, moe_gain)
    flat_routes = route_ids.reshape(-1)
    flat_weights = route_weight.reshape(-1)
    most_rows = N_SEQ * N_TENSOR * CAP

    def add_expert(running, expert_index):
        hits = flat_routes == expert_index
        counted = jnp.sum(hits.astype(jnp.int32))
        picked_pairs = jnp.nonzero(hits, size=most_rows, fill_value=0)[0].astype(jnp.int32)
        valid = jnp.arange(most_rows, dtype=jnp.int32) < counted
        pair_weights = jnp.where(valid, flat_weights[picked_pairs], jnp.zeros((), jnp.float32))
        token_rows = picked_pairs // TOP
        rows_in = expert_input[token_rows]
        gate_out = jnp.dot(rows_in, w_gate[expert_index], preferred_element_type=jnp.float32)
        up_out = jnp.dot(rows_in, w_up[expert_index], preferred_element_type=jnp.float32)
        hidden = (jnp.maximum(gate_out, 0.0) * up_out).astype(jnp.bfloat16)
        produced = jnp.dot(hidden, w_down[expert_index], preferred_element_type=jnp.float32).astype(jnp.bfloat16)
        return (running.at[token_rows].add(pair_weights[:, None] * produced.astype(jnp.float32)), None)
    summed = lax.scan(add_expert, jnp.zeros((TOKENS, D), jnp.float32), jnp.arange(EXPERTS, dtype=jnp.int32))[0]
    mixed = (residual.astype(jnp.float32) + summed).astype(jnp.bfloat16)
    return (mixed, cache)
```

```python
import functools
import math

import jax
import jax.numpy as jnp
from jax import lax
from jax.experimental import pallas as pl
from jax.experimental.pallas import tpu as pltpu
from jax.sharding import PartitionSpec as P

HEADS = 12
KV_HEADS = 2
HEAD = 128
TOP = 4
PAGE = 16
CORES = 2
CHIPS = 4


epsilon = 1e-06
MIB = 1024 * 1024


def vmem():
    return pl.BlockSpec(memory_space=pltpu.VMEM)


def anywhere():
    return pl.BlockSpec(memory_space=pl.ANY)


def params(mib):
    return pltpu.CompilerParams(vmem_limit_bytes=mib * MIB)


def place():
    index = lax.axis_index("tensor")
    return index // CORES, lax.rem(index, CORES)


def hop(value, by):
    length = lax.axis_size("tensor")
    return lax.ppermute(value, "tensor", [(i, i ^ by) for i in range(length)])


def chip_exchange(value):
    length = lax.axis_size("tensor")
    groups = [[i for i in range(length) if i % CORES == core] for core in range(CORES)]
    return lax.all_to_all(
        value, "tensor", split_axis=0, concat_axis=0, tiled=True, axis_index_groups=groups
    )


def norm_kernel(tokens_ref, gain_ref, out_ref):
    wide = tokens_ref[...].astype(jnp.float32)
    mean_sq = jnp.mean(wide * wide, axis=-1, keepdims=True)
    out_ref[...] = (wide * lax.rsqrt(mean_sq + epsilon) * gain_ref[...]).astype(jnp.bfloat16)


def norm_call(tokens, gain):
    return pl.pallas_call(
        norm_kernel,
        out_shape=jax.ShapeDtypeStruct(tokens.shape, jnp.bfloat16),
        in_specs=[vmem()] * 2,
        out_specs=vmem(),
        compiler_params=params(16),
        name="norm_tokens",
    )(tokens, gain.reshape(1, -1))


def transpose_kernel(in_ref, out_ref):
    out_ref[...] = in_ref[...].T


def transpose_call(value):
    return pl.pallas_call(
        transpose_kernel,
        out_shape=jax.ShapeDtypeStruct(value.shape[::-1], value.dtype),
        in_specs=[vmem()],
        out_specs=vmem(),
        compiler_params=params(16),
        name="transpose_w_out",
    )(value)


def project_kernel(own, by_x, by_y, by_xy, w_own, w_other, out_ref, rows_ref):
    chip, core = place()
    rows, cols = own.shape[0], w_own.shape[1]
    for hop_by, piece in enumerate((own, by_x, by_y, by_xy)):
        start = pl.multiple_of((chip ^ hop_by) * rows, rows)
        rows_ref[pl.ds(start, rows), :] = piece[...]
    for which, weights in ((core, w_own), (1 - core, w_other)):
        start = pl.multiple_of(which * cols, cols)
        out_ref[:, pl.ds(start, cols)] = jnp.dot(
            rows_ref[...], weights[...], preferred_element_type=jnp.float32
        ).astype(jnp.bfloat16)


def project_call(pieces, w_own, w_other):
    rows, width = pieces[0].shape
    return pl.pallas_call(
        project_kernel,
        out_shape=jax.ShapeDtypeStruct((CHIPS * rows, CORES * w_own.shape[1]), jnp.bfloat16),
        in_specs=[vmem()] * 6,
        out_specs=vmem(),
        scratch_shapes=[pltpu.VMEM((CHIPS * rows, width), jnp.bfloat16)],
        compiler_params=params(24),
        name="project",
    )(*pieces, w_own, w_other)


def attend_kernel(
    proj_ref, same_ref, other_ref, prev_ref, prev_other_ref, table_ref, out_ref,
    q_ref, s_ref, top_ref, sum_ref, acc_ref,
):
    chip, core = place()
    seq = lax.axis_index("seq")
    rows = prev_ref.shape[0]
    per_group = HEADS // KV_HEADS
    per_chip = HEADS // (CHIPS - 1)
    block_rows = rows * CORES * CHIPS
    n_table = table_ref.shape[0]
    experts = table_ref.shape[1] // 2
    me = seq * CORES * CHIPS + chip * CORES + core
    own_first = me * rows

    own_seg = jnp.broadcast_to(table_ref[me][experts : experts + 1, :], (rows, rows)).T
    before = jnp.zeros((rows, rows), jnp.float32)
    for i in range(n_table):
        row = table_ref[i][experts : experts + 1, :]
        before = before + jnp.where(row < own_seg, 1.0, 0.0)
    first_key = jnp.sum(before, axis=1, keepdims=True).astype(jnp.int32)
    query_pos = own_first + lax.broadcasted_iota(jnp.int32, (rows, 1), 0)
    lowest = jnp.min(first_key)
    lane = lax.broadcasted_iota(jnp.int32, (rows, rows), 1)

    for head in range(HEADS):
        j, i = head // per_chip, head % per_chip
        q_ref[head * rows : (head + 1) * rows, :] = proj_ref[
            j * rows : (j + 1) * rows, i * HEAD : (i + 1) * HEAD
        ]

    blocks = []
    for ref, which in ((same_ref, core), (other_ref, 1 - core)):
        for j in range(CHIPS):
            base = jnp.where(j <= chip, seq, seq - 1) * block_rows
            blocks.append((ref, j * rows, base + (j * CORES + which) * rows))
    for ref, which in ((prev_ref, core), (prev_other_ref, 1 - core)):
        blocks.append((ref, 0, (seq - 1) * block_rows + (chip * CORES + which) * rows))

    scale = math.log2(math.e) / math.sqrt(HEAD)
    group_rows = per_group * rows
    top_ref[...] = jnp.full(top_ref.shape, -jnp.inf, jnp.float32)
    sum_ref[...] = jnp.zeros(sum_ref.shape, jnp.float32)
    acc_ref[...] = jnp.zeros(acc_ref.shape, jnp.float32)
    used = []
    for n, (ref, row0, first) in enumerate(blocks):
        use = (first <= own_first) & (first + rows > lowest)
        used.append(use)

        @pl.when(use)
        def _(n=n, ref=ref, row0=row0, first=first):
            key_pos = first + lane
            bias = jnp.where((key_pos >= first_key) & (key_pos <= query_pos), 0.0, -jnp.inf)
            for g in range(KV_HEADS):
                keys = ref[row0 : row0 + rows, g * HEAD : (g + 1) * HEAD]
                scores = lax.dot_general(
                    q_ref[g * group_rows : (g + 1) * group_rows, :], keys,
                    (((1,), (1,)), ((), ())), preferred_element_type=jnp.float32,
                )
                scores = (scores.reshape(per_group, rows, rows) * scale + bias[None]).reshape(
                    group_rows, rows
                )
                s_ref[n, g * group_rows : (g + 1) * group_rows, :] = scores
                part = top_ref.at[g * group_rows : (g + 1) * group_rows, :]
                part[...] = jnp.maximum(part[...], scores)

    top_ref[...] = jnp.broadcast_to(
        jnp.max(top_ref[...], axis=1, keepdims=True), top_ref.shape
    )
    for n, (ref, row0, first) in enumerate(blocks):

        @pl.when(used[n])
        def _(n=n, ref=ref, row0=row0):
            for g in range(KV_HEADS):
                part = slice(g * group_rows, (g + 1) * group_rows)
                weights = jnp.exp2(s_ref[n, part, :] - top_ref[part, :])
                sum_ref[part, :] += weights
                values = ref[row0 : row0 + rows, (KV_HEADS + g) * HEAD : (KV_HEADS + g + 1) * HEAD]
                acc_ref[part, :] += jnp.dot(
                    weights.astype(jnp.bfloat16), values, preferred_element_type=jnp.float32
                )

    for head in range(HEADS):
        part = slice(head * rows, (head + 1) * rows)
        total = jnp.sum(sum_ref[part, :], axis=1, keepdims=True)
        out_ref[:, head * HEAD : (head + 1) * HEAD] = (acc_ref[part, :] / total).astype(
            jnp.bfloat16
        )


def attend_call(projected, same, other, prev, prev_other, table):
    rows = prev.shape[0]
    wide = HEADS * rows
    return pl.pallas_call(
        attend_kernel,
        out_shape=jax.ShapeDtypeStruct((rows, HEADS * HEAD), jnp.bfloat16),
        in_specs=[vmem()] * 6,
        out_specs=vmem(),
        scratch_shapes=[
            pltpu.VMEM((wide, HEAD), jnp.bfloat16),
            pltpu.VMEM((2 * CHIPS + 2, wide, rows), jnp.float32),
            pltpu.VMEM((wide, rows), jnp.float32),
            pltpu.VMEM((wide, rows), jnp.float32),
            pltpu.VMEM((wide, HEAD), jnp.float32),
        ],
        compiler_params=params(32),
        name="attend",
    )(projected, same, other, prev, prev_other, table)


def residual_kernel(*refs):
    same, other = refs[:CHIPS], refs[CHIPS : 2 * CHIPS]
    context_ref, tokens_ref, gain_ref, residual_ref, out_ref, w_ref, sem = refs[2 * CHIPS :]
    chip, core = place()
    cols = same[0].shape[0]
    copies = []
    for pieces, which in ((same, core), (other, 1 - core)):
        for hop_by, piece in enumerate(pieces):
            start = pl.multiple_of(((chip ^ hop_by) * CORES + which) * cols, cols)
            copies.append(
                pltpu.make_async_copy(
                    piece, w_ref.at[pl.ds(start, cols), :], sem.at[len(copies)]
                )
            )
    for copy in copies:
        copy.start()
    for copy in copies:
        copy.wait()
    added = lax.dot_general(
        context_ref[...], w_ref[...], (((1,), (1,)), ((), ())), preferred_element_type=jnp.float32
    )
    residual = (tokens_ref[...].astype(jnp.float32) + added).astype(jnp.bfloat16)
    residual_ref[...] = residual
    wide = residual.astype(jnp.float32)
    mean_sq = jnp.mean(wide * wide, axis=-1, keepdims=True)
    out_ref[...] = (wide * lax.rsqrt(mean_sq + epsilon) * gain_ref[...]).astype(jnp.bfloat16)


def residual_call(w_same, w_other, context, tokens, gain):
    cols, depth = w_same[0].shape
    shape = jax.ShapeDtypeStruct(tokens.shape, jnp.bfloat16)
    return pl.pallas_call(
        residual_kernel,
        out_shape=(shape, shape),
        in_specs=[anywhere()] * (2 * CHIPS) + [vmem()] * 3,
        out_specs=(vmem(), vmem()),
        scratch_shapes=[
            pltpu.VMEM((2 * CHIPS * cols, depth), jnp.bfloat16),
            pltpu.SemaphoreType.DMA((2 * CHIPS,)),
        ],
        compiler_params=params(24),
        name="residual",
    )(*w_same, *w_other, context, tokens, gain.reshape(1, -1))


def expert_kernel(
    steps, own, by_x, by_y, by_xy, table_ref,
    gate_own, up_own, down_own, gate_other, up_other, down_other,
    out_own, out_x, out_y, out_xy, rows_ref, acc_ref, total_ref,
):
    chip, core = place()
    seq = lax.axis_index("seq")
    rows = own.shape[0]
    experts = table_ref.shape[1] // 2
    step = pl.program_id(0)

    @pl.when(step == 0)
    def _():
        for hop_by, piece in enumerate((own, by_x, by_y, by_xy)):
            rows_ref[hop_by * rows : (hop_by + 1) * rows, :] = piece[...]

    def part(gate, up, down, first):
        gate_out = jnp.dot(rows_ref[...], gate[...], preferred_element_type=jnp.float32)
        up_out = jnp.dot(rows_ref[...], up[...], preferred_element_type=jnp.float32)
        hidden = (jnp.maximum(gate_out, 0.0) * up_out).astype(jnp.bfloat16)
        made = jnp.dot(hidden, down[...], preferred_element_type=jnp.float32)

        @pl.when(step == first)
        def _():
            acc_ref[...] = made

        @pl.when(step != first)
        def _():
            acc_ref[...] += made

    def weight_of(hop_by, which):
        expert = chip * CORES + which
        block = table_ref[(seq * CHIPS + (chip ^ hop_by)) * CORES + core]
        row_id = lax.broadcasted_iota(jnp.int32, block.shape, 0)
        row = jnp.sum(jnp.where(row_id == expert, block, 0.0), axis=0, keepdims=True)
        return jnp.broadcast_to(row, (rows, rows)).T[:, :1]

    @pl.when(step < steps)
    def _():
        part(gate_own, up_own, down_own, 0)

    @pl.when(step >= steps)
    def _():
        part(gate_other, up_other, down_other, steps)

    @pl.when(step == steps - 1)
    def _():
        for hop_by in range(CHIPS):
            span = slice(hop_by * rows, (hop_by + 1) * rows)
            made = acc_ref[span, :].astype(jnp.bfloat16).astype(jnp.float32)
            total_ref[span, :] = weight_of(hop_by, core) * made

    @pl.when(step == 2 * steps - 1)
    def _():
        for hop_by, out_ref in enumerate((out_own, out_x, out_y, out_xy)):
            span = slice(hop_by * rows, (hop_by + 1) * rows)
            made = acc_ref[span, :].astype(jnp.bfloat16).astype(jnp.float32)
            out_ref[...] = (total_ref[span, :] + weight_of(hop_by, 1 - core) * made).astype(
                out_ref.dtype
            )


def expert_call(pieces, table, own_weights, other_weights):
    rows, width = pieces[0].shape
    hidden = own_weights[0].shape[1]
    tile = 256
    steps = hidden // tile

    def own_tile(i):
        return jnp.minimum(i, steps - 1)

    def other_tile(i):
        return jnp.maximum(i - steps, 0)

    def weight_specs(tile_of):
        return [
            pl.BlockSpec((width, tile), lambda i: (0, tile_of(i))),
            pl.BlockSpec((width, tile), lambda i: (0, tile_of(i))),
            pl.BlockSpec((tile, width), lambda i: (tile_of(i), 0)),
        ]

    whole = pl.BlockSpec((rows, width), lambda i: (0, 0))
    return pl.pallas_call(
        functools.partial(expert_kernel, steps),
        grid=(2 * steps,),
        out_shape=tuple(
            jax.ShapeDtypeStruct((rows, width), kind)
            for kind in (jnp.float32, jnp.bfloat16, jnp.bfloat16, jnp.bfloat16)
        ),
        in_specs=[whole] * CHIPS
        + [pl.BlockSpec(table.shape, lambda i: (0, 0, 0))]
        + weight_specs(own_tile)
        + weight_specs(other_tile),
        out_specs=(whole,) * CHIPS,
        scratch_shapes=[
            pltpu.VMEM((CHIPS * rows, width), jnp.bfloat16),
            pltpu.VMEM((CHIPS * rows, width), jnp.float32),
            pltpu.VMEM((CHIPS * rows, width), jnp.float32),
        ],
        compiler_params=params(40),
        name="experts",
    )(*pieces, table, *own_weights, *other_weights)


def mix_kernel(residual_ref, own, by_x, by_y, by_xy, out_ref):
    total = own[...] + by_x[...].astype(jnp.float32)
    total = total + by_y[...].astype(jnp.float32) + by_xy[...].astype(jnp.float32)
    out_ref[...] = (residual_ref[...].astype(jnp.float32) + total).astype(jnp.bfloat16)


def mix_call(residual, pieces):
    return pl.pallas_call(
        mix_kernel,
        out_shape=jax.ShapeDtypeStruct(residual.shape, jnp.bfloat16),
        in_specs=[vmem()] * 5,
        out_specs=vmem(),
        compiler_params=params(16),
        name="mix",
    )(residual, *pieces)


def cache_kernel(table_ref, kv_ref, out_ref):
    pages = out_ref.shape[0]
    index = lax.axis_index("tensor")

    def one(logical, carry):
        slot = table_ref[0, logical]

        @pl.when(slot // pages == index)
        def _():
            start = pl.multiple_of(logical * PAGE, PAGE)
            out_ref[lax.rem(slot, pages)] = kv_ref[pl.ds(start, PAGE), :]

        return carry

    lax.fori_loop(0, table_ref.shape[1], one, 0)


def cache_call(page_table, block_kv, pages):
    return pl.pallas_call(
        cache_kernel,
        out_shape=jax.ShapeDtypeStruct((pages, PAGE, block_kv.shape[1]), jnp.bfloat16),
        in_specs=[pl.BlockSpec(memory_space=pltpu.SMEM), vmem()],
        out_specs=vmem(),
        compiler_params=params(16),
        name="cache_pages",
    )(page_table, block_kv)


def chip_body(
    tokens, segment_ids, page_table, attn_gain, w_qkv, w_out, moe_gain,
    route_ids, route_weight, w_gate, w_up, w_down,
):
    rows = tokens.shape[0]
    seq_size = lax.axis_size("seq")
    experts = lax.axis_size("tensor") * w_gate.shape[0]
    chip, core = place()

    normed = norm_call(tokens, attn_gain)
    pieces = [normed] + [hop(normed, CORES * by) for by in (1, 2, 3)]
    w_qkv_other = hop(w_qkv, 1)
    expert_own = [w_gate[0], w_up[0], w_down[0]]
    expert_other = [hop(w, 1) for w in expert_own]

    routes, weights, segs, _ = lax.optimization_barrier(
        (route_ids, route_weight, segment_ids, normed)
    )
    named = routes.T[:, None, :] == jnp.arange(experts, dtype=jnp.int32)[None, :, None]
    spread = jnp.sum(jnp.where(named, weights.T[:, None, :], 0.0), axis=0)
    seg_rows = jnp.broadcast_to(segs.astype(jnp.float32)[None, :], (experts, rows))
    table = lax.all_gather(
        jnp.concatenate([spread, seg_rows], axis=0), ("seq", "tensor"), axis=0, tiled=False
    )

    projected = chip_exchange(project_call(pieces, w_qkv, w_qkv_other))
    own_kv = projected[(CHIPS - 1) * rows :]
    prev_kv = lax.ppermute(own_kv, "seq", [(i, i + 1) for i in range(seq_size - 1)])
    going = jnp.where(
        (jnp.arange(CHIPS, dtype=jnp.int32) < chip)[:, None, None], prev_kv[None], own_kv[None]
    ).reshape(CHIPS * rows, own_kv.shape[1])
    same_kv = chip_exchange(going)
    other_kv = hop(same_kv, 1)
    prev_other = hop(prev_kv, 1)
    context = attend_call(projected, same_kv, other_kv, prev_kv, prev_other, table)

    w_out_own, _ = lax.optimization_barrier((transpose_call(w_out), projected))
    w_out_same = [w_out_own] + [hop(w_out_own, CORES * by) for by in (1, 2, 3)]
    w_out_other = [hop(w, 1) for w in w_out_same]
    residual, expert_input = residual_call(w_out_same, w_out_other, context, tokens, moe_gain)

    inputs = [expert_input] + [hop(expert_input, CORES * by) for by in (1, 2, 3)]
    made = expert_call(inputs, table, expert_own, expert_other)
    returned = [made[0]] + [hop(made[by], CORES * by) for by in (1, 2, 3)]
    mixed = mix_call(residual, returned)

    block_kv = lax.all_gather(own_kv, "tensor", axis=0, tiled=True)
    cache = cache_call(page_table, block_kv, rows // PAGE)
    return (mixed, cache)


def from_behind(value, axis, by):
    length = lax.axis_size(axis)
    pairs = [(i, i + by) for i in range(length) if 0 <= i + by < length]
    return lax.ppermute(value, axis, pairs)


def rms_scaled(values, scales):
    wide = values.astype(jnp.float32)
    mean_sq = jnp.mean(wide * wide, axis=-1, keepdims=True)
    return (wide * lax.rsqrt(mean_sq + epsilon) * scales).astype(jnp.bfloat16)


def attend(queries, keys_window, values_window, allowed):
    scores = jnp.einsum(
        "qhd,kd->hqk", queries, keys_window, preferred_element_type=jnp.float32
    ) / math.sqrt(queries.shape[-1])
    scores = jnp.where(allowed[None], scores, -jnp.inf)
    highest = jnp.max(scores, axis=-1, keepdims=True)
    weights = jnp.exp(scores - highest)
    totals = jnp.sum(weights, axis=-1, keepdims=True)
    shares = (weights / totals).astype(jnp.bfloat16)
    return jnp.einsum("hqk,kd->qhd", shares, values_window, preferred_element_type=jnp.float32)


def block_body(
    tokens,
    segment_ids,
    page_table,
    attn_gain,
    w_qkv,
    w_out,
    moe_gain,
    route_ids,
    route_weight,
    w_gate,
    w_up,
    w_down,
):
    tok_rows = tokens.shape[0]
    tensor_size = lax.axis_size("tensor")
    tensor_index = lax.axis_index("tensor")
    seq_index = lax.axis_index("seq")
    block_rows = tok_rows * tensor_size
    normed = rms_scaled(tokens, attn_gain)
    block_normed = lax.all_gather(normed, "tensor", axis=0, tiled=True)
    own_columns = jnp.dot(block_normed, w_qkv, preferred_element_type=jnp.float32).astype(
        jnp.bfloat16
    )
    projected = lax.all_to_all(own_columns, "tensor", split_axis=0, concat_axis=1, tiled=True)
    query_width = HEADS * HEAD
    queries = projected[:, :query_width].reshape(tok_rows, HEADS, HEAD)
    own_kv = projected[:, query_width:]
    block_kv, block_segs = (
        lax.all_gather(own_kv, "tensor", axis=0, tiled=True),
        lax.all_gather(segment_ids, "tensor", axis=0, tiled=True),
    )
    earlier_kv, earlier_seg_block = from_behind((block_kv, block_segs), "seq", 1)
    pages_here = tok_rows // PAGE
    pages_block = block_rows // PAGE
    slot_ids = tensor_index * pages_here + jnp.arange(pages_here, dtype=jnp.int32)
    matches = page_table[0][None, :] == slot_ids[:, None]
    logical = jnp.sum(
        jnp.where(matches, jnp.arange(pages_block, dtype=jnp.int32)[None, :], 0), axis=1
    )
    cache_pages = block_kv.reshape(pages_block, PAGE, block_kv.shape[1])[logical]
    all_kv = jnp.concatenate([earlier_kv, block_kv], axis=0)
    all_segs = jnp.concatenate([earlier_seg_block, block_segs], axis=0)
    window = block_rows + tok_rows
    first_key = tensor_index * tok_rows
    keys_window = lax.dynamic_slice_in_dim(all_kv, first_key, window, 0)
    segs_window = lax.dynamic_slice_in_dim(all_segs, first_key, window, 0)
    key_pos = (seq_index - 1) * block_rows + first_key + jnp.arange(window, dtype=jnp.int32)
    query_pos = seq_index * block_rows + first_key + jnp.arange(tok_rows, dtype=jnp.int32)
    allowed = (
        (segs_window[None, :] == segment_ids[:, None])
        & (key_pos[None, :] <= query_pos[:, None])
        & (key_pos[None, :] >= 0)
    )
    per_group = HEADS // KV_HEADS
    contexts = []
    for kv_group in range(KV_HEADS):
        key_cols = keys_window[:, kv_group * HEAD : (kv_group + 1) * HEAD]
        value_cols = keys_window[:, (KV_HEADS + kv_group) * HEAD : (KV_HEADS + kv_group + 1) * HEAD]
        contexts.append(
            attend(
                queries[:, kv_group * per_group : (kv_group + 1) * per_group],
                key_cols,
                value_cols,
                allowed,
            )
        )
    context = jnp.concatenate(contexts, axis=1).reshape(tok_rows, query_width).astype(jnp.bfloat16)
    attn_out = jnp.dot(
        context,
        lax.all_gather(w_out, "tensor", axis=1, tiled=True),
        preferred_element_type=jnp.float32,
    )
    residual = (tokens.astype(jnp.float32) + attn_out).astype(jnp.bfloat16)
    expert_input = rms_scaled(residual, moe_gain)
    experts_all = w_gate.shape[0] * tensor_size
    capacity = max(2, 3 * tok_rows * TOP // (2 * experts_all))
    flat_routes = route_ids.reshape(-1)
    expert_hits = (
        flat_routes[:, None] == jnp.arange(experts_all, dtype=jnp.int32)[None, :]
    ).astype(jnp.int32)
    earlier_hits = jnp.cumsum(expert_hits, axis=0) - expert_hits
    slot_rank = jnp.sum(earlier_hits * expert_hits, axis=1)
    dest_slot = flat_routes * capacity + slot_rank
    slot_table = (
        jnp.arange(experts_all * capacity, dtype=jnp.int32)[:, None, None]
        == dest_slot.reshape(tok_rows, TOP)[None]
    )
    dispatch = jnp.any(slot_table, axis=2).astype(jnp.bfloat16)
    outgoing = jnp.dot(dispatch, expert_input, preferred_element_type=jnp.float32).astype(
        jnp.bfloat16
    )
    outgoing = outgoing.reshape(experts_all, capacity, expert_input.shape[1])
    arrived = lax.all_to_all(outgoing, "tensor", split_axis=0, concat_axis=0, tiled=True)
    rows_flat = arrived.reshape(-1, arrived.shape[-1])
    gate_out = jnp.dot(rows_flat, w_gate[0], preferred_element_type=jnp.float32)
    up_out = jnp.dot(rows_flat, w_up[0], preferred_element_type=jnp.float32)
    hidden = (jnp.maximum(gate_out, 0.0) * up_out).astype(jnp.bfloat16)
    produced = jnp.dot(hidden, w_down[0], preferred_element_type=jnp.float32).astype(jnp.bfloat16)
    returned = lax.all_to_all(
        produced.reshape(arrived.shape), "tensor", split_axis=0, concat_axis=0, tiled=True
    )
    picked = returned.reshape(-1, returned.shape[-1])[dest_slot].reshape(
        tok_rows, TOP, returned.shape[-1]
    )
    routed_sum = jnp.einsum("tk,tkd->td", route_weight, picked.astype(jnp.float32))
    mixed = (residual.astype(jnp.float32) + routed_sum).astype(jnp.bfloat16)
    return (mixed, cache_pages)


def by_chips(mesh):
    size = mesh.shape["tensor"]
    return size == CORES * CHIPS and (HEADS + 2 * KV_HEADS) % size == 0


def solution(mesh):
    return jax.shard_map(
        chip_body if by_chips(mesh) else block_body,
        mesh=mesh,
        in_specs=(
            P(("seq", "tensor"), None),
            P(("seq", "tensor")),
            P("seq", None),
            P(),
            P(None, "tensor"),
            P(None, "tensor"),
            P(),
            P(("seq", "tensor"), None),
            P(("seq", "tensor"), None),
            P("tensor", None, None),
            P("tensor", None, None),
            P("tensor", None, None),
        ),
        out_specs=(P(("seq", "tensor"), None), P(("seq", "tensor"), None, None)),
        check_vma=False,
    )
```

```python
import functools
import math

import jax
import jax.numpy as jnp
from jax import lax
from jax.experimental import pallas as pl
from jax.experimental.pallas import tpu as pltpu
from jax.sharding import PartitionSpec as P

HEADS = 12
KV_HEADS = 2
HEAD = 128
TOP = 4
PAGE = 16
CORES = 2
CHIPS = 4


epsilon = 1e-06
MIB = 1024 * 1024


LONG = pl.CostEstimate(flops=20 * 10**9, bytes_accessed=1, transcendentals=0)


ORDER = (0, 3, 1, 2)


def vmem():
    return pl.BlockSpec(memory_space=pltpu.VMEM)


def anywhere():
    return pl.BlockSpec(memory_space=pl.ANY)


def params(mib):
    return pltpu.CompilerParams(vmem_limit_bytes=mib * MIB)


def place():
    index = lax.axis_index("tensor")
    return index // CORES, lax.rem(index, CORES)


def hop(value, by):
    length = lax.axis_size("tensor")
    return lax.ppermute(value, "tensor", [(i, i ^ by) for i in range(length)])


def rms_rows(wide, gain_ref):
    mean_sq = jnp.mean(wide * wide, axis=-1, keepdims=True)
    return (wide * lax.rsqrt(mean_sq + epsilon) * gain_ref[...]).astype(jnp.bfloat16)


def project_kernel(first, second, gain_ref, w_own, w_other, out_ref, rows_ref):
    core = place()[1]
    rows, cols = first.shape[0], w_own.shape[1]
    rows_ref[:rows, :] = rms_rows(first[...].astype(jnp.float32), gain_ref)
    rows_ref[rows:, :] = rms_rows(second[...].astype(jnp.float32), gain_ref)
    for which, weights in ((core, w_own), (1 - core, w_other)):
        span = pl.ds(pl.multiple_of(which * cols, cols), cols)
        out_ref[:, span] = jnp.dot(
            rows_ref[...], weights[...], preferred_element_type=jnp.float32
        ).astype(jnp.bfloat16)


def project_call(first, second, gain, w_own, w_other):
    rows, width = first.shape
    return pl.pallas_call(
        project_kernel,
        out_shape=jax.ShapeDtypeStruct((2 * rows, CORES * w_own.shape[1]), jnp.bfloat16),
        in_specs=[vmem()] * 5,
        out_specs=vmem(),
        scratch_shapes=[pltpu.VMEM((2 * rows, width), jnp.bfloat16)],
        cost_estimate=LONG,
        compiler_params=params(16),
        name="project",
    )(first, second, gain, w_own, w_other)


def pack_kernel(own, by_x, by_y, by_xy, segs_ref, routes_ref, shares_ref, out_ref):
    chip = place()[0]
    rows, width = own.shape
    for hop_by, piece in enumerate((own, by_x, by_y, by_xy)):

        @pl.when(chip ^ hop_by == CHIPS - 1)
        def _(piece=piece):
            out_ref[:rows, :] = piece[...]

    experts = PAGE // 2
    named = lax.broadcasted_iota(jnp.int32, (experts, rows), 0)
    table = jnp.zeros((experts, rows), jnp.float32)
    for k in range(TOP):
        routed = jnp.broadcast_to(routes_ref[k : k + 1, :], (experts, rows)) == named
        table = table + jnp.where(routed, shares_ref[k : k + 1, :], 0.0)
    segs = jnp.broadcast_to(segs_ref[...].astype(jnp.float32), (experts, rows))
    out_ref[rows:, :rows] = jnp.concatenate([segs, table], axis=0).astype(jnp.bfloat16)
    for part in (1, 2):
        table = table - table.astype(jnp.bfloat16).astype(jnp.float32)
        out_ref[rows:, part * rows : (part + 1) * rows] = jnp.concatenate(
            [segs, table], axis=0
        ).astype(jnp.bfloat16)
    out_ref[rows:, 3 * rows :] = jnp.zeros((PAGE, width - 3 * rows), jnp.bfloat16)


def pack_call(pieces, segment_ids, routes, shares):
    rows, width = pieces[0].shape
    return pl.pallas_call(
        pack_kernel,
        out_shape=jax.ShapeDtypeStruct((rows + PAGE, width), jnp.bfloat16),
        in_specs=[vmem()] * (CHIPS + 3),
        out_specs=vmem(),
        compiler_params=params(16),
        name="pack_kv",
    )(*pieces, segment_ids.reshape(1, rows), routes.T, shares.T)


def choose_kernel(own, prev, *out_refs):
    chip = place()[0]
    rows = own.shape[0] - PAGE
    row_id = lax.broadcasted_iota(jnp.int32, (PAGE, own.shape[1]), 0)
    for hop_by, out_ref in enumerate(out_refs, 1):
        later = (chip ^ hop_by) > chip

        @pl.when(later)
        def _(out_ref=out_ref):
            out_ref[...] = own[...]

        @pl.when(jnp.logical_not(later))
        def _(out_ref=out_ref):
            out_ref[:rows, :] = prev[:rows, :]
            below, mine = prev[rows:, :].astype(jnp.float32), own[rows:, :].astype(jnp.float32)
            out_ref[rows:, :] = jnp.where(row_id < PAGE // 2, below, mine).astype(jnp.bfloat16)


def choose_call(own, prev):
    return pl.pallas_call(
        choose_kernel,
        out_shape=(jax.ShapeDtypeStruct(own.shape, own.dtype),) * (CHIPS - 1),
        in_specs=[vmem()] * 2,
        out_specs=(vmem(),) * (CHIPS - 1),
        compiler_params=params(16),
        name="choose_kv",
    )(own, prev)


def attend_kernel(*refs):
    projected, refs = refs[:CHIPS], refs[CHIPS:]
    windows, refs = refs[: 2 * (CHIPS + 1)], refs[2 * (CHIPS + 1) :]
    out_ref, q_ref, s_ref, top_ref, sum_ref, acc_ref = refs
    chip, core = place()
    seq = lax.axis_index("seq")
    rows = out_ref.shape[0]
    per_group = HEADS // KV_HEADS
    per_chip = HEADS // (CHIPS - 1)
    block_rows = rows * CORES * CHIPS
    own_first = seq * block_rows + (chip * CORES + core) * rows

    def segs_of(ref):
        return ref[rows : rows + 1, :rows].astype(jnp.float32)

    own_segs = segs_of(windows[0])
    query_seg = jnp.broadcast_to(own_segs, (rows, rows)).T
    query_pos = lax.broadcasted_iota(jnp.int32, (rows, rows), 0) + own_first
    lane = lax.broadcasted_iota(jnp.int32, (rows, rows), 1)
    lowest = jnp.min(own_segs)

    for hop_by, piece in enumerate(projected):
        source = chip ^ hop_by

        @pl.when(source < CHIPS - 1)
        def _(source=source, piece=piece):
            for i in range(per_chip):
                start = pl.multiple_of((source * per_chip + i) * rows, rows)
                q_ref[pl.ds(start, rows), :] = piece[:, i * HEAD : (i + 1) * HEAD]

    pairs = []
    for n in range(CHIPS + 1):
        if n == 0:
            base, source = seq, chip
        elif n == CHIPS:
            base, source = seq - 1, chip
        else:
            source = chip ^ n
            base = jnp.where(source < chip, seq, seq - 1)
        first = base * block_rows + source * CORES * rows
        refs = (windows[n], windows[n + CHIPS + 1])
        pairs.append((refs, (first + core * rows, first + (1 - core) * rows)))

    scale = math.log2(math.e) / math.sqrt(HEAD)
    group_rows = per_group * rows
    used = []
    for n, (refs, firsts) in enumerate(pairs):
        use = (firsts[0] >= 0) & (firsts[0] <= own_first)
        last_seg = jnp.max(jnp.maximum(segs_of(refs[0]), segs_of(refs[1])))
        used.append(use & (last_seg >= lowest))

        def scores_of(n=n, refs=refs, firsts=firsts):
            bias = []
            for ref, first in zip(refs, firsts):
                allowed = (segs_of(ref) == query_seg) & (first + lane <= query_pos)
                bias.append(jnp.where(allowed, 0.0, -jnp.inf))
            bias = jnp.concatenate(bias, axis=1)
            for g in range(KV_HEADS):
                span = slice(g * HEAD, (g + 1) * HEAD)
                keys = jnp.concatenate([ref[:rows, span] for ref in refs], axis=0)
                part = slice(g * group_rows, (g + 1) * group_rows)
                scores = lax.dot_general(
                    q_ref[part, :], keys, (((1,), (1,)), ((), ())),
                    preferred_element_type=jnp.float32,
                )
                scores = scores.reshape(per_group, rows, 2 * rows) * scale + bias[None]
                scores = scores.reshape(group_rows, 2 * rows)
                s_ref[n, part, :] = scores
                high = jnp.maximum(scores[:, :rows], scores[:, rows:])
                top_ref[part, :] = high if n == 0 else jnp.maximum(top_ref[part, :], high)

        if n == 0:
            scores_of()
        else:
            pl.when(used[n])(scores_of)

    top_ref[...] = jnp.broadcast_to(jnp.max(top_ref[...], axis=1, keepdims=True), top_ref.shape)
    for n, (refs, firsts) in enumerate(pairs):

        def weigh(n=n, refs=refs):
            for g in range(KV_HEADS):
                part = slice(g * group_rows, (g + 1) * group_rows)
                top = top_ref[part, :]
                weights = jnp.exp2(s_ref[n, part, :] - jnp.concatenate([top, top], axis=1))
                span = slice((KV_HEADS + g) * HEAD, (KV_HEADS + g + 1) * HEAD)
                values = jnp.concatenate([ref[:rows, span] for ref in refs], axis=0)
                made = jnp.dot(
                    weights.astype(jnp.bfloat16), values, preferred_element_type=jnp.float32
                )
                sums = weights[:, :rows] + weights[:, rows:]
                if n == 0:
                    sum_ref[part, :] = sums
                    acc_ref[part, :] = made
                else:
                    sum_ref[part, :] += sums
                    acc_ref[part, :] += made

        if n == 0:
            weigh()
        else:
            pl.when(used[n])(weigh)

    for head in range(HEADS):
        part = slice(head * rows, (head + 1) * rows)
        total = jnp.sum(sum_ref[part, :], axis=1, keepdims=True)
        out_ref[:, head * HEAD : (head + 1) * HEAD] = (acc_ref[part, :] / total).astype(
            jnp.bfloat16
        )


def attend_call(projected, windows):
    rows = projected[0].shape[0]
    wide = HEADS * rows
    return pl.pallas_call(
        attend_kernel,
        out_shape=jax.ShapeDtypeStruct((rows, HEADS * HEAD), jnp.bfloat16),
        in_specs=[vmem()] * (len(projected) + len(windows)),
        out_specs=vmem(),
        scratch_shapes=[
            pltpu.VMEM((wide, HEAD), jnp.bfloat16),
            pltpu.VMEM((CHIPS + 1, wide, 2 * rows), jnp.float32),
            pltpu.VMEM((wide, rows), jnp.float32),
            pltpu.VMEM((wide, rows), jnp.float32),
            pltpu.VMEM((wide, HEAD), jnp.float32),
        ],
        cost_estimate=LONG,
        compiler_params=params(32),
        name="attend",
    )(*projected, *windows)


def assemble_kernel(same, other, out_ref):
    chip, core = place()
    cols = same[0].shape[0]
    for pieces, which in ((same, core), (other, 1 - core)):
        done = 0
        for piece in pieces:
            count = piece.shape[0]
            start = ((chip ^ (done // cols)) * CORES + which) * cols + done % cols
            out_ref[pl.ds(pl.multiple_of(start, PAGE), count), :] = piece[...]
            done += count


def assemble_call(same, other):
    shape = (CORES * CHIPS * same[0].shape[0], same[0].shape[1])
    count = len(same)
    return pl.pallas_call(
        lambda *refs: assemble_kernel(refs[:count], refs[count:-1], refs[-1]),
        out_shape=jax.ShapeDtypeStruct(shape, jnp.bfloat16),
        in_specs=[vmem()] * (2 * count),
        out_specs=vmem(),
        compiler_params=params(16),
        name="assemble_w_out",
    )(*same, *other)


def expert_kernel(tile, *refs):
    context, tokens, tables = refs[:2], refs[2:4], refs[4:6]
    w_ref, gain_ref = refs[6:8]
    held, outs, (rows_ref, hidden_ref, total_ref) = refs[8:14], refs[-5:-3], refs[-3:]
    chip, core = place()
    rows, width = context[0].shape
    hidden = hidden_ref.shape[1]
    spans = [slice(i * rows, (i + 1) * rows) for i in range(2)]
    for span, piece in zip(spans, context):
        rows_ref[span, :] = piece[...]
    added = lax.dot_general(
        rows_ref[...], w_ref[...], (((1,), (1,)), ((), ())), preferred_element_type=jnp.float32
    )
    for span, piece in zip(spans, tokens):
        residual = (piece[...].astype(jnp.float32) + added[span]).astype(jnp.bfloat16)
        wide = residual.astype(jnp.float32)
        if outs[0].dtype == jnp.float32 and span.start == 0:
            total_ref[span, :] = wide
        else:
            total_ref[span, :] = jnp.zeros_like(wide)
        rows_ref[span, :] = rms_rows(wide, gain_ref)

    for which in range(CORES):
        expert = chip * CORES + (core if which == 0 else 1 - core)
        gate, up, down = held[3 * which : 3 * which + 3]
        shares = []
        for table in tables:
            below = table[rows:, :].astype(jnp.float32)
            row_id = lax.broadcasted_iota(jnp.int32, below.shape, 0)
            row = jnp.sum(
                jnp.where(row_id == PAGE // 2 + expert, below, 0.0), axis=0, keepdims=True
            )
            row = row[:, :rows] + row[:, rows : 2 * rows] + row[:, 2 * rows : 3 * rows]
            shares.append(jnp.broadcast_to(row, (rows, rows)).T[:, :1])
        for column in range(0, hidden, tile):
            span = slice(column, column + tile)
            gate_out = jnp.dot(rows_ref[...], gate[:, span], preferred_element_type=jnp.float32)
            up_out = jnp.dot(rows_ref[...], up[:, span], preferred_element_type=jnp.float32)
            hidden_ref[:, span] = (jnp.maximum(gate_out, 0.0) * up_out).astype(jnp.bfloat16)
        for column in range(0, width, 2 * tile):
            cols = slice(column, column + 2 * tile)
            made = jnp.dot(hidden_ref[...], down[:, cols], preferred_element_type=jnp.float32)
            made = made.astype(jnp.bfloat16).astype(jnp.float32)
            for span, share, out_ref in zip(spans, shares, outs):
                total = total_ref[span, cols] + share * made[span]
                if which == 0:
                    total_ref[span, cols] = total
                else:
                    out_ref[:, cols] = total.astype(out_ref.dtype)


def expert_call(context, tokens, tables, w_all, gain, weights, kinds, *earlier):
    rows, width = tokens[0].shape
    hidden = weights[0].shape[1]
    return pl.pallas_call(
        functools.partial(expert_kernel, 256),
        out_shape=tuple(jax.ShapeDtypeStruct((rows, width), kind) for kind in kinds),
        in_specs=[vmem()] * 14 + [anywhere()] * len(earlier),
        out_specs=(vmem(), vmem()),
        scratch_shapes=[
            pltpu.VMEM((2 * rows, width), jnp.bfloat16),
            pltpu.VMEM((2 * rows, hidden), jnp.bfloat16),
            pltpu.VMEM((2 * rows, width), jnp.float32),
        ],
        cost_estimate=LONG,
        compiler_params=params(32),
        name="experts",
    )(*context, *tokens, *tables, w_all, gain, *weights, *earlier)


def mix_kernel(own, by_x, by_y, by_xy, out_ref):
    total = by_x[...].astype(jnp.float32) + by_y[...].astype(jnp.float32)
    total = total + by_xy[...].astype(jnp.float32)
    out_ref[...] = (own[...] + total).astype(jnp.bfloat16)


def mix_call(pieces):
    return pl.pallas_call(
        mix_kernel,
        out_shape=jax.ShapeDtypeStruct(pieces[0].shape, jnp.bfloat16),
        in_specs=[vmem()] * CHIPS,
        out_specs=vmem(),
        compiler_params=params(16),
        name="mix",
    )(*pieces)


def cache_kernel(table_ref, *refs):
    same, other, (out_ref, held) = refs[:2], refs[2:4], refs[4:]
    core = place()[1]
    page_rows = held.shape[1]
    pages = page_rows // PAGE
    for i, hop_by in enumerate(ORDER):
        source = (CHIPS - 1 ^ hop_by) * CORES
        span = slice(i % 2 * page_rows, (i % 2 + 1) * page_rows)
        held[source + core] = same[i // 2][span, :]
        held[source + 1 - core] = other[i // 2][span, :]

    def one(logical, carry):
        slot = table_ref[0, logical]
        to = slot // pages

        @pl.when(lax.rem(to, CORES) == core)
        def _():
            from_row = pl.multiple_of(lax.rem(logical, pages) * PAGE, PAGE)
            to_row = pl.multiple_of(lax.rem(slot, pages) * PAGE, PAGE)
            out_ref[to // CORES, pl.ds(to_row, PAGE), :] = held[
                logical // pages, pl.ds(from_row, PAGE), :
            ]

        return carry

    lax.fori_loop(0, table_ref.shape[1], one, 0, unroll=8)


def cache_call(page_table, same, other):
    rows, width = same[0].shape[0] // 2, same[0].shape[1]
    return pl.pallas_call(
        cache_kernel,
        out_shape=jax.ShapeDtypeStruct((CHIPS, rows, width), jnp.bfloat16),
        in_specs=[pl.BlockSpec(memory_space=pltpu.SMEM)] + [vmem()] * 4,
        out_specs=vmem(),
        scratch_shapes=[pltpu.VMEM((CORES * CHIPS, rows, width), jnp.bfloat16)],
        compiler_params=params(16),
        name="cache_pages",
    )(page_table, *same, *other)


def join_kernel(*refs):
    pieces, out_ref = refs[:CHIPS], refs[CHIPS]
    for hop_by, piece in enumerate(pieces):

        @pl.when(place()[0] ^ hop_by == CHIPS - 1)
        def _(piece=piece):
            out_ref[...] = piece[...]


def join_call(pieces):
    return pl.pallas_call(
        join_kernel,
        out_shape=jax.ShapeDtypeStruct(pieces[0].shape, pieces[0].dtype),
        in_specs=[vmem()] * CHIPS,
        out_specs=vmem(),
        compiler_params=params(16),
        name="join_pages",
    )(*pieces)


def hold_kernel(in_ref, *refs):
    refs[-1][...] = in_ref[...]


def hold_call(value, *earlier):
    return pl.pallas_call(
        hold_kernel,
        out_shape=jax.ShapeDtypeStruct(value.shape, value.dtype),
        in_specs=[vmem()] + [anywhere()] * len(earlier),
        out_specs=vmem(),
        cost_estimate=LONG,
        compiler_params=params(16),
        name="hold",
    )(value, *earlier)


def after(value, other):
    return lax.optimization_barrier((value, other))[0]


def chip_body(
    tokens, segment_ids, page_table, attn_gain, w_qkv, w_out, moe_gain,
    route_ids, route_weight, w_gate, w_up, w_down,
):
    rows = tokens.shape[0]
    seq_size = lax.axis_size("seq")

    def chips(value, by):
        return hop(value, CORES * by)

    gate, up, down = w_gate[0], w_up[0], w_down[0]
    w_own = w_out.T

    tokens_xy, tokens_x, tokens_y = chips(tokens, 3), chips(tokens, 1), chips(tokens, 2)
    w_qkv_other = hop(w_qkv, 1)
    made = project_call(tokens, tokens_xy, attn_gain, w_qkv, w_qkv_other)
    late = project_call(tokens_x, tokens_y, attn_gain, w_qkv, w_qkv_other)
    projected = [made[:rows], chips(late[:rows], 1), chips(late[rows:], 2), chips(made[rows:], 3)]
    gate_other, up_other = hop(after(gate, tokens_xy), 1), hop(after(up, made), 1)

    paged = cache_call(page_table, (made, late), (hop(after(made, late), 1), hop(late, 1)))
    own_kv = pack_call(
        after(projected, (paged, gate_other, up_other)), segment_ids, route_ids, route_weight
    )
    prev_kv = lax.ppermute(own_kv, "seq", [(i, i + 1) for i in range(seq_size - 1)])
    w_going, down_going = after((w_own, down), late)
    w_x, w_y = chips(w_going, 1), chips(w_going, 2)
    down_other, w_own_other = hop(down_going, 1), hop(w_going, 1)

    sent = choose_call(own_kv, after(prev_kv, (w_x, w_y, down_other, w_own_other)))
    kv_xy, kv_x, kv_y = chips(sent[2], 3), chips(sent[0], 1), chips(sent[1], 2)
    half = w_own.shape[0] // 2
    w_relayed = [hold_call(w_y[:half], *sent), hold_call(w_x[half:], *sent)]
    w_diagonal = [chips(w_relayed[0], 1), chips(w_relayed[1], 2)]
    windows = [own_kv, kv_x, kv_y, kv_xy, prev_kv]
    windows_other = [hop(w, 1) for w in windows]
    w_other = [w_own_other] + [hop(after(w, sent), 1) for w in (w_x, w_y)]
    windows_other = after(windows_other, (w_other, w_relayed))
    context = after(attend_call(projected, windows + windows_other), w_diagonal)
    context_xy, context_x, context_y = chips(context, 3), chips(context, 1), chips(context, 2)
    last = CHIPS - 1
    paged = after(paged, context)
    pages = [paged[last]]
    for by in (1, 2, 3):
        pairs = [(last * CORES + k, (last ^ by) * CORES + k) for k in range(CORES)]
        pages.append(lax.ppermute(paged[last ^ by], "tensor", pairs))
    pages = join_call(pages)
    w_other += [hop(w, 1) for w in w_diagonal]
    w_all = assemble_call([w_own, w_x, w_y] + w_diagonal, w_other)

    weights = [gate, up, down, gate_other, up_other, down_other]
    out, out_xy = expert_call(
        (context, context_xy), (tokens, tokens_xy), (own_kv, kv_xy), w_all, moe_gain, weights,
        (jnp.float32, jnp.bfloat16),
    )
    back_xy = chips(out_xy, 3)
    out_x, out_y = expert_call(
        (context_x, context_y), (tokens_x, tokens_y), (kv_x, kv_y), w_all, moe_gain, weights,
        (jnp.bfloat16, jnp.bfloat16), out_xy,
    )
    back_x, back_y = chips(out_x, 1), chips(out_y, 2)
    mixed = mix_call((out, back_x, back_y, back_xy))
    return (mixed, pages.reshape(rows // PAGE, PAGE, pages.shape[1]))


def from_behind(value, axis, by):
    length = lax.axis_size(axis)
    pairs = [(i, i + by) for i in range(length) if 0 <= i + by < length]
    return lax.ppermute(value, axis, pairs)


def rms_scaled(values, scales):
    wide = values.astype(jnp.float32)
    mean_sq = jnp.mean(wide * wide, axis=-1, keepdims=True)
    return (wide * lax.rsqrt(mean_sq + epsilon) * scales).astype(jnp.bfloat16)


def attend(queries, keys_window, values_window, allowed):
    scores = jnp.einsum(
        "qhd,kd->hqk", queries, keys_window, preferred_element_type=jnp.float32
    ) / math.sqrt(queries.shape[-1])
    scores = jnp.where(allowed[None], scores, -jnp.inf)
    highest = jnp.max(scores, axis=-1, keepdims=True)
    weights = jnp.exp(scores - highest)
    totals = jnp.sum(weights, axis=-1, keepdims=True)
    shares = (weights / totals).astype(jnp.bfloat16)
    return jnp.einsum("hqk,kd->qhd", shares, values_window, preferred_element_type=jnp.float32)


def block_body(
    tokens,
    segment_ids,
    page_table,
    attn_gain,
    w_qkv,
    w_out,
    moe_gain,
    route_ids,
    route_weight,
    w_gate,
    w_up,
    w_down,
):
    tok_rows = tokens.shape[0]
    tensor_size = lax.axis_size("tensor")
    tensor_index = lax.axis_index("tensor")
    seq_index = lax.axis_index("seq")
    block_rows = tok_rows * tensor_size
    normed = rms_scaled(tokens, attn_gain)
    block_normed = lax.all_gather(normed, "tensor", axis=0, tiled=True)
    own_columns = jnp.dot(block_normed, w_qkv, preferred_element_type=jnp.float32).astype(
        jnp.bfloat16
    )
    projected = lax.all_to_all(own_columns, "tensor", split_axis=0, concat_axis=1, tiled=True)
    query_width = HEADS * HEAD
    queries = projected[:, :query_width].reshape(tok_rows, HEADS, HEAD)
    own_kv = projected[:, query_width:]
    block_kv, block_segs = (
        lax.all_gather(own_kv, "tensor", axis=0, tiled=True),
        lax.all_gather(segment_ids, "tensor", axis=0, tiled=True),
    )
    earlier_kv, earlier_seg_block = from_behind((block_kv, block_segs), "seq", 1)
    pages_here = tok_rows // PAGE
    pages_block = block_rows // PAGE
    slot_ids = tensor_index * pages_here + jnp.arange(pages_here, dtype=jnp.int32)
    matches = page_table[0][None, :] == slot_ids[:, None]
    logical = jnp.sum(
        jnp.where(matches, jnp.arange(pages_block, dtype=jnp.int32)[None, :], 0), axis=1
    )
    cache_pages = block_kv.reshape(pages_block, PAGE, block_kv.shape[1])[logical]
    all_kv = jnp.concatenate([earlier_kv, block_kv], axis=0)
    all_segs = jnp.concatenate([earlier_seg_block, block_segs], axis=0)
    window = block_rows + tok_rows
    first_key = tensor_index * tok_rows
    keys_window = lax.dynamic_slice_in_dim(all_kv, first_key, window, 0)
    segs_window = lax.dynamic_slice_in_dim(all_segs, first_key, window, 0)
    key_pos = (seq_index - 1) * block_rows + first_key + jnp.arange(window, dtype=jnp.int32)
    query_pos = seq_index * block_rows + first_key + jnp.arange(tok_rows, dtype=jnp.int32)
    allowed = (
        (segs_window[None, :] == segment_ids[:, None])
        & (key_pos[None, :] <= query_pos[:, None])
        & (key_pos[None, :] >= 0)
    )
    per_group = HEADS // KV_HEADS
    contexts = []
    for kv_group in range(KV_HEADS):
        key_cols = keys_window[:, kv_group * HEAD : (kv_group + 1) * HEAD]
        value_cols = keys_window[:, (KV_HEADS + kv_group) * HEAD : (KV_HEADS + kv_group + 1) * HEAD]
        contexts.append(
            attend(
                queries[:, kv_group * per_group : (kv_group + 1) * per_group],
                key_cols,
                value_cols,
                allowed,
            )
        )
    context = jnp.concatenate(contexts, axis=1).reshape(tok_rows, query_width).astype(jnp.bfloat16)
    attn_out = jnp.dot(
        context,
        lax.all_gather(w_out, "tensor", axis=1, tiled=True),
        preferred_element_type=jnp.float32,
    )
    residual = (tokens.astype(jnp.float32) + attn_out).astype(jnp.bfloat16)
    expert_input = rms_scaled(residual, moe_gain)
    experts_all = w_gate.shape[0] * tensor_size
    capacity = max(2, 3 * tok_rows * TOP // (2 * experts_all))
    flat_routes = route_ids.reshape(-1)
    expert_hits = (
        flat_routes[:, None] == jnp.arange(experts_all, dtype=jnp.int32)[None, :]
    ).astype(jnp.int32)
    earlier_hits = jnp.cumsum(expert_hits, axis=0) - expert_hits
    slot_rank = jnp.sum(earlier_hits * expert_hits, axis=1)
    dest_slot = flat_routes * capacity + slot_rank
    slot_table = (
        jnp.arange(experts_all * capacity, dtype=jnp.int32)[:, None, None]
        == dest_slot.reshape(tok_rows, TOP)[None]
    )
    dispatch = jnp.any(slot_table, axis=2).astype(jnp.bfloat16)
    outgoing = jnp.dot(dispatch, expert_input, preferred_element_type=jnp.float32).astype(
        jnp.bfloat16
    )
    outgoing = outgoing.reshape(experts_all, capacity, expert_input.shape[1])
    arrived = lax.all_to_all(outgoing, "tensor", split_axis=0, concat_axis=0, tiled=True)
    rows_flat = arrived.reshape(-1, arrived.shape[-1])
    gate_out = jnp.dot(rows_flat, w_gate[0], preferred_element_type=jnp.float32)
    up_out = jnp.dot(rows_flat, w_up[0], preferred_element_type=jnp.float32)
    hidden = (jnp.maximum(gate_out, 0.0) * up_out).astype(jnp.bfloat16)
    produced = jnp.dot(hidden, w_down[0], preferred_element_type=jnp.float32).astype(jnp.bfloat16)
    returned = lax.all_to_all(
        produced.reshape(arrived.shape), "tensor", split_axis=0, concat_axis=0, tiled=True
    )
    picked = returned.reshape(-1, returned.shape[-1])[dest_slot].reshape(
        tok_rows, TOP, returned.shape[-1]
    )
    routed_sum = jnp.einsum("tk,tkd->td", route_weight, picked.astype(jnp.float32))
    mixed = (residual.astype(jnp.float32) + routed_sum).astype(jnp.bfloat16)
    return (mixed, cache_pages)


def by_chips(mesh):
    size = mesh.shape["tensor"]
    return size == CORES * CHIPS and (HEADS + 2 * KV_HEADS) % size == 0


def solution(mesh):
    return jax.shard_map(
        chip_body if by_chips(mesh) else block_body,
        mesh=mesh,
        in_specs=(
            P(("seq", "tensor"), None),
            P(("seq", "tensor")),
            P("seq", None),
            P(),
            P(None, "tensor"),
            P(None, "tensor"),
            P(),
            P(("seq", "tensor"), None),
            P(("seq", "tensor"), None),
            P("tensor", None, None),
            P("tensor", None, None),
            P("tensor", None, None),
        ),
        out_specs=(P(("seq", "tensor"), None), P(("seq", "tensor"), None, None)),
        check_vma=False,
    )
```

```python
import functools
import math

import jax
import jax.numpy as jnp
from jax import lax
from jax.experimental import pallas as pl
from jax.experimental.pallas import tpu as pltpu
from jax.sharding import PartitionSpec as P

HEADS = 12
KV_HEADS = 2
HEAD = 128
TOP = 4
PAGE = 16
CORES = 2
CHIPS = 4


epsilon = 1e-06
MIB = 1024 * 1024


LONG = pl.CostEstimate(flops=20 * 10**9, bytes_accessed=1, transcendentals=0)


ORDER = (0, 3, 1, 2)


def vmem():
    return pl.BlockSpec(memory_space=pltpu.VMEM)


def anywhere():
    return pl.BlockSpec(memory_space=pl.ANY)


def params(mib):
    return pltpu.CompilerParams(vmem_limit_bytes=mib * MIB)


def place():
    index = lax.axis_index("tensor")
    return index // CORES, lax.rem(index, CORES)


def hop(value, by):
    length = lax.axis_size("tensor")
    return lax.ppermute(value, "tensor", [(i, i ^ by) for i in range(length)])


def rms_rows(wide, gain_ref):
    mean_sq = jnp.mean(wide * wide, axis=-1, keepdims=True)
    return (wide * lax.rsqrt(mean_sq + epsilon) * gain_ref[...]).astype(jnp.bfloat16)


def project_kernel(count, *refs):
    pieces, (gain_ref, w_own, w_other) = refs[:count], refs[count : count + 3]
    out_ref, rows_ref = refs[-2:]
    core = place()[1]
    cols = w_own.shape[1]
    at = 0
    for piece in pieces:
        span = slice(at, at + piece.shape[0])
        rows_ref[span, :] = rms_rows(piece[...].astype(jnp.float32), gain_ref)
        at += piece.shape[0]
    for which, weights in ((core, w_own), (1 - core, w_other)):
        span = pl.ds(pl.multiple_of(which * cols, cols), cols)
        out_ref[:, span] = jnp.dot(
            rows_ref[...], weights[...], preferred_element_type=jnp.float32
        ).astype(jnp.bfloat16)


def project_call(pieces, gain, w_own, w_other, *earlier):
    rows, width = sum(p.shape[0] for p in pieces), pieces[0].shape[1]
    return pl.pallas_call(
        functools.partial(project_kernel, len(pieces)),
        out_shape=jax.ShapeDtypeStruct((rows, CORES * w_own.shape[1]), jnp.bfloat16),
        in_specs=[vmem()] * (len(pieces) + 3) + [anywhere()] * len(earlier),
        out_specs=vmem(),
        scratch_shapes=[pltpu.VMEM((rows, width), jnp.bfloat16)],
        cost_estimate=LONG,
        compiler_params=params(16),
        name="project",
    )(*pieces, gain, w_own, w_other, *earlier)


def pack_kernel(own, by_x, by_y, by_xy, segs_ref, routes_ref, shares_ref, out_ref):
    chip = place()[0]
    rows, width = own.shape
    for hop_by, piece in enumerate((own, by_x, by_y, by_xy)):

        @pl.when(chip ^ hop_by == CHIPS - 1)
        def _(piece=piece):
            out_ref[:rows, :] = piece[...]

    experts = PAGE // 2
    named = lax.broadcasted_iota(jnp.int32, (experts, rows), 0)
    table = jnp.zeros((experts, rows), jnp.float32)
    for k in range(TOP):
        routed = jnp.broadcast_to(routes_ref[k : k + 1, :], (experts, rows)) == named
        table = table + jnp.where(routed, shares_ref[k : k + 1, :], 0.0)
    segs = jnp.broadcast_to(segs_ref[...].astype(jnp.float32), (experts, rows))
    out_ref[rows:, :rows] = jnp.concatenate([segs, table], axis=0).astype(jnp.bfloat16)
    for part in (1, 2):
        table = table - table.astype(jnp.bfloat16).astype(jnp.float32)
        out_ref[rows:, part * rows : (part + 1) * rows] = jnp.concatenate(
            [segs, table], axis=0
        ).astype(jnp.bfloat16)
    out_ref[rows:, 3 * rows :] = jnp.zeros((PAGE, width - 3 * rows), jnp.bfloat16)


def pack_call(pieces, segment_ids, routes, shares):
    rows, width = pieces[0].shape
    return pl.pallas_call(
        pack_kernel,
        out_shape=jax.ShapeDtypeStruct((rows + PAGE, width), jnp.bfloat16),
        in_specs=[vmem()] * (CHIPS + 3),
        out_specs=vmem(),
        compiler_params=params(16),
        name="pack_kv",
    )(*pieces, segment_ids.reshape(1, rows), routes.T, shares.T)


def choose_kernel(own, prev, *out_refs):
    chip = place()[0]
    rows = own.shape[0] - PAGE
    row_id = lax.broadcasted_iota(jnp.int32, (PAGE, own.shape[1]), 0)
    for hop_by, out_ref in enumerate(out_refs, 1):
        later = (chip ^ hop_by) > chip

        @pl.when(later)
        def _(out_ref=out_ref):
            out_ref[...] = own[...]

        @pl.when(jnp.logical_not(later))
        def _(out_ref=out_ref):
            out_ref[:rows, :] = prev[:rows, :]
            below, mine = prev[rows:, :].astype(jnp.float32), own[rows:, :].astype(jnp.float32)
            out_ref[rows:, :] = jnp.where(row_id < PAGE // 2, below, mine).astype(jnp.bfloat16)


def choose_call(own, prev):
    return pl.pallas_call(
        choose_kernel,
        out_shape=(jax.ShapeDtypeStruct(own.shape, own.dtype),) * (CHIPS - 1),
        in_specs=[vmem()] * 2,
        out_specs=(vmem(),) * (CHIPS - 1),
        compiler_params=params(16),
        name="choose_kv",
    )(own, prev)


def attend_kernel(*refs):
    projected, refs = refs[:CHIPS], refs[CHIPS:]
    windows, refs = refs[: 2 * (CHIPS + 1)], refs[2 * (CHIPS + 1) :]
    out_ref, q_ref, s_ref, top_ref, sum_ref, acc_ref = refs
    chip, core = place()
    seq = lax.axis_index("seq")
    rows = out_ref.shape[0]
    per_group = HEADS // KV_HEADS
    per_chip = HEADS // (CHIPS - 1)
    block_rows = rows * CORES * CHIPS
    own_first = seq * block_rows + (chip * CORES + core) * rows

    def segs_of(ref):
        return ref[rows : rows + 1, :rows].astype(jnp.float32)

    own_segs = segs_of(windows[0])
    query_seg = jnp.broadcast_to(own_segs, (rows, rows)).T
    query_pos = lax.broadcasted_iota(jnp.int32, (rows, rows), 0) + own_first
    lane = lax.broadcasted_iota(jnp.int32, (rows, rows), 1)
    lowest = jnp.min(own_segs)

    for hop_by, piece in enumerate(projected):
        source = chip ^ hop_by

        @pl.when(source < CHIPS - 1)
        def _(source=source, piece=piece):
            for i in range(per_chip):
                start = pl.multiple_of((source * per_chip + i) * rows, rows)
                q_ref[pl.ds(start, rows), :] = piece[:, i * HEAD : (i + 1) * HEAD]

    pairs = []
    for n in range(CHIPS + 1):
        if n == 0:
            base, source = seq, chip
        elif n == CHIPS:
            base, source = seq - 1, chip
        else:
            source = chip ^ n
            base = jnp.where(source < chip, seq, seq - 1)
        first = base * block_rows + source * CORES * rows
        refs = (windows[n], windows[n + CHIPS + 1])
        pairs.append((refs, (first + core * rows, first + (1 - core) * rows)))

    scale = math.log2(math.e) / math.sqrt(HEAD)
    group_rows = per_group * rows
    used = []
    for n, (refs, firsts) in enumerate(pairs):
        use = (firsts[0] >= 0) & (firsts[0] <= own_first)
        last_seg = jnp.max(jnp.maximum(segs_of(refs[0]), segs_of(refs[1])))
        used.append(use & (last_seg >= lowest))

        def scores_of(n=n, refs=refs, firsts=firsts):
            bias = []
            for ref, first in zip(refs, firsts):
                allowed = (segs_of(ref) == query_seg) & (first + lane <= query_pos)
                bias.append(jnp.where(allowed, 0.0, -jnp.inf))
            bias = jnp.concatenate(bias, axis=1)
            for g in range(KV_HEADS):
                span = slice(g * HEAD, (g + 1) * HEAD)
                keys = jnp.concatenate([ref[:rows, span] for ref in refs], axis=0)
                part = slice(g * group_rows, (g + 1) * group_rows)
                scores = lax.dot_general(
                    q_ref[part, :], keys, (((1,), (1,)), ((), ())),
                    preferred_element_type=jnp.float32,
                )
                scores = scores.reshape(per_group, rows, 2 * rows) * scale + bias[None]
                scores = scores.reshape(group_rows, 2 * rows)
                s_ref[n, part, :] = scores
                high = jnp.maximum(scores[:, :rows], scores[:, rows:])
                top_ref[part, :] = high if n == 0 else jnp.maximum(top_ref[part, :], high)

        if n == 0:
            scores_of()
        else:
            pl.when(used[n])(scores_of)

    top_ref[...] = jnp.broadcast_to(jnp.max(top_ref[...], axis=1, keepdims=True), top_ref.shape)
    for n, (refs, firsts) in enumerate(pairs):

        def weigh(n=n, refs=refs):
            for g in range(KV_HEADS):
                part = slice(g * group_rows, (g + 1) * group_rows)
                top = top_ref[part, :]
                weights = jnp.exp2(s_ref[n, part, :] - jnp.concatenate([top, top], axis=1))
                span = slice((KV_HEADS + g) * HEAD, (KV_HEADS + g + 1) * HEAD)
                values = jnp.concatenate([ref[:rows, span] for ref in refs], axis=0)
                made = jnp.dot(
                    weights.astype(jnp.bfloat16), values, preferred_element_type=jnp.float32
                )
                sums = weights[:, :rows] + weights[:, rows:]
                if n == 0:
                    sum_ref[part, :] = sums
                    acc_ref[part, :] = made
                else:
                    sum_ref[part, :] += sums
                    acc_ref[part, :] += made

        if n == 0:
            weigh()
        else:
            pl.when(used[n])(weigh)

    for head in range(HEADS):
        part = slice(head * rows, (head + 1) * rows)
        total = jnp.sum(sum_ref[part, :], axis=1, keepdims=True)
        out_ref[:, head * HEAD : (head + 1) * HEAD] = (acc_ref[part, :] / total).astype(
            jnp.bfloat16
        )


def attend_call(projected, windows):
    rows = projected[0].shape[0]
    wide = HEADS * rows
    return pl.pallas_call(
        attend_kernel,
        out_shape=jax.ShapeDtypeStruct((rows, HEADS * HEAD), jnp.bfloat16),
        in_specs=[vmem()] * (len(projected) + len(windows)),
        out_specs=vmem(),
        scratch_shapes=[
            pltpu.VMEM((wide, HEAD), jnp.bfloat16),
            pltpu.VMEM((CHIPS + 1, wide, 2 * rows), jnp.float32),
            pltpu.VMEM((wide, rows), jnp.float32),
            pltpu.VMEM((wide, rows), jnp.float32),
            pltpu.VMEM((wide, HEAD), jnp.float32),
        ],
        compiler_params=params(32),
        name="attend",
    )(*projected, *windows)


def assemble_kernel(same, other, out_ref):
    chip, core = place()
    cols = same[0].shape[0]
    for pieces, which in ((same, core), (other, 1 - core)):
        done = 0
        for piece in pieces:
            count = piece.shape[0]
            start = ((chip ^ (done // cols)) * CORES + which) * cols + done % cols
            out_ref[pl.ds(pl.multiple_of(start, PAGE), count), :] = piece[...]
            done += count


def assemble_call(same, other):
    shape = (CORES * CHIPS * same[0].shape[0], same[0].shape[1])
    count = len(same)
    return pl.pallas_call(
        lambda *refs: assemble_kernel(refs[:count], refs[count:-1], refs[-1]),
        out_shape=jax.ShapeDtypeStruct(shape, jnp.bfloat16),
        in_specs=[vmem()] * (2 * count),
        out_specs=vmem(),
        compiler_params=params(16),
        name="assemble_w_out",
    )(*same, *other)


def expert_kernel(tile, count, *refs):
    context, tables, (w_ref, gain_ref), held = refs[:2], refs[2:4], refs[4:6], refs[6:12]
    tokens, outs, (rows_ref, hidden_ref, total_ref) = refs[12 : 12 + count], refs[-5:-3], refs[-3:]
    chip, core = place()
    rows, width = context[0].shape
    hidden = hidden_ref.shape[1]
    spans = [slice(i * rows, (i + 1) * rows) for i in range(2)]
    for span, piece in zip(spans, context):
        rows_ref[span, :] = piece[...]
    added = lax.dot_general(
        rows_ref[...], w_ref[...], (((1,), (1,)), ((), ())), preferred_element_type=jnp.float32
    )
    at = 0
    for piece in tokens:
        span = slice(at, at + piece.shape[0])
        at += piece.shape[0]
        residual = (piece[...].astype(jnp.float32) + added[span]).astype(jnp.bfloat16)
        wide = residual.astype(jnp.float32)
        if outs[0].dtype == jnp.float32 and span.start == 0:
            total_ref[span, :] = wide
        else:
            total_ref[span, :] = jnp.zeros_like(wide)
        rows_ref[span, :] = rms_rows(wide, gain_ref)

    for which in range(CORES):
        expert = chip * CORES + (core if which == 0 else 1 - core)
        gate, up, down = held[3 * which : 3 * which + 3]
        shares = []
        for table in tables:
            below = table[rows:, :].astype(jnp.float32)
            row_id = lax.broadcasted_iota(jnp.int32, below.shape, 0)
            row = jnp.sum(
                jnp.where(row_id == PAGE // 2 + expert, below, 0.0), axis=0, keepdims=True
            )
            row = row[:, :rows] + row[:, rows : 2 * rows] + row[:, 2 * rows : 3 * rows]
            shares.append(jnp.broadcast_to(row, (rows, rows)).T[:, :1])
        for column in range(0, hidden, tile):
            span = slice(column, column + tile)
            gate_out = jnp.dot(rows_ref[...], gate[:, span], preferred_element_type=jnp.float32)
            up_out = jnp.dot(rows_ref[...], up[:, span], preferred_element_type=jnp.float32)
            hidden_ref[:, span] = (jnp.maximum(gate_out, 0.0) * up_out).astype(jnp.bfloat16)
        for column in range(0, width, 2 * tile):
            cols = slice(column, column + 2 * tile)
            made = jnp.dot(hidden_ref[...], down[:, cols], preferred_element_type=jnp.float32)
            made = made.astype(jnp.bfloat16).astype(jnp.float32)
            for span, share, out_ref in zip(spans, shares, outs):
                total = total_ref[span, cols] + share * made[span]
                if which == 0:
                    total_ref[span, cols] = total
                else:
                    out_ref[:, cols] = total.astype(out_ref.dtype)


def expert_call(context, tokens, tables, w_all, gain, weights, kinds, *earlier):
    rows, width = tokens[0].shape
    hidden = weights[0].shape[1]
    return pl.pallas_call(
        functools.partial(expert_kernel, 256, len(tokens)),
        out_shape=tuple(jax.ShapeDtypeStruct((rows, width), kind) for kind in kinds),
        in_specs=[vmem()] * (12 + len(tokens)) + [anywhere()] * len(earlier),
        out_specs=(vmem(), vmem()),
        scratch_shapes=[
            pltpu.VMEM((2 * rows, width), jnp.bfloat16),
            pltpu.VMEM((2 * rows, hidden), jnp.bfloat16),
            pltpu.VMEM((2 * rows, width), jnp.float32),
        ],
        cost_estimate=LONG,
        compiler_params=params(32),
        name="experts",
    )(*context, *tables, w_all, gain, *weights, *tokens, *earlier)


def mix_kernel(own, by_x, by_y, by_xy, out_ref):
    total = by_x[...].astype(jnp.float32) + by_y[...].astype(jnp.float32)
    total = total + by_xy[...].astype(jnp.float32)
    out_ref[...] = (own[...] + total).astype(jnp.bfloat16)


def mix_call(pieces):
    return pl.pallas_call(
        mix_kernel,
        out_shape=jax.ShapeDtypeStruct(pieces[0].shape, jnp.bfloat16),
        in_specs=[vmem()] * CHIPS,
        out_specs=vmem(),
        compiler_params=params(16),
        name="mix",
    )(*pieces)


def cache_kernel(table_ref, *refs):
    same, other, (out_ref, held) = refs[:2], refs[2:4], refs[4:]
    core = place()[1]
    page_rows = held.shape[1]
    pages = page_rows // PAGE
    for i, hop_by in enumerate(ORDER):
        source = (CHIPS - 1 ^ hop_by) * CORES
        span = slice(i % 2 * page_rows, (i % 2 + 1) * page_rows)
        held[source + core] = same[i // 2][span, :]
        held[source + 1 - core] = other[i // 2][span, :]

    def one(logical, carry):
        slot = table_ref[0, logical]
        to = slot // pages

        @pl.when(lax.rem(to, CORES) == core)
        def _():
            from_row = pl.multiple_of(lax.rem(logical, pages) * PAGE, PAGE)
            to_row = pl.multiple_of(lax.rem(slot, pages) * PAGE, PAGE)
            out_ref[to // CORES, pl.ds(to_row, PAGE), :] = held[
                logical // pages, pl.ds(from_row, PAGE), :
            ]

        return carry

    lax.fori_loop(0, table_ref.shape[1], one, 0, unroll=8)


def cache_call(page_table, same, other):
    rows, width = same[0].shape[0] // 2, same[0].shape[1]
    return pl.pallas_call(
        cache_kernel,
        out_shape=jax.ShapeDtypeStruct((CHIPS, rows, width), jnp.bfloat16),
        in_specs=[pl.BlockSpec(memory_space=pltpu.SMEM)] + [vmem()] * 4,
        out_specs=vmem(),
        scratch_shapes=[pltpu.VMEM((CORES * CHIPS, rows, width), jnp.bfloat16)],
        cost_estimate=LONG,
        compiler_params=params(16),
        name="cache_pages",
    )(page_table, *same, *other)


def join_kernel(*refs):
    pieces, out_ref = refs[:CHIPS], refs[CHIPS]
    for hop_by, piece in enumerate(pieces):

        @pl.when(place()[0] ^ hop_by == CHIPS - 1)
        def _(piece=piece):
            out_ref[...] = piece[...]


def join_call(pieces):
    return pl.pallas_call(
        join_kernel,
        out_shape=jax.ShapeDtypeStruct(pieces[0].shape, pieces[0].dtype),
        in_specs=[vmem()] * CHIPS,
        out_specs=vmem(),
        cost_estimate=LONG,
        compiler_params=params(16),
        name="join_pages",
    )(*pieces)


def hold_kernel(in_ref, *refs):
    refs[-1][...] = in_ref[...]


def hold_call(value, *earlier):
    return pl.pallas_call(
        hold_kernel,
        out_shape=jax.ShapeDtypeStruct(value.shape, value.dtype),
        in_specs=[vmem()] + [anywhere()] * len(earlier),
        out_specs=vmem(),
        cost_estimate=LONG,
        compiler_params=params(16),
        name="hold",
    )(value, *earlier)


def after(value, other):
    return lax.optimization_barrier((value, other))[0]


def chip_body(
    tokens, segment_ids, page_table, attn_gain, w_qkv, w_out, moe_gain,
    route_ids, route_weight, w_gate, w_up, w_down,
):
    rows = tokens.shape[0]
    seq_size = lax.axis_size("seq")

    def chips(value, by):
        return hop(value, CORES * by)

    gate, up, down = w_gate[0], w_up[0], w_down[0]
    w_own = w_out.T

    tokens_x, tokens_y = chips(tokens, 1), chips(tokens, 2)
    w_qkv_other, gate_other = hop(w_qkv, 1), hop(gate, 1)
    tokens_xy = [chips(tokens_y[: rows // 2], 1), chips(tokens_x[rows // 2 :], 2)]
    late = project_call((tokens_x, tokens_y), attn_gain, w_qkv, w_qkv_other)
    made = project_call((tokens, *tokens_xy), attn_gain, w_qkv, w_qkv_other, late)
    projected = [made[:rows], chips(late[:rows], 1), chips(late[rows:], 2), chips(made[rows:], 3)]
    up_other = hop(after(up, tokens_x), 1)

    paged = cache_call(page_table, (made, late), (hop(made, 1), hop(after(late, made), 1)))
    own_kv = pack_call(
        after(projected, (paged, gate_other, up_other)), segment_ids, route_ids, route_weight
    )
    prev_kv = lax.ppermute(own_kv, "seq", [(i, i + 1) for i in range(seq_size - 1)])
    last = CHIPS - 1
    pages = [paged[last]]
    for by in (1, 2, 3):
        pairs = [(last * CORES + k, (last ^ by) * CORES + k) for k in range(CORES)]
        pages.append(lax.ppermute(paged[last ^ by], "tensor", pairs))
    pages = join_call(pages)
    w_going, down_going = after((w_own, down), own_kv)
    w_x, w_y = chips(w_going, 1), chips(w_going, 2)
    down_other, w_own_other = hop(down_going, 1), hop(w_going, 1)

    done = (w_x, w_y, down_other, w_own_other, pages)
    sent = choose_call(own_kv, after(prev_kv, done))
    kv_xy, kv_x, kv_y = chips(sent[2], 3), chips(sent[0], 1), chips(sent[1], 2)
    kv_xy = hold_call(kv_xy)
    half = w_own.shape[0] // 2
    w_relayed = [hold_call(w_y[:half], *sent), hold_call(w_x[half:], *sent)]
    w_diagonal = [chips(w_relayed[0], 1), chips(w_relayed[1], 2)]
    windows = [own_kv, kv_x, kv_y, kv_xy, prev_kv]
    windows_other = [hop(w, 1) for w in windows]
    w_other = [w_own_other] + [hop(after(w, sent), 1) for w in (w_x, w_y)]
    windows_other = after(windows_other, (w_other, w_relayed))
    context = after(attend_call(projected, windows + windows_other), w_diagonal)
    context_xy, context_x, context_y = chips(context, 3), chips(context, 1), chips(context, 2)
    w_other += [hop(w, 1) for w in w_diagonal]
    w_all = assemble_call([w_own, w_x, w_y] + w_diagonal, w_other)

    weights = [gate, up, down, gate_other, up_other, down_other]
    out, out_xy = expert_call(
        (context, context_xy), (tokens, *tokens_xy), (own_kv, kv_xy), w_all, moe_gain, weights,
        (jnp.float32, jnp.bfloat16),
    )
    back_xy = hold_call(chips(out_xy, 3))
    out_x, out_y = expert_call(
        (context_x, context_y), (tokens_x, tokens_y), (kv_x, kv_y), w_all, moe_gain, weights,
        (jnp.bfloat16, jnp.bfloat16), out_xy,
    )
    back_x, back_y = chips(out_x, 1), chips(out_y, 2)
    mixed = mix_call((out, back_x, back_y, back_xy))
    return (mixed, pages.reshape(rows // PAGE, PAGE, pages.shape[1]))


def from_behind(value, axis, by):
    length = lax.axis_size(axis)
    pairs = [(i, i + by) for i in range(length) if 0 <= i + by < length]
    return lax.ppermute(value, axis, pairs)


def rms_scaled(values, scales):
    wide = values.astype(jnp.float32)
    mean_sq = jnp.mean(wide * wide, axis=-1, keepdims=True)
    return (wide * lax.rsqrt(mean_sq + epsilon) * scales).astype(jnp.bfloat16)


def attend(queries, keys_window, values_window, allowed):
    scores = jnp.einsum(
        "qhd,kd->hqk", queries, keys_window, preferred_element_type=jnp.float32
    ) / math.sqrt(queries.shape[-1])
    scores = jnp.where(allowed[None], scores, -jnp.inf)
    highest = jnp.max(scores, axis=-1, keepdims=True)
    weights = jnp.exp(scores - highest)
    totals = jnp.sum(weights, axis=-1, keepdims=True)
    shares = (weights / totals).astype(jnp.bfloat16)
    return jnp.einsum("hqk,kd->qhd", shares, values_window, preferred_element_type=jnp.float32)


def block_body(
    tokens,
    segment_ids,
    page_table,
    attn_gain,
    w_qkv,
    w_out,
    moe_gain,
    route_ids,
    route_weight,
    w_gate,
    w_up,
    w_down,
):
    tok_rows = tokens.shape[0]
    tensor_size = lax.axis_size("tensor")
    tensor_index = lax.axis_index("tensor")
    seq_index = lax.axis_index("seq")
    block_rows = tok_rows * tensor_size
    normed = rms_scaled(tokens, attn_gain)
    block_normed = lax.all_gather(normed, "tensor", axis=0, tiled=True)
    own_columns = jnp.dot(block_normed, w_qkv, preferred_element_type=jnp.float32).astype(
        jnp.bfloat16
    )
    projected = lax.all_to_all(own_columns, "tensor", split_axis=0, concat_axis=1, tiled=True)
    query_width = HEADS * HEAD
    queries = projected[:, :query_width].reshape(tok_rows, HEADS, HEAD)
    own_kv = projected[:, query_width:]
    block_kv, block_segs = (
        lax.all_gather(own_kv, "tensor", axis=0, tiled=True),
        lax.all_gather(segment_ids, "tensor", axis=0, tiled=True),
    )
    earlier_kv, earlier_seg_block = from_behind((block_kv, block_segs), "seq", 1)
    pages_here = tok_rows // PAGE
    pages_block = block_rows // PAGE
    slot_ids = tensor_index * pages_here + jnp.arange(pages_here, dtype=jnp.int32)
    matches = page_table[0][None, :] == slot_ids[:, None]
    logical = jnp.sum(
        jnp.where(matches, jnp.arange(pages_block, dtype=jnp.int32)[None, :], 0), axis=1
    )
    cache_pages = block_kv.reshape(pages_block, PAGE, block_kv.shape[1])[logical]
    all_kv = jnp.concatenate([earlier_kv, block_kv], axis=0)
    all_segs = jnp.concatenate([earlier_seg_block, block_segs], axis=0)
    window = block_rows + tok_rows
    first_key = tensor_index * tok_rows
    keys_window = lax.dynamic_slice_in_dim(all_kv, first_key, window, 0)
    segs_window = lax.dynamic_slice_in_dim(all_segs, first_key, window, 0)
    key_pos = (seq_index - 1) * block_rows + first_key + jnp.arange(window, dtype=jnp.int32)
    query_pos = seq_index * block_rows + first_key + jnp.arange(tok_rows, dtype=jnp.int32)
    allowed = (
        (segs_window[None, :] == segment_ids[:, None])
        & (key_pos[None, :] <= query_pos[:, None])
        & (key_pos[None, :] >= 0)
    )
    per_group = HEADS // KV_HEADS
    contexts = []
    for kv_group in range(KV_HEADS):
        key_cols = keys_window[:, kv_group * HEAD : (kv_group + 1) * HEAD]
        value_cols = keys_window[:, (KV_HEADS + kv_group) * HEAD : (KV_HEADS + kv_group + 1) * HEAD]
        contexts.append(
            attend(
                queries[:, kv_group * per_group : (kv_group + 1) * per_group],
                key_cols,
                value_cols,
                allowed,
            )
        )
    context = jnp.concatenate(contexts, axis=1).reshape(tok_rows, query_width).astype(jnp.bfloat16)
    attn_out = jnp.dot(
        context,
        lax.all_gather(w_out, "tensor", axis=1, tiled=True),
        preferred_element_type=jnp.float32,
    )
    residual = (tokens.astype(jnp.float32) + attn_out).astype(jnp.bfloat16)
    expert_input = rms_scaled(residual, moe_gain)
    experts_all = w_gate.shape[0] * tensor_size
    capacity = max(2, 3 * tok_rows * TOP // (2 * experts_all))
    flat_routes = route_ids.reshape(-1)
    expert_hits = (
        flat_routes[:, None] == jnp.arange(experts_all, dtype=jnp.int32)[None, :]
    ).astype(jnp.int32)
    earlier_hits = jnp.cumsum(expert_hits, axis=0) - expert_hits
    slot_rank = jnp.sum(earlier_hits * expert_hits, axis=1)
    dest_slot = flat_routes * capacity + slot_rank
    slot_table = (
        jnp.arange(experts_all * capacity, dtype=jnp.int32)[:, None, None]
        == dest_slot.reshape(tok_rows, TOP)[None]
    )
    dispatch = jnp.any(slot_table, axis=2).astype(jnp.bfloat16)
    outgoing = jnp.dot(dispatch, expert_input, preferred_element_type=jnp.float32).astype(
        jnp.bfloat16
    )
    outgoing = outgoing.reshape(experts_all, capacity, expert_input.shape[1])
    arrived = lax.all_to_all(outgoing, "tensor", split_axis=0, concat_axis=0, tiled=True)
    rows_flat = arrived.reshape(-1, arrived.shape[-1])
    gate_out = jnp.dot(rows_flat, w_gate[0], preferred_element_type=jnp.float32)
    up_out = jnp.dot(rows_flat, w_up[0], preferred_element_type=jnp.float32)
    hidden = (jnp.maximum(gate_out, 0.0) * up_out).astype(jnp.bfloat16)
    produced = jnp.dot(hidden, w_down[0], preferred_element_type=jnp.float32).astype(jnp.bfloat16)
    returned = lax.all_to_all(
        produced.reshape(arrived.shape), "tensor", split_axis=0, concat_axis=0, tiled=True
    )
    picked = returned.reshape(-1, returned.shape[-1])[dest_slot].reshape(
        tok_rows, TOP, returned.shape[-1]
    )
    routed_sum = jnp.einsum("tk,tkd->td", route_weight, picked.astype(jnp.float32))
    mixed = (residual.astype(jnp.float32) + routed_sum).astype(jnp.bfloat16)
    return (mixed, cache_pages)


def by_chips(mesh):
    size = mesh.shape["tensor"]
    return size == CORES * CHIPS and (HEADS + 2 * KV_HEADS) % size == 0


def solution(mesh):
    return jax.shard_map(
        chip_body if by_chips(mesh) else block_body,
        mesh=mesh,
        in_specs=(
            P(("seq", "tensor"), None),
            P(("seq", "tensor")),
            P("seq", None),
            P(),
            P(None, "tensor"),
            P(None, "tensor"),
            P(),
            P(("seq", "tensor"), None),
            P(("seq", "tensor"), None),
            P("tensor", None, None),
            P("tensor", None, None),
            P("tensor", None, None),
        ),
        out_specs=(P(("seq", "tensor"), None), P(("seq", "tensor"), None, None)),
        check_vma=False,
    )
```

```python
import functools
import math

import jax
import jax.numpy as jnp
from jax import lax
from jax.experimental import pallas as pl
from jax.experimental.pallas import tpu as pltpu
from jax.sharding import PartitionSpec as P

HEADS = 12
KV_HEADS = 2
HEAD = 128
TOP = 4
PAGE = 16
CORES = 2
CHIPS = 4


epsilon = 1e-06
MIB = 1024 * 1024


LONG = pl.CostEstimate(flops=20 * 10**9, bytes_accessed=1, transcendentals=0)


ORDER = (0, 3, 1, 2)


def vmem():
    return pl.BlockSpec(memory_space=pltpu.VMEM)


def anywhere():
    return pl.BlockSpec(memory_space=pl.ANY)


def params(mib):
    return pltpu.CompilerParams(vmem_limit_bytes=mib * MIB)


def place():
    index = lax.axis_index("tensor")
    return index // CORES, lax.rem(index, CORES)


def hop(value, by):
    length = lax.axis_size("tensor")
    return lax.ppermute(value, "tensor", [(i, i ^ by) for i in range(length)])


def rms_rows(wide, gain_ref):
    mean_sq = jnp.mean(wide * wide, axis=-1, keepdims=True)
    return (wide * lax.rsqrt(mean_sq + epsilon) * gain_ref[...]).astype(jnp.bfloat16)


def project_kernel(count, *refs):
    pieces, (gain_ref, w_own, w_other) = refs[:count], refs[count : count + 3]
    out_ref, rows_ref = refs[-2:]
    core = place()[1]
    cols = w_own.shape[1]
    at = 0
    for piece in pieces:
        span = slice(at, at + piece.shape[0])
        rows_ref[span, :] = rms_rows(piece[...].astype(jnp.float32), gain_ref)
        at += piece.shape[0]
    for which, weights in ((core, w_own), (1 - core, w_other)):
        span = pl.ds(pl.multiple_of(which * cols, cols), cols)
        out_ref[:, span] = jnp.dot(
            rows_ref[...], weights[...], preferred_element_type=jnp.float32
        ).astype(jnp.bfloat16)


def project_call(pieces, gain, w_own, w_other, *earlier):
    rows, width = sum(p.shape[0] for p in pieces), pieces[0].shape[1]
    return pl.pallas_call(
        functools.partial(project_kernel, len(pieces)),
        out_shape=jax.ShapeDtypeStruct((rows, CORES * w_own.shape[1]), jnp.bfloat16),
        in_specs=[vmem()] * (len(pieces) + 3) + [anywhere()] * len(earlier),
        out_specs=vmem(),
        scratch_shapes=[pltpu.VMEM((rows, width), jnp.bfloat16)],
        cost_estimate=LONG,
        compiler_params=params(16),
        name="project",
    )(*pieces, gain, w_own, w_other, *earlier)


def pack_kernel(own, by_x, by_y, by_xy, segs_ref, routes_ref, shares_ref, out_ref):
    chip = place()[0]
    rows, width = own.shape
    for hop_by, piece in enumerate((own, by_x, by_y, by_xy)):

        @pl.when(chip ^ hop_by == CHIPS - 1)
        def _(piece=piece):
            out_ref[:rows, :] = piece[...]

    experts = PAGE // 2
    named = lax.broadcasted_iota(jnp.int32, (experts, rows), 0)
    table = jnp.zeros((experts, rows), jnp.float32)
    for k in range(TOP):
        routed = jnp.broadcast_to(routes_ref[k : k + 1, :], (experts, rows)) == named
        table = table + jnp.where(routed, shares_ref[k : k + 1, :], 0.0)
    segs = jnp.broadcast_to(segs_ref[...].astype(jnp.float32), (experts, rows))
    out_ref[rows:, :rows] = jnp.concatenate([segs, table], axis=0).astype(jnp.bfloat16)
    for part in (1, 2):
        table = table - table.astype(jnp.bfloat16).astype(jnp.float32)
        out_ref[rows:, part * rows : (part + 1) * rows] = jnp.concatenate(
            [segs, table], axis=0
        ).astype(jnp.bfloat16)
    out_ref[rows:, 3 * rows :] = jnp.zeros((PAGE, width - 3 * rows), jnp.bfloat16)


def pack_call(pieces, segment_ids, routes, shares):
    rows, width = pieces[0].shape
    return pl.pallas_call(
        pack_kernel,
        out_shape=jax.ShapeDtypeStruct((rows + PAGE, width), jnp.bfloat16),
        in_specs=[vmem()] * (CHIPS + 3),
        out_specs=vmem(),
        compiler_params=params(16),
        name="pack_kv",
    )(*pieces, segment_ids.reshape(1, rows), routes.T, shares.T)


def choose_kernel(own, prev, *out_refs):
    chip = place()[0]
    rows = own.shape[0] - PAGE
    row_id = lax.broadcasted_iota(jnp.int32, (PAGE, own.shape[1]), 0)
    for hop_by, out_ref in enumerate(out_refs, 1):
        later = (chip ^ hop_by) > chip

        @pl.when(later)
        def _(out_ref=out_ref):
            out_ref[...] = own[...]

        @pl.when(jnp.logical_not(later))
        def _(out_ref=out_ref):
            out_ref[:rows, :] = prev[:rows, :]
            below, mine = prev[rows:, :].astype(jnp.float32), own[rows:, :].astype(jnp.float32)
            out_ref[rows:, :] = jnp.where(row_id < PAGE // 2, below, mine).astype(jnp.bfloat16)


def choose_call(own, prev):
    return pl.pallas_call(
        choose_kernel,
        out_shape=(jax.ShapeDtypeStruct(own.shape, own.dtype),) * (CHIPS - 1),
        in_specs=[vmem()] * 2,
        out_specs=(vmem(),) * (CHIPS - 1),
        compiler_params=params(16),
        name="choose_kv",
    )(own, prev)


def attend_kernel(*refs):
    projected, refs = refs[:CHIPS], refs[CHIPS:]
    windows, refs = refs[: 2 * (CHIPS + 1)], refs[2 * (CHIPS + 1) :]
    out_ref, q_ref, s_ref, top_ref, sum_ref, acc_ref = refs
    chip, core = place()
    seq = lax.axis_index("seq")
    rows = out_ref.shape[0]
    per_group = HEADS // KV_HEADS
    per_chip = HEADS // (CHIPS - 1)
    block_rows = rows * CORES * CHIPS
    own_first = seq * block_rows + (chip * CORES + core) * rows

    def segs_of(ref):
        return ref[rows : rows + 1, :rows].astype(jnp.float32)

    own_segs = segs_of(windows[0])
    query_seg = jnp.broadcast_to(own_segs, (rows, rows)).T
    query_pos = lax.broadcasted_iota(jnp.int32, (rows, rows), 0) + own_first
    lane = lax.broadcasted_iota(jnp.int32, (rows, rows), 1)
    lowest = jnp.min(own_segs)

    for hop_by, piece in enumerate(projected):
        source = chip ^ hop_by

        @pl.when(source < CHIPS - 1)
        def _(source=source, piece=piece):
            for i in range(per_chip):
                start = pl.multiple_of((source * per_chip + i) * rows, rows)
                q_ref[pl.ds(start, rows), :] = piece[:, i * HEAD : (i + 1) * HEAD]

    pairs = []
    for n in range(CHIPS + 1):
        if n == 0:
            base, source = seq, chip
        elif n == CHIPS:
            base, source = seq - 1, chip
        else:
            source = chip ^ n
            base = jnp.where(source < chip, seq, seq - 1)
        first = base * block_rows + source * CORES * rows
        refs = (windows[n], windows[n + CHIPS + 1])
        pairs.append((refs, (first + core * rows, first + (1 - core) * rows)))

    scale = math.log2(math.e) / math.sqrt(HEAD)
    group_rows = per_group * rows
    used = []
    for n, (refs, firsts) in enumerate(pairs):
        use = (firsts[0] >= 0) & (firsts[0] <= own_first)
        last_seg = jnp.max(jnp.maximum(segs_of(refs[0]), segs_of(refs[1])))
        used.append(use & (last_seg >= lowest))

        def scores_of(n=n, refs=refs, firsts=firsts):
            bias = []
            for ref, first in zip(refs, firsts):
                allowed = (segs_of(ref) == query_seg) & (first + lane <= query_pos)
                bias.append(jnp.where(allowed, 0.0, -jnp.inf))
            bias = jnp.concatenate(bias, axis=1)
            for g in range(KV_HEADS):
                span = slice(g * HEAD, (g + 1) * HEAD)
                keys = jnp.concatenate([ref[:rows, span] for ref in refs], axis=0)
                part = slice(g * group_rows, (g + 1) * group_rows)
                scores = lax.dot_general(
                    q_ref[part, :], keys, (((1,), (1,)), ((), ())),
                    preferred_element_type=jnp.float32,
                )
                scores = scores.reshape(per_group, rows, 2 * rows) * scale + bias[None]
                scores = scores.reshape(group_rows, 2 * rows)
                s_ref[n, part, :] = scores
                high = jnp.maximum(scores[:, :rows], scores[:, rows:])
                top_ref[part, :] = high if n == 0 else jnp.maximum(top_ref[part, :], high)

        if n == 0:
            scores_of()
        else:
            pl.when(used[n])(scores_of)

    top_ref[...] = jnp.broadcast_to(jnp.max(top_ref[...], axis=1, keepdims=True), top_ref.shape)
    for n, (refs, firsts) in enumerate(pairs):

        def weigh(n=n, refs=refs):
            for g in range(KV_HEADS):
                part = slice(g * group_rows, (g + 1) * group_rows)
                top = top_ref[part, :]
                weights = jnp.exp2(s_ref[n, part, :] - jnp.concatenate([top, top], axis=1))
                span = slice((KV_HEADS + g) * HEAD, (KV_HEADS + g + 1) * HEAD)
                values = jnp.concatenate([ref[:rows, span] for ref in refs], axis=0)
                made = jnp.dot(
                    weights.astype(jnp.bfloat16), values, preferred_element_type=jnp.float32
                )
                sums = weights[:, :rows] + weights[:, rows:]
                if n == 0:
                    sum_ref[part, :] = sums
                    acc_ref[part, :] = made
                else:
                    sum_ref[part, :] += sums
                    acc_ref[part, :] += made

        if n == 0:
            weigh()
        else:
            pl.when(used[n])(weigh)

    for head in range(HEADS):
        part = slice(head * rows, (head + 1) * rows)
        total = jnp.sum(sum_ref[part, :], axis=1, keepdims=True)
        out_ref[:, head * HEAD : (head + 1) * HEAD] = (acc_ref[part, :] / total).astype(
            jnp.bfloat16
        )


def attend_call(projected, windows):
    rows = projected[0].shape[0]
    wide = HEADS * rows
    return pl.pallas_call(
        attend_kernel,
        out_shape=jax.ShapeDtypeStruct((rows, HEADS * HEAD), jnp.bfloat16),
        in_specs=[vmem()] * (len(projected) + len(windows)),
        out_specs=vmem(),
        scratch_shapes=[
            pltpu.VMEM((wide, HEAD), jnp.bfloat16),
            pltpu.VMEM((CHIPS + 1, wide, 2 * rows), jnp.float32),
            pltpu.VMEM((wide, rows), jnp.float32),
            pltpu.VMEM((wide, rows), jnp.float32),
            pltpu.VMEM((wide, HEAD), jnp.float32),
        ],
        compiler_params=params(32),
        name="attend",
    )(*projected, *windows)


def assemble_kernel(same, other, out_ref):
    chip, core = place()
    cols = same[0].shape[0]
    for pieces, which in ((same, core), (other, 1 - core)):
        done = 0
        for piece in pieces:
            count = piece.shape[0]
            start = ((chip ^ (done // cols)) * CORES + which) * cols + done % cols
            out_ref[pl.ds(pl.multiple_of(start, PAGE), count), :] = piece[...]
            done += count


def assemble_call(same, other):
    shape = (CORES * CHIPS * same[0].shape[0], same[0].shape[1])
    count = len(same)
    return pl.pallas_call(
        lambda *refs: assemble_kernel(refs[:count], refs[count:-1], refs[-1]),
        out_shape=jax.ShapeDtypeStruct(shape, jnp.bfloat16),
        in_specs=[vmem()] * (2 * count),
        out_specs=vmem(),
        compiler_params=params(16),
        name="assemble_w_out",
    )(*same, *other)


def expert_kernel(tile, pieces, count, *refs):
    tables, (w_ref, gain_ref), held = refs[:2], refs[2:4], refs[4:10]
    context, tokens = refs[10 : 10 + pieces], refs[10 + pieces : 10 + pieces + count]
    outs, (rows_ref, hidden_ref, total_ref) = refs[-5:-3], refs[-3:]
    chip, core = place()
    rows, width = outs[0].shape
    hidden = hidden_ref.shape[1]
    spans = [slice(i * rows, (i + 1) * rows) for i in range(2)]
    at = 0
    for piece in context:
        rows_ref[at : at + piece.shape[0], :] = piece[...]
        at += piece.shape[0]
    added = lax.dot_general(
        rows_ref[...], w_ref[...], (((1,), (1,)), ((), ())), preferred_element_type=jnp.float32
    )
    at = 0
    for piece in tokens:
        span = slice(at, at + piece.shape[0])
        at += piece.shape[0]
        residual = (piece[...].astype(jnp.float32) + added[span]).astype(jnp.bfloat16)
        wide = residual.astype(jnp.float32)
        if outs[0].dtype == jnp.float32 and span.start == 0:
            total_ref[span, :] = wide
        else:
            total_ref[span, :] = jnp.zeros_like(wide)
        rows_ref[span, :] = rms_rows(wide, gain_ref)

    for which in range(CORES):
        expert = chip * CORES + (core if which == 0 else 1 - core)
        gate, up, down = held[3 * which : 3 * which + 3]
        shares = []
        for table in tables:
            below = table[rows:, :].astype(jnp.float32)
            row_id = lax.broadcasted_iota(jnp.int32, below.shape, 0)
            row = jnp.sum(
                jnp.where(row_id == PAGE // 2 + expert, below, 0.0), axis=0, keepdims=True
            )
            row = row[:, :rows] + row[:, rows : 2 * rows] + row[:, 2 * rows : 3 * rows]
            shares.append(jnp.broadcast_to(row, (rows, rows)).T[:, :1])
        for column in range(0, hidden, tile):
            span = slice(column, column + tile)
            gate_out = jnp.dot(rows_ref[...], gate[:, span], preferred_element_type=jnp.float32)
            up_out = jnp.dot(rows_ref[...], up[:, span], preferred_element_type=jnp.float32)
            hidden_ref[:, span] = (jnp.maximum(gate_out, 0.0) * up_out).astype(jnp.bfloat16)
        for column in range(0, width, 2 * tile):
            cols = slice(column, column + 2 * tile)
            made = jnp.dot(hidden_ref[...], down[:, cols], preferred_element_type=jnp.float32)
            made = made.astype(jnp.bfloat16).astype(jnp.float32)
            for span, share, out_ref in zip(spans, shares, outs):
                total = total_ref[span, cols] + share * made[span]
                if which == 0:
                    total_ref[span, cols] = total
                else:
                    out_ref[:, cols] = total.astype(out_ref.dtype)


def expert_call(context, tokens, tables, w_all, gain, weights, kinds, *earlier):
    rows, width = tokens[0].shape
    hidden = weights[0].shape[1]
    return pl.pallas_call(
        functools.partial(expert_kernel, 256, len(context), len(tokens)),
        out_shape=tuple(jax.ShapeDtypeStruct((rows, width), kind) for kind in kinds),
        in_specs=[vmem()] * (10 + len(context) + len(tokens)) + [anywhere()] * len(earlier),
        out_specs=(vmem(), vmem()),
        scratch_shapes=[
            pltpu.VMEM((2 * rows, width), jnp.bfloat16),
            pltpu.VMEM((2 * rows, hidden), jnp.bfloat16),
            pltpu.VMEM((2 * rows, width), jnp.float32),
        ],
        cost_estimate=LONG,
        compiler_params=params(32),
        name="experts",
    )(*tables, w_all, gain, *weights, *context, *tokens, *earlier)


def mix_kernel(own, by_x, by_y, by_xy, out_ref):
    total = by_x[...].astype(jnp.float32) + by_y[...].astype(jnp.float32)
    total = total + by_xy[...].astype(jnp.float32)
    out_ref[...] = (own[...] + total).astype(jnp.bfloat16)


def mix_call(pieces):
    return pl.pallas_call(
        mix_kernel,
        out_shape=jax.ShapeDtypeStruct(pieces[0].shape, jnp.bfloat16),
        in_specs=[vmem()] * CHIPS,
        out_specs=vmem(),
        compiler_params=params(16),
        name="mix",
    )(*pieces)


def cache_kernel(table_ref, *refs):
    same, other, (out_ref, held) = refs[:2], refs[2:4], refs[4:]
    core = place()[1]
    page_rows = held.shape[1]
    pages = page_rows // PAGE
    for i, hop_by in enumerate(ORDER):
        source = (CHIPS - 1 ^ hop_by) * CORES
        span = slice(i % 2 * page_rows, (i % 2 + 1) * page_rows)
        held[source + core] = same[i // 2][span, :]
        held[source + 1 - core] = other[i // 2][span, :]

    def one(logical, carry):
        slot = table_ref[0, logical]
        to = slot // pages

        @pl.when(lax.rem(to, CORES) == core)
        def _():
            from_row = pl.multiple_of(lax.rem(logical, pages) * PAGE, PAGE)
            to_row = pl.multiple_of(lax.rem(slot, pages) * PAGE, PAGE)
            out_ref[to // CORES, pl.ds(to_row, PAGE), :] = held[
                logical // pages, pl.ds(from_row, PAGE), :
            ]

        return carry

    lax.fori_loop(0, table_ref.shape[1], one, 0, unroll=8)


def cache_call(page_table, same, other):
    rows, width = same[0].shape[0] // 2, same[0].shape[1]
    return pl.pallas_call(
        cache_kernel,
        out_shape=jax.ShapeDtypeStruct((CHIPS, rows, width), jnp.bfloat16),
        in_specs=[pl.BlockSpec(memory_space=pltpu.SMEM)] + [vmem()] * 4,
        out_specs=vmem(),
        scratch_shapes=[pltpu.VMEM((CORES * CHIPS, rows, width), jnp.bfloat16)],
        cost_estimate=LONG,
        compiler_params=params(16),
        name="cache_pages",
    )(page_table, *same, *other)


def join_kernel(*refs):
    pieces, out_ref = refs[:CHIPS], refs[CHIPS]
    for hop_by, piece in enumerate(pieces):

        @pl.when(place()[0] ^ hop_by == CHIPS - 1)
        def _(piece=piece):
            out_ref[...] = piece[...]


def join_call(pieces):
    return pl.pallas_call(
        join_kernel,
        out_shape=jax.ShapeDtypeStruct(pieces[0].shape, pieces[0].dtype),
        in_specs=[vmem()] * CHIPS,
        out_specs=vmem(),
        compiler_params=params(16),
        name="join_pages",
    )(*pieces)


def hold_kernel(in_ref, *refs):
    refs[-1][...] = in_ref[...]


def hold_call(value, *earlier):
    return pl.pallas_call(
        hold_kernel,
        out_shape=jax.ShapeDtypeStruct(value.shape, value.dtype),
        in_specs=[vmem()] + [anywhere()] * len(earlier),
        out_specs=vmem(),
        cost_estimate=LONG,
        compiler_params=params(16),
        name="hold",
    )(value, *earlier)


def after(value, other):
    return lax.optimization_barrier((value, other))[0]


def chip_body(
    tokens, segment_ids, page_table, attn_gain, w_qkv, w_out, moe_gain,
    route_ids, route_weight, w_gate, w_up, w_down,
):
    rows = tokens.shape[0]
    seq_size = lax.axis_size("seq")

    def chips(value, by):
        return hop(value, CORES * by)

    gate, up, down = w_gate[0], w_up[0], w_down[0]
    w_own = w_out.T

    tokens_x, tokens_y = chips(tokens, 1), chips(tokens, 2)
    w_qkv_other, gate_other = hop(w_qkv, 1), hop(gate, 1)
    tokens_xy = [chips(tokens_y[: rows // 2], 1), chips(tokens_x[rows // 2 :], 2)]
    late = project_call((tokens_x, tokens_y), attn_gain, w_qkv, w_qkv_other)
    made = project_call((tokens, *tokens_xy), attn_gain, w_qkv, w_qkv_other, late)
    projected = [made[:rows], chips(late[:rows], 1), chips(late[rows:], 2), chips(made[rows:], 3)]
    up_other = hop(after(up, tokens_x), 1)

    paged = cache_call(page_table, (made, late), (hop(made, 1), hop(after(late, made), 1)))
    own_kv = pack_call(
        after(projected, (paged, gate_other, up_other)), segment_ids, route_ids, route_weight
    )
    prev_kv = lax.ppermute(own_kv, "seq", [(i, i + 1) for i in range(seq_size - 1)])
    w_going, down_going = after((w_own, down), own_kv)
    w_x, w_y = chips(w_going, 1), chips(w_going, 2)
    down_other, w_own_other = hop(down_going, 1), hop(w_going, 1)

    sent = choose_call(own_kv, after(prev_kv, (w_x, w_y, down_other, w_own_other)))
    kv_xy, kv_x, kv_y = chips(sent[2], 3), chips(sent[0], 1), chips(sent[1], 2)
    kv_xy = hold_call(kv_xy)
    half = w_own.shape[0] // 2
    w_relayed = [hold_call(w_y[:half], *sent), hold_call(w_x[half:], *sent)]
    w_diagonal = [chips(w_relayed[0], 1), chips(w_relayed[1], 2)]
    windows = [own_kv, kv_x, kv_y, kv_xy, prev_kv]
    windows_other = [hop(w, 1) for w in windows]
    w_other = [w_own_other] + [hop(after(w, sent), 1) for w in (w_x, w_y)]
    windows_other = after(windows_other, (w_other, w_relayed))
    context = after(attend_call(projected, windows + windows_other), w_diagonal)
    context_x, context_y = chips(context, 1), chips(context, 2)
    context_xy = [chips(context_y[: rows // 2], 1), chips(context_x[rows // 2 :], 2)]
    last = CHIPS - 1
    paged = after(paged, (context_x, context_y))
    pages = [paged[last]]
    for by in (1, 2, 3):
        pairs = [(last * CORES + k, (last ^ by) * CORES + k) for k in range(CORES)]
        pages.append(lax.ppermute(paged[last ^ by], "tensor", pairs))
    pages = join_call(pages)
    w_other += [hop(w, 1) for w in w_diagonal]
    w_all = assemble_call([w_own, w_x, w_y] + w_diagonal, w_other)

    weights = [gate, up, down, gate_other, up_other, down_other]
    out_x, out_y = expert_call(
        (context_x, context_y), (tokens_x, tokens_y), (kv_x, kv_y), w_all, moe_gain, weights,
        (jnp.bfloat16, jnp.bfloat16),
    )
    back_x, back_y = hold_call(chips(out_x, 1)), hold_call(chips(out_y, 2))
    out, out_xy = expert_call(
        (context, *context_xy), (tokens, *tokens_xy), (own_kv, kv_xy), w_all, moe_gain, weights,
        (jnp.float32, jnp.bfloat16), out_x, pages,
    )
    back_xy = chips(out_xy, 3)
    mixed = mix_call((out, back_x, back_y, back_xy))
    return (mixed, pages.reshape(rows // PAGE, PAGE, pages.shape[1]))


def from_behind(value, axis, by):
    length = lax.axis_size(axis)
    pairs = [(i, i + by) for i in range(length) if 0 <= i + by < length]
    return lax.ppermute(value, axis, pairs)


def rms_scaled(values, scales):
    wide = values.astype(jnp.float32)
    mean_sq = jnp.mean(wide * wide, axis=-1, keepdims=True)
    return (wide * lax.rsqrt(mean_sq + epsilon) * scales).astype(jnp.bfloat16)


def attend(queries, keys_window, values_window, allowed):
    scores = jnp.einsum(
        "qhd,kd->hqk", queries, keys_window, preferred_element_type=jnp.float32
    ) / math.sqrt(queries.shape[-1])
    scores = jnp.where(allowed[None], scores, -jnp.inf)
    highest = jnp.max(scores, axis=-1, keepdims=True)
    weights = jnp.exp(scores - highest)
    totals = jnp.sum(weights, axis=-1, keepdims=True)
    shares = (weights / totals).astype(jnp.bfloat16)
    return jnp.einsum("hqk,kd->qhd", shares, values_window, preferred_element_type=jnp.float32)


def block_body(
    tokens,
    segment_ids,
    page_table,
    attn_gain,
    w_qkv,
    w_out,
    moe_gain,
    route_ids,
    route_weight,
    w_gate,
    w_up,
    w_down,
):
    tok_rows = tokens.shape[0]
    tensor_size = lax.axis_size("tensor")
    tensor_index = lax.axis_index("tensor")
    seq_index = lax.axis_index("seq")
    block_rows = tok_rows * tensor_size
    normed = rms_scaled(tokens, attn_gain)
    block_normed = lax.all_gather(normed, "tensor", axis=0, tiled=True)
    own_columns = jnp.dot(block_normed, w_qkv, preferred_element_type=jnp.float32).astype(
        jnp.bfloat16
    )
    projected = lax.all_to_all(own_columns, "tensor", split_axis=0, concat_axis=1, tiled=True)
    query_width = HEADS * HEAD
    queries = projected[:, :query_width].reshape(tok_rows, HEADS, HEAD)
    own_kv = projected[:, query_width:]
    block_kv, block_segs = (
        lax.all_gather(own_kv, "tensor", axis=0, tiled=True),
        lax.all_gather(segment_ids, "tensor", axis=0, tiled=True),
    )
    earlier_kv, earlier_seg_block = from_behind((block_kv, block_segs), "seq", 1)
    pages_here = tok_rows // PAGE
    pages_block = block_rows // PAGE
    slot_ids = tensor_index * pages_here + jnp.arange(pages_here, dtype=jnp.int32)
    matches = page_table[0][None, :] == slot_ids[:, None]
    logical = jnp.sum(
        jnp.where(matches, jnp.arange(pages_block, dtype=jnp.int32)[None, :], 0), axis=1
    )
    cache_pages = block_kv.reshape(pages_block, PAGE, block_kv.shape[1])[logical]
    all_kv = jnp.concatenate([earlier_kv, block_kv], axis=0)
    all_segs = jnp.concatenate([earlier_seg_block, block_segs], axis=0)
    window = block_rows + tok_rows
    first_key = tensor_index * tok_rows
    keys_window = lax.dynamic_slice_in_dim(all_kv, first_key, window, 0)
    segs_window = lax.dynamic_slice_in_dim(all_segs, first_key, window, 0)
    key_pos = (seq_index - 1) * block_rows + first_key + jnp.arange(window, dtype=jnp.int32)
    query_pos = seq_index * block_rows + first_key + jnp.arange(tok_rows, dtype=jnp.int32)
    allowed = (
        (segs_window[None, :] == segment_ids[:, None])
        & (key_pos[None, :] <= query_pos[:, None])
        & (key_pos[None, :] >= 0)
    )
    per_group = HEADS // KV_HEADS
    contexts = []
    for kv_group in range(KV_HEADS):
        key_cols = keys_window[:, kv_group * HEAD : (kv_group + 1) * HEAD]
        value_cols = keys_window[:, (KV_HEADS + kv_group) * HEAD : (KV_HEADS + kv_group + 1) * HEAD]
        contexts.append(
            attend(
                queries[:, kv_group * per_group : (kv_group + 1) * per_group],
                key_cols,
                value_cols,
                allowed,
            )
        )
    context = jnp.concatenate(contexts, axis=1).reshape(tok_rows, query_width).astype(jnp.bfloat16)
    attn_out = jnp.dot(
        context,
        lax.all_gather(w_out, "tensor", axis=1, tiled=True),
        preferred_element_type=jnp.float32,
    )
    residual = (tokens.astype(jnp.float32) + attn_out).astype(jnp.bfloat16)
    expert_input = rms_scaled(residual, moe_gain)
    experts_all = w_gate.shape[0] * tensor_size
    capacity = max(2, 3 * tok_rows * TOP // (2 * experts_all))
    flat_routes = route_ids.reshape(-1)
    expert_hits = (
        flat_routes[:, None] == jnp.arange(experts_all, dtype=jnp.int32)[None, :]
    ).astype(jnp.int32)
    earlier_hits = jnp.cumsum(expert_hits, axis=0) - expert_hits
    slot_rank = jnp.sum(earlier_hits * expert_hits, axis=1)
    dest_slot = flat_routes * capacity + slot_rank
    slot_table = (
        jnp.arange(experts_all * capacity, dtype=jnp.int32)[:, None, None]
        == dest_slot.reshape(tok_rows, TOP)[None]
    )
    dispatch = jnp.any(slot_table, axis=2).astype(jnp.bfloat16)
    outgoing = jnp.dot(dispatch, expert_input, preferred_element_type=jnp.float32).astype(
        jnp.bfloat16
    )
    outgoing = outgoing.reshape(experts_all, capacity, expert_input.shape[1])
    arrived = lax.all_to_all(outgoing, "tensor", split_axis=0, concat_axis=0, tiled=True)
    rows_flat = arrived.reshape(-1, arrived.shape[-1])
    gate_out = jnp.dot(rows_flat, w_gate[0], preferred_element_type=jnp.float32)
    up_out = jnp.dot(rows_flat, w_up[0], preferred_element_type=jnp.float32)
    hidden = (jnp.maximum(gate_out, 0.0) * up_out).astype(jnp.bfloat16)
    produced = jnp.dot(hidden, w_down[0], preferred_element_type=jnp.float32).astype(jnp.bfloat16)
    returned = lax.all_to_all(
        produced.reshape(arrived.shape), "tensor", split_axis=0, concat_axis=0, tiled=True
    )
    picked = returned.reshape(-1, returned.shape[-1])[dest_slot].reshape(
        tok_rows, TOP, returned.shape[-1]
    )
    routed_sum = jnp.einsum("tk,tkd->td", route_weight, picked.astype(jnp.float32))
    mixed = (residual.astype(jnp.float32) + routed_sum).astype(jnp.bfloat16)
    return (mixed, cache_pages)


def by_chips(mesh):
    size = mesh.shape["tensor"]
    return size == CORES * CHIPS and (HEADS + 2 * KV_HEADS) % size == 0


def solution(mesh):
    return jax.shard_map(
        chip_body if by_chips(mesh) else block_body,
        mesh=mesh,
        in_specs=(
            P(("seq", "tensor"), None),
            P(("seq", "tensor")),
            P("seq", None),
            P(),
            P(None, "tensor"),
            P(None, "tensor"),
            P(),
            P(("seq", "tensor"), None),
            P(("seq", "tensor"), None),
            P("tensor", None, None),
            P("tensor", None, None),
            P("tensor", None, None),
        ),
        out_specs=(P(("seq", "tensor"), None), P(("seq", "tensor"), None, None)),
        check_vma=False,
    )
```

```python
import functools
import math

import jax
import jax.numpy as jnp
from jax import lax
from jax.experimental import pallas as pl
from jax.experimental.pallas import tpu as pltpu
from jax.sharding import PartitionSpec as P

HEADS = 12
KV_HEADS = 2
HEAD = 128
TOP = 4
PAGE = 16
CORES = 2
CHIPS = 4


epsilon = 1e-06
MIB = 1024 * 1024


LONG = pl.CostEstimate(flops=20 * 10**9, bytes_accessed=1, transcendentals=0)


ORDER = (0, 3, 1, 2)


def vmem():
    return pl.BlockSpec(memory_space=pltpu.VMEM)


def anywhere():
    return pl.BlockSpec(memory_space=pl.ANY)


def params(mib):
    return pltpu.CompilerParams(vmem_limit_bytes=mib * MIB)


def place():
    index = lax.axis_index("tensor")
    return index // CORES, lax.rem(index, CORES)


def hop(value, by):
    length = lax.axis_size("tensor")
    return lax.ppermute(value, "tensor", [(i, i ^ by) for i in range(length)])


def rms_rows(wide, gain_ref):
    mean_sq = jnp.mean(wide * wide, axis=-1, keepdims=True)
    return (wide * lax.rsqrt(mean_sq + epsilon) * gain_ref[...]).astype(jnp.bfloat16)


def project_kernel(count, *refs):
    pieces, (gain_ref, w_own, w_other) = refs[:count], refs[count : count + 3]
    out_ref, rows_ref = refs[-2:]
    core = place()[1]
    cols = w_own.shape[1]
    at = 0
    for piece in pieces:
        span = slice(at, at + piece.shape[0])
        rows_ref[span, :] = rms_rows(piece[...].astype(jnp.float32), gain_ref)
        at += piece.shape[0]
    for which, weights in ((core, w_own), (1 - core, w_other)):
        span = pl.ds(pl.multiple_of(which * cols, cols), cols)
        out_ref[:, span] = jnp.dot(
            rows_ref[...], weights[...], preferred_element_type=jnp.float32
        ).astype(jnp.bfloat16)


def project_call(pieces, gain, w_own, w_other, *earlier):
    rows, width = sum(p.shape[0] for p in pieces), pieces[0].shape[1]
    return pl.pallas_call(
        functools.partial(project_kernel, len(pieces)),
        out_shape=jax.ShapeDtypeStruct((rows, CORES * w_own.shape[1]), jnp.bfloat16),
        in_specs=[vmem()] * (len(pieces) + 3) + [anywhere()] * len(earlier),
        out_specs=vmem(),
        scratch_shapes=[pltpu.VMEM((rows, width), jnp.bfloat16)],
        cost_estimate=LONG,
        compiler_params=params(16),
        name="project",
    )(*pieces, gain, w_own, w_other, *earlier)


def pack_kernel(own, by_x, by_y, by_xy, segs_ref, routes_ref, shares_ref, out_ref):
    chip = place()[0]
    rows, width = own.shape
    for hop_by, piece in enumerate((own, by_x, by_y, by_xy)):

        @pl.when(chip ^ hop_by == CHIPS - 1)
        def _(piece=piece):
            out_ref[:rows, :] = piece[...]

    experts = PAGE // 2
    named = lax.broadcasted_iota(jnp.int32, (experts, rows), 0)
    table = jnp.zeros((experts, rows), jnp.float32)
    for k in range(TOP):
        routed = jnp.broadcast_to(routes_ref[k : k + 1, :], (experts, rows)) == named
        table = table + jnp.where(routed, shares_ref[k : k + 1, :], 0.0)
    segs = jnp.broadcast_to(segs_ref[...].astype(jnp.float32), (experts, rows))
    out_ref[rows:, :rows] = jnp.concatenate([segs, table], axis=0).astype(jnp.bfloat16)
    for part in (1, 2):
        table = table - table.astype(jnp.bfloat16).astype(jnp.float32)
        out_ref[rows:, part * rows : (part + 1) * rows] = jnp.concatenate(
            [segs, table], axis=0
        ).astype(jnp.bfloat16)
    out_ref[rows:, 3 * rows :] = jnp.zeros((PAGE, width - 3 * rows), jnp.bfloat16)


def pack_call(pieces, segment_ids, routes, shares):
    rows, width = pieces[0].shape
    return pl.pallas_call(
        pack_kernel,
        out_shape=jax.ShapeDtypeStruct((rows + PAGE, width), jnp.bfloat16),
        in_specs=[vmem()] * (CHIPS + 3),
        out_specs=vmem(),
        compiler_params=params(16),
        name="pack_kv",
    )(*pieces, segment_ids.reshape(1, rows), routes.T, shares.T)


def choose_kernel(own, prev, *out_refs):
    chip = place()[0]
    rows = own.shape[0] - PAGE
    row_id = lax.broadcasted_iota(jnp.int32, (PAGE, own.shape[1]), 0)
    for hop_by, out_ref in enumerate(out_refs, 1):
        later = (chip ^ hop_by) > chip

        @pl.when(later)
        def _(out_ref=out_ref):
            out_ref[...] = own[...]

        @pl.when(jnp.logical_not(later))
        def _(out_ref=out_ref):
            out_ref[:rows, :] = prev[:rows, :]
            below, mine = prev[rows:, :].astype(jnp.float32), own[rows:, :].astype(jnp.float32)
            out_ref[rows:, :] = jnp.where(row_id < PAGE // 2, below, mine).astype(jnp.bfloat16)


def choose_call(own, prev):
    return pl.pallas_call(
        choose_kernel,
        out_shape=(jax.ShapeDtypeStruct(own.shape, own.dtype),) * (CHIPS - 1),
        in_specs=[vmem()] * 2,
        out_specs=(vmem(),) * (CHIPS - 1),
        compiler_params=params(16),
        name="choose_kv",
    )(own, prev)


def attend_kernel(*refs):
    projected, refs = refs[:CHIPS], refs[CHIPS:]
    windows, refs = refs[: 2 * (CHIPS + 1)], refs[2 * (CHIPS + 1) :]
    out_ref, q_ref, s_ref, top_ref, sum_ref, acc_ref = refs
    chip, core = place()
    seq = lax.axis_index("seq")
    rows = out_ref.shape[0]
    per_group = HEADS // KV_HEADS
    per_chip = HEADS // (CHIPS - 1)
    block_rows = rows * CORES * CHIPS
    own_first = seq * block_rows + (chip * CORES + core) * rows

    def segs_of(ref):
        return ref[rows : rows + 1, :rows].astype(jnp.float32)

    own_segs = segs_of(windows[0])
    query_seg = jnp.broadcast_to(own_segs, (rows, rows)).T
    query_pos = lax.broadcasted_iota(jnp.int32, (rows, rows), 0) + own_first
    lane = lax.broadcasted_iota(jnp.int32, (rows, rows), 1)
    lowest = jnp.min(own_segs)

    for hop_by, piece in enumerate(projected):
        source = chip ^ hop_by

        @pl.when(source < CHIPS - 1)
        def _(source=source, piece=piece):
            for i in range(per_chip):
                start = pl.multiple_of((source * per_chip + i) * rows, rows)
                q_ref[pl.ds(start, rows), :] = piece[:, i * HEAD : (i + 1) * HEAD]

    pairs = []
    for n in range(CHIPS + 1):
        if n == 0:
            base, source = seq, chip
        elif n == CHIPS:
            base, source = seq - 1, chip
        else:
            source = chip ^ n
            base = jnp.where(source < chip, seq, seq - 1)
        first = base * block_rows + source * CORES * rows
        refs = (windows[n], windows[n + CHIPS + 1])
        pairs.append((refs, (first + core * rows, first + (1 - core) * rows)))

    scale = math.log2(math.e) / math.sqrt(HEAD)
    group_rows = per_group * rows
    used = []
    for n, (refs, firsts) in enumerate(pairs):
        use = (firsts[0] >= 0) & (firsts[0] <= own_first)
        last_seg = jnp.max(jnp.maximum(segs_of(refs[0]), segs_of(refs[1])))
        used.append(use & (last_seg >= lowest))

        def scores_of(n=n, refs=refs, firsts=firsts):
            bias = []
            for ref, first in zip(refs, firsts):
                allowed = (segs_of(ref) == query_seg) & (first + lane <= query_pos)
                bias.append(jnp.where(allowed, 0.0, -jnp.inf))
            bias = jnp.concatenate(bias, axis=1)
            for g in range(KV_HEADS):
                span = slice(g * HEAD, (g + 1) * HEAD)
                keys = jnp.concatenate([ref[:rows, span] for ref in refs], axis=0)
                part = slice(g * group_rows, (g + 1) * group_rows)
                scores = lax.dot_general(
                    q_ref[part, :], keys, (((1,), (1,)), ((), ())),
                    preferred_element_type=jnp.float32,
                )
                scores = scores.reshape(per_group, rows, 2 * rows) * scale + bias[None]
                scores = scores.reshape(group_rows, 2 * rows)
                s_ref[n, part, :] = scores
                high = jnp.maximum(scores[:, :rows], scores[:, rows:])
                top_ref[part, :] = high if n == 0 else jnp.maximum(top_ref[part, :], high)

        if n == 0:
            scores_of()
        else:
            pl.when(used[n])(scores_of)

    top_ref[...] = jnp.broadcast_to(jnp.max(top_ref[...], axis=1, keepdims=True), top_ref.shape)
    for n, (refs, firsts) in enumerate(pairs):

        def weigh(n=n, refs=refs):
            for g in range(KV_HEADS):
                part = slice(g * group_rows, (g + 1) * group_rows)
                top = top_ref[part, :]
                weights = jnp.exp2(s_ref[n, part, :] - jnp.concatenate([top, top], axis=1))
                span = slice((KV_HEADS + g) * HEAD, (KV_HEADS + g + 1) * HEAD)
                values = jnp.concatenate([ref[:rows, span] for ref in refs], axis=0)
                made = jnp.dot(
                    weights.astype(jnp.bfloat16), values, preferred_element_type=jnp.float32
                )
                sums = weights[:, :rows] + weights[:, rows:]
                if n == 0:
                    sum_ref[part, :] = sums
                    acc_ref[part, :] = made
                else:
                    sum_ref[part, :] += sums
                    acc_ref[part, :] += made

        if n == 0:
            weigh()
        else:
            pl.when(used[n])(weigh)

    for head in range(HEADS):
        part = slice(head * rows, (head + 1) * rows)
        total = jnp.sum(sum_ref[part, :], axis=1, keepdims=True)
        out_ref[:, head * HEAD : (head + 1) * HEAD] = (acc_ref[part, :] / total).astype(
            jnp.bfloat16
        )


def attend_call(projected, windows):
    rows = projected[0].shape[0]
    wide = HEADS * rows
    return pl.pallas_call(
        attend_kernel,
        out_shape=jax.ShapeDtypeStruct((rows, HEADS * HEAD), jnp.bfloat16),
        in_specs=[vmem()] * (len(projected) + len(windows)),
        out_specs=vmem(),
        scratch_shapes=[
            pltpu.VMEM((wide, HEAD), jnp.bfloat16),
            pltpu.VMEM((CHIPS + 1, wide, 2 * rows), jnp.float32),
            pltpu.VMEM((wide, rows), jnp.float32),
            pltpu.VMEM((wide, rows), jnp.float32),
            pltpu.VMEM((wide, HEAD), jnp.float32),
        ],
        compiler_params=params(32),
        name="attend",
    )(*projected, *windows)


def assemble_kernel(same, other, out_ref):
    chip, core = place()
    cols = same[0].shape[0]
    for pieces, which in ((same, core), (other, 1 - core)):
        done = 0
        for piece in pieces:
            count = piece.shape[0]
            start = ((chip ^ (done // cols)) * CORES + which) * cols + done % cols
            out_ref[pl.ds(pl.multiple_of(start, PAGE), count), :] = piece[...]
            done += count


def assemble_call(same, other):
    shape = (CORES * CHIPS * same[0].shape[0], same[0].shape[1])
    count = len(same)
    return pl.pallas_call(
        lambda *refs: assemble_kernel(refs[:count], refs[count:-1], refs[-1]),
        out_shape=jax.ShapeDtypeStruct(shape, jnp.bfloat16),
        in_specs=[vmem()] * (2 * count),
        out_specs=vmem(),
        compiler_params=params(16),
        name="assemble_w_out",
    )(*same, *other)


def expert_kernel(tile, pieces, count, *refs):
    tables, (w_ref, gain_ref), held = refs[:2], refs[2:4], refs[4:10]
    context, tokens = refs[10 : 10 + pieces], refs[10 + pieces : 10 + pieces + count]
    outs, (rows_ref, hidden_ref, total_ref) = refs[-5:-3], refs[-3:]
    chip, core = place()
    rows, width = outs[0].shape
    hidden = hidden_ref.shape[1]
    spans = [slice(i * rows, (i + 1) * rows) for i in range(2)]
    at = 0
    for piece in context:
        rows_ref[at : at + piece.shape[0], :] = piece[...]
        at += piece.shape[0]
    added = lax.dot_general(
        rows_ref[...], w_ref[...], (((1,), (1,)), ((), ())), preferred_element_type=jnp.float32
    )
    at = 0
    for piece in tokens:
        span = slice(at, at + piece.shape[0])
        at += piece.shape[0]
        residual = (piece[...].astype(jnp.float32) + added[span]).astype(jnp.bfloat16)
        wide = residual.astype(jnp.float32)
        if outs[0].dtype == jnp.float32 and span.start == 0:
            total_ref[span, :] = wide
        else:
            total_ref[span, :] = jnp.zeros_like(wide)
        rows_ref[span, :] = rms_rows(wide, gain_ref)

    for which in range(CORES):
        expert = chip * CORES + (core if which == 0 else 1 - core)
        gate, up, down = held[3 * which : 3 * which + 3]
        shares = []
        for table in tables:
            below = table[rows:, :].astype(jnp.float32)
            row_id = lax.broadcasted_iota(jnp.int32, below.shape, 0)
            row = jnp.sum(
                jnp.where(row_id == PAGE // 2 + expert, below, 0.0), axis=0, keepdims=True
            )
            row = row[:, :rows] + row[:, rows : 2 * rows] + row[:, 2 * rows : 3 * rows]
            shares.append(jnp.broadcast_to(row, (rows, rows)).T[:, :1])
        for column in range(0, hidden, tile):
            span = slice(column, column + tile)
            gate_out = jnp.dot(rows_ref[...], gate[:, span], preferred_element_type=jnp.float32)
            up_out = jnp.dot(rows_ref[...], up[:, span], preferred_element_type=jnp.float32)
            hidden_ref[:, span] = (jnp.maximum(gate_out, 0.0) * up_out).astype(jnp.bfloat16)
        for column in range(0, width, 2 * tile):
            cols = slice(column, column + 2 * tile)
            made = jnp.dot(hidden_ref[...], down[:, cols], preferred_element_type=jnp.float32)
            made = made.astype(jnp.bfloat16).astype(jnp.float32)
            for span, share, out_ref in zip(spans, shares, outs):
                total = total_ref[span, cols] + share * made[span]
                if which == 0:
                    total_ref[span, cols] = total
                else:
                    out_ref[:, cols] = total.astype(out_ref.dtype)


def expert_call(context, tokens, tables, w_all, gain, weights, kinds, *earlier):
    rows, width = tokens[0].shape
    hidden = weights[0].shape[1]
    return pl.pallas_call(
        functools.partial(expert_kernel, 256, len(context), len(tokens)),
        out_shape=tuple(jax.ShapeDtypeStruct((rows, width), kind) for kind in kinds),
        in_specs=[vmem()] * (10 + len(context) + len(tokens)) + [anywhere()] * len(earlier),
        out_specs=(vmem(), vmem()),
        scratch_shapes=[
            pltpu.VMEM((2 * rows, width), jnp.bfloat16),
            pltpu.VMEM((2 * rows, hidden), jnp.bfloat16),
            pltpu.VMEM((2 * rows, width), jnp.float32),
        ],
        cost_estimate=LONG,
        compiler_params=params(32),
        name="experts",
    )(*tables, w_all, gain, *weights, *context, *tokens, *earlier)


def mix_kernel(own, by_x, by_y, by_xy, out_ref):
    total = by_x[...].astype(jnp.float32) + by_y[...].astype(jnp.float32)
    total = total + by_xy[...].astype(jnp.float32)
    out_ref[...] = (own[...] + total).astype(jnp.bfloat16)


def mix_call(pieces):
    return pl.pallas_call(
        mix_kernel,
        out_shape=jax.ShapeDtypeStruct(pieces[0].shape, jnp.bfloat16),
        in_specs=[vmem()] * CHIPS,
        out_specs=vmem(),
        compiler_params=params(16),
        name="mix",
    )(*pieces)


def cache_kernel(table_ref, *refs):
    same, other, (out_ref, held) = refs[:2], refs[2:4], refs[4:]
    core = place()[1]
    page_rows = held.shape[1]
    pages = page_rows // PAGE
    for i, hop_by in enumerate(ORDER):
        source = (CHIPS - 1 ^ hop_by) * CORES
        span = slice(i % 2 * page_rows, (i % 2 + 1) * page_rows)
        held[source + core] = same[i // 2][span, :]
        held[source + 1 - core] = other[i // 2][span, :]

    def one(logical, carry):
        slot = table_ref[0, logical]
        to = slot // pages

        @pl.when(lax.rem(to, CORES) == core)
        def _():
            from_row = pl.multiple_of(lax.rem(logical, pages) * PAGE, PAGE)
            to_row = pl.multiple_of(lax.rem(slot, pages) * PAGE, PAGE)
            out_ref[to // CORES, pl.ds(to_row, PAGE), :] = held[
                logical // pages, pl.ds(from_row, PAGE), :
            ]

        return carry

    lax.fori_loop(0, table_ref.shape[1], one, 0, unroll=8)


def cache_call(page_table, same, other):
    rows, width = same[0].shape[0] // 2, same[0].shape[1]
    return pl.pallas_call(
        cache_kernel,
        out_shape=jax.ShapeDtypeStruct((CHIPS, rows, width), jnp.bfloat16),
        in_specs=[pl.BlockSpec(memory_space=pltpu.SMEM)] + [vmem()] * 4,
        out_specs=vmem(),
        scratch_shapes=[pltpu.VMEM((CORES * CHIPS, rows, width), jnp.bfloat16)],
        compiler_params=params(16),
        name="cache_pages",
    )(page_table, *same, *other)


def join_kernel(*refs):
    pieces, out_ref = refs[:CHIPS], refs[CHIPS]
    for hop_by, piece in enumerate(pieces):

        @pl.when(place()[0] ^ hop_by == CHIPS - 1)
        def _(piece=piece):
            out_ref[...] = piece[...]


def join_call(pieces):
    return pl.pallas_call(
        join_kernel,
        out_shape=jax.ShapeDtypeStruct(pieces[0].shape, pieces[0].dtype),
        in_specs=[vmem()] * CHIPS,
        out_specs=vmem(),
        compiler_params=params(16),
        name="join_pages",
    )(*pieces)


def hold_kernel(in_ref, *refs):
    refs[-1][...] = in_ref[...]


def hold_call(value, *earlier):
    return pl.pallas_call(
        hold_kernel,
        out_shape=jax.ShapeDtypeStruct(value.shape, value.dtype),
        in_specs=[vmem()] + [anywhere()] * len(earlier),
        out_specs=vmem(),
        cost_estimate=LONG,
        compiler_params=params(16),
        name="hold",
    )(value, *earlier)


def after(value, other):
    return lax.optimization_barrier((value, other))[0]


def chip_body(
    tokens, segment_ids, page_table, attn_gain, w_qkv, w_out, moe_gain,
    route_ids, route_weight, w_gate, w_up, w_down,
):
    rows = tokens.shape[0]
    seq_size = lax.axis_size("seq")

    def chips(value, by):
        return hop(value, CORES * by)

    gate, up, down = w_gate[0], w_up[0], w_down[0]
    w_own = w_out.T

    tokens_x, tokens_y = chips(tokens, 1), chips(tokens, 2)
    w_qkv_other, gate_other = hop(w_qkv, 1), hop(gate, 1)
    tokens_xy = [chips(tokens_y[: rows // 2], 1), chips(tokens_x[rows // 2 :], 2)]
    late = project_call((tokens_x, tokens_y), attn_gain, w_qkv, w_qkv_other)
    made = project_call((tokens, *tokens_xy), attn_gain, w_qkv, w_qkv_other, late)
    projected = [
        made[:rows],
        hold_call(chips(late[:rows], 1)),
        hold_call(chips(late[rows:], 2)),
        chips(made[rows:], 3),
    ]
    up_other = hop(after(up, tokens_x), 1)

    own_kv = pack_call(
        after(projected, (gate_other, up_other)), segment_ids, route_ids, route_weight
    )
    prev_kv = lax.ppermute(own_kv, "seq", [(i, i + 1) for i in range(seq_size - 1)])
    w_going, down_going = after((w_own, down), own_kv)
    mine = after((made, late), own_kv)
    paged = cache_call(page_table, mine, [hop(kv, 1) for kv in mine])
    w_x, w_y = chips(w_going, 1), chips(w_going, 2)
    down_other, w_own_other = hop(down_going, 1), hop(w_going, 1)

    sent = choose_call(own_kv, after(prev_kv, (w_x, w_y, down_other, w_own_other)))
    kv_xy, kv_x, kv_y = chips(sent[2], 3), chips(sent[0], 1), chips(sent[1], 2)
    kv_xy = hold_call(kv_xy)
    half = w_own.shape[0] // 2
    w_relayed = [hold_call(w_y[:half], *sent), hold_call(w_x[half:], *sent)]
    w_diagonal = [chips(w_relayed[0], 1), chips(w_relayed[1], 2)]
    windows = [own_kv, kv_x, kv_y, kv_xy, prev_kv]
    windows_other = [hop(w, 1) for w in windows]
    w_other = [w_own_other] + [hop(after(w, sent), 1) for w in (w_x, w_y)]
    windows_other = after(windows_other, (w_other, w_relayed))
    context = after(attend_call(projected, windows + windows_other), w_diagonal)
    context_x, context_y = chips(context, 1), chips(context, 2)
    context_xy = [chips(context_y[: rows // 2], 1), chips(context_x[rows // 2 :], 2)]
    last = CHIPS - 1
    paged = after(paged, (context_x, context_y))
    pages = [paged[last]]
    for by in (1, 2, 3):
        pairs = [(last * CORES + k, (last ^ by) * CORES + k) for k in range(CORES)]
        pages.append(lax.ppermute(paged[last ^ by], "tensor", pairs))
    pages = join_call(pages)
    w_other += [hop(w, 1) for w in w_diagonal]
    w_all = assemble_call([w_own, w_x, w_y] + w_diagonal, w_other)

    weights = [gate, up, down, gate_other, up_other, down_other]
    out_x, out_y = expert_call(
        (context_x, context_y), (tokens_x, tokens_y), (kv_x, kv_y), w_all, moe_gain, weights,
        (jnp.bfloat16, jnp.bfloat16),
    )
    back_x, back_y = hold_call(chips(out_x, 1)), hold_call(chips(out_y, 2))
    out, out_xy = expert_call(
        (context, *context_xy), (tokens, *tokens_xy), (own_kv, kv_xy), w_all, moe_gain, weights,
        (jnp.float32, jnp.bfloat16), out_x, pages,
    )
    back_xy = chips(out_xy, 3)
    mixed = mix_call((out, back_x, back_y, back_xy))
    return (mixed, pages.reshape(rows // PAGE, PAGE, pages.shape[1]))


def from_behind(value, axis, by):
    length = lax.axis_size(axis)
    pairs = [(i, i + by) for i in range(length) if 0 <= i + by < length]
    return lax.ppermute(value, axis, pairs)


def rms_scaled(values, scales):
    wide = values.astype(jnp.float32)
    mean_sq = jnp.mean(wide * wide, axis=-1, keepdims=True)
    return (wide * lax.rsqrt(mean_sq + epsilon) * scales).astype(jnp.bfloat16)


def attend(queries, keys_window, values_window, allowed):
    scores = jnp.einsum(
        "qhd,kd->hqk", queries, keys_window, preferred_element_type=jnp.float32
    ) / math.sqrt(queries.shape[-1])
    scores = jnp.where(allowed[None], scores, -jnp.inf)
    highest = jnp.max(scores, axis=-1, keepdims=True)
    weights = jnp.exp(scores - highest)
    totals = jnp.sum(weights, axis=-1, keepdims=True)
    shares = (weights / totals).astype(jnp.bfloat16)
    return jnp.einsum("hqk,kd->qhd", shares, values_window, preferred_element_type=jnp.float32)


def block_body(
    tokens,
    segment_ids,
    page_table,
    attn_gain,
    w_qkv,
    w_out,
    moe_gain,
    route_ids,
    route_weight,
    w_gate,
    w_up,
    w_down,
):
    tok_rows = tokens.shape[0]
    tensor_size = lax.axis_size("tensor")
    tensor_index = lax.axis_index("tensor")
    seq_index = lax.axis_index("seq")
    block_rows = tok_rows * tensor_size
    normed = rms_scaled(tokens, attn_gain)
    block_normed = lax.all_gather(normed, "tensor", axis=0, tiled=True)
    own_columns = jnp.dot(block_normed, w_qkv, preferred_element_type=jnp.float32).astype(
        jnp.bfloat16
    )
    projected = lax.all_to_all(own_columns, "tensor", split_axis=0, concat_axis=1, tiled=True)
    query_width = HEADS * HEAD
    queries = projected[:, :query_width].reshape(tok_rows, HEADS, HEAD)
    own_kv = projected[:, query_width:]
    block_kv, block_segs = (
        lax.all_gather(own_kv, "tensor", axis=0, tiled=True),
        lax.all_gather(segment_ids, "tensor", axis=0, tiled=True),
    )
    earlier_kv, earlier_seg_block = from_behind((block_kv, block_segs), "seq", 1)
    pages_here = tok_rows // PAGE
    pages_block = block_rows // PAGE
    slot_ids = tensor_index * pages_here + jnp.arange(pages_here, dtype=jnp.int32)
    matches = page_table[0][None, :] == slot_ids[:, None]
    logical = jnp.sum(
        jnp.where(matches, jnp.arange(pages_block, dtype=jnp.int32)[None, :], 0), axis=1
    )
    cache_pages = block_kv.reshape(pages_block, PAGE, block_kv.shape[1])[logical]
    all_kv = jnp.concatenate([earlier_kv, block_kv], axis=0)
    all_segs = jnp.concatenate([earlier_seg_block, block_segs], axis=0)
    window = block_rows + tok_rows
    first_key = tensor_index * tok_rows
    keys_window = lax.dynamic_slice_in_dim(all_kv, first_key, window, 0)
    segs_window = lax.dynamic_slice_in_dim(all_segs, first_key, window, 0)
    key_pos = (seq_index - 1) * block_rows + first_key + jnp.arange(window, dtype=jnp.int32)
    query_pos = seq_index * block_rows + first_key + jnp.arange(tok_rows, dtype=jnp.int32)
    allowed = (
        (segs_window[None, :] == segment_ids[:, None])
        & (key_pos[None, :] <= query_pos[:, None])
        & (key_pos[None, :] >= 0)
    )
    per_group = HEADS // KV_HEADS
    contexts = []
    for kv_group in range(KV_HEADS):
        key_cols = keys_window[:, kv_group * HEAD : (kv_group + 1) * HEAD]
        value_cols = keys_window[:, (KV_HEADS + kv_group) * HEAD : (KV_HEADS + kv_group + 1) * HEAD]
        contexts.append(
            attend(
                queries[:, kv_group * per_group : (kv_group + 1) * per_group],
                key_cols,
                value_cols,
                allowed,
            )
        )
    context = jnp.concatenate(contexts, axis=1).reshape(tok_rows, query_width).astype(jnp.bfloat16)
    attn_out = jnp.dot(
        context,
        lax.all_gather(w_out, "tensor", axis=1, tiled=True),
        preferred_element_type=jnp.float32,
    )
    residual = (tokens.astype(jnp.float32) + attn_out).astype(jnp.bfloat16)
    expert_input = rms_scaled(residual, moe_gain)
    experts_all = w_gate.shape[0] * tensor_size
    capacity = max(2, 3 * tok_rows * TOP // (2 * experts_all))
    flat_routes = route_ids.reshape(-1)
    expert_hits = (
        flat_routes[:, None] == jnp.arange(experts_all, dtype=jnp.int32)[None, :]
    ).astype(jnp.int32)
    earlier_hits = jnp.cumsum(expert_hits, axis=0) - expert_hits
    slot_rank = jnp.sum(earlier_hits * expert_hits, axis=1)
    dest_slot = flat_routes * capacity + slot_rank
    slot_table = (
        jnp.arange(experts_all * capacity, dtype=jnp.int32)[:, None, None]
        == dest_slot.reshape(tok_rows, TOP)[None]
    )
    dispatch = jnp.any(slot_table, axis=2).astype(jnp.bfloat16)
    outgoing = jnp.dot(dispatch, expert_input, preferred_element_type=jnp.float32).astype(
        jnp.bfloat16
    )
    outgoing = outgoing.reshape(experts_all, capacity, expert_input.shape[1])
    arrived = lax.all_to_all(outgoing, "tensor", split_axis=0, concat_axis=0, tiled=True)
    rows_flat = arrived.reshape(-1, arrived.shape[-1])
    gate_out = jnp.dot(rows_flat, w_gate[0], preferred_element_type=jnp.float32)
    up_out = jnp.dot(rows_flat, w_up[0], preferred_element_type=jnp.float32)
    hidden = (jnp.maximum(gate_out, 0.0) * up_out).astype(jnp.bfloat16)
    produced = jnp.dot(hidden, w_down[0], preferred_element_type=jnp.float32).astype(jnp.bfloat16)
    returned = lax.all_to_all(
        produced.reshape(arrived.shape), "tensor", split_axis=0, concat_axis=0, tiled=True
    )
    picked = returned.reshape(-1, returned.shape[-1])[dest_slot].reshape(
        tok_rows, TOP, returned.shape[-1]
    )
    routed_sum = jnp.einsum("tk,tkd->td", route_weight, picked.astype(jnp.float32))
    mixed = (residual.astype(jnp.float32) + routed_sum).astype(jnp.bfloat16)
    return (mixed, cache_pages)


def by_chips(mesh):
    size = mesh.shape["tensor"]
    return size == CORES * CHIPS and (HEADS + 2 * KV_HEADS) % size == 0


def solution(mesh):
    return jax.shard_map(
        chip_body if by_chips(mesh) else block_body,
        mesh=mesh,
        in_specs=(
            P(("seq", "tensor"), None),
            P(("seq", "tensor")),
            P("seq", None),
            P(),
            P(None, "tensor"),
            P(None, "tensor"),
            P(),
            P(("seq", "tensor"), None),
            P(("seq", "tensor"), None),
            P("tensor", None, None),
            P("tensor", None, None),
            P("tensor", None, None),
        ),
        out_specs=(P(("seq", "tensor"), None), P(("seq", "tensor"), None, None)),
        check_vma=False,
    )
```

```python
import functools
import math

import jax
import jax.numpy as jnp
from jax import lax
from jax.experimental import pallas as pl
from jax.experimental.pallas import tpu as pltpu
from jax.sharding import PartitionSpec as P

HEADS = 12
KV_HEADS = 2
HEAD = 128
TOP = 4
PAGE = 16
CORES = 2
CHIPS = 4


epsilon = 1e-06
MIB = 1024 * 1024


LONG = pl.CostEstimate(flops=20 * 10**9, bytes_accessed=1, transcendentals=0)


ORDER = (0, 3, 1, 2)


def vmem():
    return pl.BlockSpec(memory_space=pltpu.VMEM)


def anywhere():
    return pl.BlockSpec(memory_space=pl.ANY)


def params(mib):
    return pltpu.CompilerParams(vmem_limit_bytes=mib * MIB)


def place():
    index = lax.axis_index("tensor")
    return index // CORES, lax.rem(index, CORES)


def hop(value, by):
    length = lax.axis_size("tensor")
    return lax.ppermute(value, "tensor", [(i, i ^ by) for i in range(length)])


def rms_rows(wide, gain_ref):
    mean_sq = jnp.mean(wide * wide, axis=-1, keepdims=True)
    return (wide * lax.rsqrt(mean_sq + epsilon) * gain_ref[...]).astype(jnp.bfloat16)


def project_kernel(count, *refs):
    pieces, (gain_ref, w_own, w_other) = refs[:count], refs[count : count + 3]
    out_ref, rows_ref = refs[-2:]
    core = place()[1]
    cols = w_own.shape[1]
    at = 0
    for piece in pieces:
        span = slice(at, at + piece.shape[0])
        rows_ref[span, :] = rms_rows(piece[...].astype(jnp.float32), gain_ref)
        at += piece.shape[0]
    for which, weights in ((core, w_own), (1 - core, w_other)):
        span = pl.ds(pl.multiple_of(which * cols, cols), cols)
        out_ref[:, span] = jnp.dot(
            rows_ref[...], weights[...], preferred_element_type=jnp.float32
        ).astype(jnp.bfloat16)


def project_call(pieces, gain, w_own, w_other, *earlier):
    rows, width = sum(p.shape[0] for p in pieces), pieces[0].shape[1]
    return pl.pallas_call(
        functools.partial(project_kernel, len(pieces)),
        out_shape=jax.ShapeDtypeStruct((rows, CORES * w_own.shape[1]), jnp.bfloat16),
        in_specs=[vmem()] * (len(pieces) + 3) + [anywhere()] * len(earlier),
        out_specs=vmem(),
        scratch_shapes=[pltpu.VMEM((rows, width), jnp.bfloat16)],
        cost_estimate=LONG,
        compiler_params=params(16),
        name="project",
    )(*pieces, gain, w_own, w_other, *earlier)


def pack_kernel(own, by_x, by_y, by_xy, segs_ref, routes_ref, shares_ref, out_ref):
    chip = place()[0]
    rows, width = own.shape
    for hop_by, piece in enumerate((own, by_x, by_y, by_xy)):

        @pl.when(chip ^ hop_by == CHIPS - 1)
        def _(piece=piece):
            out_ref[:rows, :] = piece[...]

    experts = PAGE // 2
    named = lax.broadcasted_iota(jnp.int32, (experts, rows), 0)
    table = jnp.zeros((experts, rows), jnp.float32)
    for k in range(TOP):
        routed = jnp.broadcast_to(routes_ref[k : k + 1, :], (experts, rows)) == named
        table = table + jnp.where(routed, shares_ref[k : k + 1, :], 0.0)
    segs = jnp.broadcast_to(segs_ref[...].astype(jnp.float32), (experts, rows))
    out_ref[rows:, :rows] = jnp.concatenate([segs, table], axis=0).astype(jnp.bfloat16)
    for part in (1, 2):
        table = table - table.astype(jnp.bfloat16).astype(jnp.float32)
        out_ref[rows:, part * rows : (part + 1) * rows] = jnp.concatenate(
            [segs, table], axis=0
        ).astype(jnp.bfloat16)
    out_ref[rows:, 3 * rows :] = jnp.zeros((PAGE, width - 3 * rows), jnp.bfloat16)


def pack_call(pieces, segment_ids, routes, shares):
    rows, width = pieces[0].shape
    return pl.pallas_call(
        pack_kernel,
        out_shape=jax.ShapeDtypeStruct((rows + PAGE, width), jnp.bfloat16),
        in_specs=[vmem()] * (CHIPS + 3),
        out_specs=vmem(),
        compiler_params=params(16),
        name="pack_kv",
    )(*pieces, segment_ids.reshape(1, rows), routes.T, shares.T)


def choose_kernel(own, prev, *out_refs):
    chip = place()[0]
    rows = own.shape[0] - PAGE
    row_id = lax.broadcasted_iota(jnp.int32, (PAGE, own.shape[1]), 0)
    for hop_by, out_ref in enumerate(out_refs, 1):
        later = (chip ^ hop_by) > chip

        @pl.when(later)
        def _(out_ref=out_ref):
            out_ref[...] = own[...]

        @pl.when(jnp.logical_not(later))
        def _(out_ref=out_ref):
            out_ref[:rows, :] = prev[:rows, :]
            below, mine = prev[rows:, :].astype(jnp.float32), own[rows:, :].astype(jnp.float32)
            out_ref[rows:, :] = jnp.where(row_id < PAGE // 2, below, mine).astype(jnp.bfloat16)


def choose_call(own, prev):
    return pl.pallas_call(
        choose_kernel,
        out_shape=(jax.ShapeDtypeStruct(own.shape, own.dtype),) * (CHIPS - 1),
        in_specs=[vmem()] * 2,
        out_specs=(vmem(),) * (CHIPS - 1),
        compiler_params=params(16),
        name="choose_kv",
    )(own, prev)


def attend_kernel(*refs):
    projected, refs = refs[:CHIPS], refs[CHIPS:]
    windows, refs = refs[: 2 * (CHIPS + 1)], refs[2 * (CHIPS + 1) :]
    out_ref, q_ref, s_ref, top_ref, sum_ref, acc_ref = refs
    chip, core = place()
    seq = lax.axis_index("seq")
    rows = out_ref.shape[0]
    per_group = HEADS // KV_HEADS
    per_chip = HEADS // (CHIPS - 1)
    block_rows = rows * CORES * CHIPS
    own_first = seq * block_rows + (chip * CORES + core) * rows

    def segs_of(ref):
        return ref[rows : rows + 1, :rows].astype(jnp.float32)

    own_segs = segs_of(windows[0])
    query_seg = jnp.broadcast_to(own_segs, (rows, rows)).T
    query_pos = lax.broadcasted_iota(jnp.int32, (rows, rows), 0) + own_first
    lane = lax.broadcasted_iota(jnp.int32, (rows, rows), 1)
    lowest = jnp.min(own_segs)

    for hop_by, piece in enumerate(projected):
        source = chip ^ hop_by

        @pl.when(source < CHIPS - 1)
        def _(source=source, piece=piece):
            for i in range(per_chip):
                start = pl.multiple_of((source * per_chip + i) * rows, rows)
                q_ref[pl.ds(start, rows), :] = piece[:, i * HEAD : (i + 1) * HEAD]

    pairs = []
    for n in range(CHIPS + 1):
        if n == 0:
            base, source = seq, chip
        elif n == CHIPS:
            base, source = seq - 1, chip
        else:
            source = chip ^ n
            base = jnp.where(source < chip, seq, seq - 1)
        first = base * block_rows + source * CORES * rows
        refs = (windows[n], windows[n + CHIPS + 1])
        pairs.append((refs, (first + core * rows, first + (1 - core) * rows)))

    scale = math.log2(math.e) / math.sqrt(HEAD)
    group_rows = per_group * rows
    used = []
    for n, (refs, firsts) in enumerate(pairs):
        use = (firsts[0] >= 0) & (firsts[0] <= own_first)
        last_seg = jnp.max(jnp.maximum(segs_of(refs[0]), segs_of(refs[1])))
        used.append(use & (last_seg >= lowest))

        def scores_of(n=n, refs=refs, firsts=firsts):
            bias = []
            for ref, first in zip(refs, firsts):
                allowed = (segs_of(ref) == query_seg) & (first + lane <= query_pos)
                bias.append(jnp.where(allowed, 0.0, -jnp.inf))
            bias = jnp.concatenate(bias, axis=1)
            for g in range(KV_HEADS):
                span = slice(g * HEAD, (g + 1) * HEAD)
                keys = jnp.concatenate([ref[:rows, span] for ref in refs], axis=0)
                part = slice(g * group_rows, (g + 1) * group_rows)
                scores = lax.dot_general(
                    q_ref[part, :], keys, (((1,), (1,)), ((), ())),
                    preferred_element_type=jnp.float32,
                )
                scores = scores.reshape(per_group, rows, 2 * rows) * scale + bias[None]
                scores = scores.reshape(group_rows, 2 * rows)
                s_ref[n, part, :] = scores
                high = jnp.maximum(scores[:, :rows], scores[:, rows:])
                top_ref[part, :] = high if n == 0 else jnp.maximum(top_ref[part, :], high)

        if n == 0:
            scores_of()
        else:
            pl.when(used[n])(scores_of)

    top_ref[...] = jnp.broadcast_to(jnp.max(top_ref[...], axis=1, keepdims=True), top_ref.shape)
    for n, (refs, firsts) in enumerate(pairs):

        def weigh(n=n, refs=refs):
            for g in range(KV_HEADS):
                part = slice(g * group_rows, (g + 1) * group_rows)
                top = top_ref[part, :]
                weights = jnp.exp2(s_ref[n, part, :] - jnp.concatenate([top, top], axis=1))
                span = slice((KV_HEADS + g) * HEAD, (KV_HEADS + g + 1) * HEAD)
                values = jnp.concatenate([ref[:rows, span] for ref in refs], axis=0)
                made = jnp.dot(
                    weights.astype(jnp.bfloat16), values, preferred_element_type=jnp.float32
                )
                sums = weights[:, :rows] + weights[:, rows:]
                if n == 0:
                    sum_ref[part, :] = sums
                    acc_ref[part, :] = made
                else:
                    sum_ref[part, :] += sums
                    acc_ref[part, :] += made

        if n == 0:
            weigh()
        else:
            pl.when(used[n])(weigh)

    for head in range(HEADS):
        part = slice(head * rows, (head + 1) * rows)
        total = jnp.sum(sum_ref[part, :], axis=1, keepdims=True)
        out_ref[:, head * HEAD : (head + 1) * HEAD] = (acc_ref[part, :] / total).astype(
            jnp.bfloat16
        )


def attend_call(projected, windows):
    rows = projected[0].shape[0]
    wide = HEADS * rows
    return pl.pallas_call(
        attend_kernel,
        out_shape=jax.ShapeDtypeStruct((rows, HEADS * HEAD), jnp.bfloat16),
        in_specs=[vmem()] * (len(projected) + len(windows)),
        out_specs=vmem(),
        scratch_shapes=[
            pltpu.VMEM((wide, HEAD), jnp.bfloat16),
            pltpu.VMEM((CHIPS + 1, wide, 2 * rows), jnp.float32),
            pltpu.VMEM((wide, rows), jnp.float32),
            pltpu.VMEM((wide, rows), jnp.float32),
            pltpu.VMEM((wide, HEAD), jnp.float32),
        ],
        compiler_params=params(32),
        name="attend",
    )(*projected, *windows)


def assemble_kernel(same, other, out_ref):
    chip, core = place()
    cols = same[0].shape[0]
    for pieces, which in ((same, core), (other, 1 - core)):
        done = 0
        for piece in pieces:
            count = piece.shape[0]
            start = ((chip ^ (done // cols)) * CORES + which) * cols + done % cols
            out_ref[pl.ds(pl.multiple_of(start, PAGE), count), :] = piece[...]
            done += count


def assemble_call(same, other):
    shape = (CORES * CHIPS * same[0].shape[0], same[0].shape[1])
    count = len(same)
    return pl.pallas_call(
        lambda *refs: assemble_kernel(refs[:count], refs[count:-1], refs[-1]),
        out_shape=jax.ShapeDtypeStruct(shape, jnp.bfloat16),
        in_specs=[vmem()] * (2 * count),
        out_specs=vmem(),
        compiler_params=params(16),
        name="assemble_w_out",
    )(*same, *other)


def expert_kernel(tile, pieces, count, *refs):
    tables, (w_ref, gain_ref), held = refs[:2], refs[2:4], refs[4:10]
    context, tokens = refs[10 : 10 + pieces], refs[10 + pieces : 10 + pieces + count]
    outs, (rows_ref, hidden_ref, total_ref) = refs[-5:-3], refs[-3:]
    chip, core = place()
    rows, width = outs[0].shape
    hidden = hidden_ref.shape[1]
    spans = [slice(i * rows, (i + 1) * rows) for i in range(2)]
    at = 0
    for piece in context:
        rows_ref[at : at + piece.shape[0], :] = piece[...]
        at += piece.shape[0]
    added = lax.dot_general(
        rows_ref[...], w_ref[...], (((1,), (1,)), ((), ())), preferred_element_type=jnp.float32
    )
    at = 0
    for piece in tokens:
        span = slice(at, at + piece.shape[0])
        at += piece.shape[0]
        residual = (piece[...].astype(jnp.float32) + added[span]).astype(jnp.bfloat16)
        wide = residual.astype(jnp.float32)
        if outs[0].dtype == jnp.float32 and span.start == 0:
            total_ref[span, :] = wide
        else:
            total_ref[span, :] = jnp.zeros_like(wide)
        rows_ref[span, :] = rms_rows(wide, gain_ref)

    for which in range(CORES):
        expert = chip * CORES + (core if which == 0 else 1 - core)
        gate, up, down = held[3 * which : 3 * which + 3]
        shares = []
        for table in tables:
            below = table[rows:, :].astype(jnp.float32)
            row_id = lax.broadcasted_iota(jnp.int32, below.shape, 0)
            row = jnp.sum(
                jnp.where(row_id == PAGE // 2 + expert, below, 0.0), axis=0, keepdims=True
            )
            row = row[:, :rows] + row[:, rows : 2 * rows] + row[:, 2 * rows : 3 * rows]
            shares.append(jnp.broadcast_to(row, (rows, rows)).T[:, :1])
        for column in range(0, hidden, tile):
            span = slice(column, column + tile)
            gate_out = jnp.dot(rows_ref[...], gate[:, span], preferred_element_type=jnp.float32)
            up_out = jnp.dot(rows_ref[...], up[:, span], preferred_element_type=jnp.float32)
            hidden_ref[:, span] = (jnp.maximum(gate_out, 0.0) * up_out).astype(jnp.bfloat16)
        for column in range(0, width, 2 * tile):
            cols = slice(column, column + 2 * tile)
            made = jnp.dot(hidden_ref[...], down[:, cols], preferred_element_type=jnp.float32)
            made = made.astype(jnp.bfloat16).astype(jnp.float32)
            for span, share, out_ref in zip(spans, shares, outs):
                total = total_ref[span, cols] + share * made[span]
                if which == 0:
                    total_ref[span, cols] = total
                else:
                    out_ref[:, cols] = total.astype(out_ref.dtype)


def expert_call(context, tokens, tables, w_all, gain, weights, kinds, *earlier):
    rows, width = tokens[0].shape
    hidden = weights[0].shape[1]
    return pl.pallas_call(
        functools.partial(expert_kernel, 256, len(context), len(tokens)),
        out_shape=tuple(jax.ShapeDtypeStruct((rows, width), kind) for kind in kinds),
        in_specs=[vmem()] * (10 + len(context) + len(tokens)) + [anywhere()] * len(earlier),
        out_specs=(vmem(), vmem()),
        scratch_shapes=[
            pltpu.VMEM((2 * rows, width), jnp.bfloat16),
            pltpu.VMEM((2 * rows, hidden), jnp.bfloat16),
            pltpu.VMEM((2 * rows, width), jnp.float32),
        ],
        cost_estimate=LONG,
        compiler_params=params(32),
        name="experts",
    )(*tables, w_all, gain, *weights, *context, *tokens, *earlier)


def mix_kernel(own, by_x, by_y, by_xy, out_ref):
    total = by_x[...].astype(jnp.float32) + by_y[...].astype(jnp.float32)
    total = total + by_xy[...].astype(jnp.float32)
    out_ref[...] = (own[...] + total).astype(jnp.bfloat16)


def mix_call(pieces):
    return pl.pallas_call(
        mix_kernel,
        out_shape=jax.ShapeDtypeStruct(pieces[0].shape, jnp.bfloat16),
        in_specs=[vmem()] * CHIPS,
        out_specs=vmem(),
        compiler_params=params(16),
        name="mix",
    )(*pieces)


def cache_kernel(table_ref, *refs):
    same, other, (out_ref, held) = refs[:2], refs[2:4], refs[4:]
    core = place()[1]
    page_rows = held.shape[1]
    pages = page_rows // PAGE
    for i, hop_by in enumerate(ORDER):
        source = (CHIPS - 1 ^ hop_by) * CORES
        span = slice(i % 2 * page_rows, (i % 2 + 1) * page_rows)
        held[source + core] = same[i // 2][span, :]
        held[source + 1 - core] = other[i // 2][span, :]

    def one(logical, carry):
        slot = table_ref[0, logical]
        to = slot // pages

        @pl.when(lax.rem(to, CORES) == core)
        def _():
            from_row = pl.multiple_of(lax.rem(logical, pages) * PAGE, PAGE)
            to_row = pl.multiple_of(lax.rem(slot, pages) * PAGE, PAGE)
            out_ref[to // CORES, pl.ds(to_row, PAGE), :] = held[
                logical // pages, pl.ds(from_row, PAGE), :
            ]

        return carry

    lax.fori_loop(0, table_ref.shape[1], one, 0, unroll=8)


def cache_call(page_table, same, other):
    rows, width = same[0].shape[0] // 2, same[0].shape[1]
    return pl.pallas_call(
        cache_kernel,
        out_shape=jax.ShapeDtypeStruct((CHIPS, rows, width), jnp.bfloat16),
        in_specs=[pl.BlockSpec(memory_space=pltpu.SMEM)] + [vmem()] * 4,
        out_specs=vmem(),
        scratch_shapes=[pltpu.VMEM((CORES * CHIPS, rows, width), jnp.bfloat16)],
        compiler_params=params(16),
        name="cache_pages",
    )(page_table, *same, *other)


def join_kernel(*refs):
    pieces, out_ref = refs[:CHIPS], refs[CHIPS]
    for hop_by, piece in enumerate(pieces):

        @pl.when(place()[0] ^ hop_by == CHIPS - 1)
        def _(piece=piece):
            out_ref[...] = piece[...]


def join_call(pieces):
    return pl.pallas_call(
        join_kernel,
        out_shape=jax.ShapeDtypeStruct(pieces[0].shape, pieces[0].dtype),
        in_specs=[vmem()] * CHIPS,
        out_specs=vmem(),
        compiler_params=params(16),
        name="join_pages",
    )(*pieces)


def hold_kernel(in_ref, *refs):
    refs[-1][...] = in_ref[...]


def hold_call(value, *earlier):
    return pl.pallas_call(
        hold_kernel,
        out_shape=jax.ShapeDtypeStruct(value.shape, value.dtype),
        in_specs=[vmem()] + [anywhere()] * len(earlier),
        out_specs=vmem(),
        cost_estimate=LONG,
        compiler_params=params(16),
        name="hold",
    )(value, *earlier)


def after(value, other):
    return lax.optimization_barrier((value, other))[0]


def chip_body(
    tokens, segment_ids, page_table, attn_gain, w_qkv, w_out, moe_gain,
    route_ids, route_weight, w_gate, w_up, w_down,
):
    rows = tokens.shape[0]
    seq_size = lax.axis_size("seq")

    def chips(value, by):
        return hop(value, CORES * by)

    gate, up, down = w_gate[0], w_up[0], w_down[0]
    w_own = w_out.T

    tokens_x, tokens_y = chips(tokens, 1), chips(tokens, 2)
    w_qkv_other, gate_other = hop(w_qkv, 1), hop(gate, 1)
    tokens_xy = [chips(tokens_y[: rows // 2], 1), chips(tokens_x[rows // 2 :], 2)]
    late = project_call((tokens_x, tokens_y), attn_gain, w_qkv, w_qkv_other)
    made = project_call((tokens, *tokens_xy), attn_gain, w_qkv, w_qkv_other, late)
    projected = [
        made[:rows],
        hold_call(chips(late[:rows], 1)),
        hold_call(chips(late[rows:], 2)),
        chips(made[rows:], 3),
    ]
    up_other = hop(after(up, tokens_x), 1)

    own_kv = pack_call(
        after(projected, (gate_other, up_other)), segment_ids, route_ids, route_weight
    )
    prev_kv = lax.ppermute(own_kv, "seq", [(i, i + 1) for i in range(seq_size - 1)])
    w_going, down_going = after((w_own, down), own_kv)
    mine = after((made, late), own_kv)
    paged = cache_call(page_table, mine, [hop(kv, 1) for kv in mine])
    w_x, w_y = chips(w_going, 1), chips(w_going, 2)
    down_other, w_own_other = hop(down_going, 1), hop(w_going, 1)

    sent = choose_call(own_kv, after(prev_kv, (w_x, w_y, down_other, w_own_other)))
    kv_xy, kv_x, kv_y = chips(sent[2], 3), chips(sent[0], 1), chips(sent[1], 2)
    kv_xy = hold_call(kv_xy)
    half = w_own.shape[0] // 2
    w_relayed = [hold_call(w_y[:half], *sent), hold_call(w_x[half:], *sent)]
    w_diagonal = [chips(w_relayed[0], 1), chips(w_relayed[1], 2)]
    windows = [own_kv, kv_x, kv_y, kv_xy, prev_kv]
    windows_other = [hop(w, 1) for w in windows]
    w_other = [w_own_other] + [hop(after(w, sent), 1) for w in (w_x, w_y)]
    windows_other = after(windows_other, (w_other, w_relayed))
    context = after(attend_call(projected, windows + windows_other), w_diagonal)
    context_x, context_y = chips(context, 1), chips(context, 2)
    context_xy = [chips(context_y[: rows // 2], 1), chips(context_x[rows // 2 :], 2)]
    last = CHIPS - 1
    paged = after(paged, (context_x, context_y))
    pages = [paged[last]]
    for by in (1, 2, 3):
        pairs = [(last * CORES + k, (last ^ by) * CORES + k) for k in range(CORES)]
        pages.append(lax.ppermute(paged[last ^ by], "tensor", pairs))
    w_other += [hop(w, 1) for w in w_diagonal]
    w_all = assemble_call([w_own, w_x, w_y] + w_diagonal, w_other)

    weights = [gate, up, down, gate_other, up_other, down_other]
    out_x, out_y = expert_call(
        (context_x, context_y), (tokens_x, tokens_y), (kv_x, kv_y), w_all, moe_gain, weights,
        (jnp.bfloat16, jnp.bfloat16),
    )
    back_x, back_y = hold_call(chips(out_x, 1)), hold_call(chips(out_y, 2))
    out, out_xy = expert_call(
        (context, *context_xy), (tokens, *tokens_xy), (own_kv, kv_xy), w_all, moe_gain, weights,
        (jnp.float32, jnp.bfloat16), out_x, *pages[1:],
    )
    back_xy = chips(out_xy, 3)
    pages = join_call(after(pages, out_xy))
    mixed = mix_call((out, back_x, back_y, back_xy))
    return (mixed, pages.reshape(rows // PAGE, PAGE, pages.shape[1]))


def from_behind(value, axis, by):
    length = lax.axis_size(axis)
    pairs = [(i, i + by) for i in range(length) if 0 <= i + by < length]
    return lax.ppermute(value, axis, pairs)


def rms_scaled(values, scales):
    wide = values.astype(jnp.float32)
    mean_sq = jnp.mean(wide * wide, axis=-1, keepdims=True)
    return (wide * lax.rsqrt(mean_sq + epsilon) * scales).astype(jnp.bfloat16)


def attend(queries, keys_window, values_window, allowed):
    scores = jnp.einsum(
        "qhd,kd->hqk", queries, keys_window, preferred_element_type=jnp.float32
    ) / math.sqrt(queries.shape[-1])
    scores = jnp.where(allowed[None], scores, -jnp.inf)
    highest = jnp.max(scores, axis=-1, keepdims=True)
    weights = jnp.exp(scores - highest)
    totals = jnp.sum(weights, axis=-1, keepdims=True)
    shares = (weights / totals).astype(jnp.bfloat16)
    return jnp.einsum("hqk,kd->qhd", shares, values_window, preferred_element_type=jnp.float32)


def block_body(
    tokens,
    segment_ids,
    page_table,
    attn_gain,
    w_qkv,
    w_out,
    moe_gain,
    route_ids,
    route_weight,
    w_gate,
    w_up,
    w_down,
):
    tok_rows = tokens.shape[0]
    tensor_size = lax.axis_size("tensor")
    tensor_index = lax.axis_index("tensor")
    seq_index = lax.axis_index("seq")
    block_rows = tok_rows * tensor_size
    normed = rms_scaled(tokens, attn_gain)
    block_normed = lax.all_gather(normed, "tensor", axis=0, tiled=True)
    own_columns = jnp.dot(block_normed, w_qkv, preferred_element_type=jnp.float32).astype(
        jnp.bfloat16
    )
    projected = lax.all_to_all(own_columns, "tensor", split_axis=0, concat_axis=1, tiled=True)
    query_width = HEADS * HEAD
    queries = projected[:, :query_width].reshape(tok_rows, HEADS, HEAD)
    own_kv = projected[:, query_width:]
    block_kv, block_segs = (
        lax.all_gather(own_kv, "tensor", axis=0, tiled=True),
        lax.all_gather(segment_ids, "tensor", axis=0, tiled=True),
    )
    earlier_kv, earlier_seg_block = from_behind((block_kv, block_segs), "seq", 1)
    pages_here = tok_rows // PAGE
    pages_block = block_rows // PAGE
    slot_ids = tensor_index * pages_here + jnp.arange(pages_here, dtype=jnp.int32)
    matches = page_table[0][None, :] == slot_ids[:, None]
    logical = jnp.sum(
        jnp.where(matches, jnp.arange(pages_block, dtype=jnp.int32)[None, :], 0), axis=1
    )
    cache_pages = block_kv.reshape(pages_block, PAGE, block_kv.shape[1])[logical]
    all_kv = jnp.concatenate([earlier_kv, block_kv], axis=0)
    all_segs = jnp.concatenate([earlier_seg_block, block_segs], axis=0)
    window = block_rows + tok_rows
    first_key = tensor_index * tok_rows
    keys_window = lax.dynamic_slice_in_dim(all_kv, first_key, window, 0)
    segs_window = lax.dynamic_slice_in_dim(all_segs, first_key, window, 0)
    key_pos = (seq_index - 1) * block_rows + first_key + jnp.arange(window, dtype=jnp.int32)
    query_pos = seq_index * block_rows + first_key + jnp.arange(tok_rows, dtype=jnp.int32)
    allowed = (
        (segs_window[None, :] == segment_ids[:, None])
        & (key_pos[None, :] <= query_pos[:, None])
        & (key_pos[None, :] >= 0)
    )
    per_group = HEADS // KV_HEADS
    contexts = []
    for kv_group in range(KV_HEADS):
        key_cols = keys_window[:, kv_group * HEAD : (kv_group + 1) * HEAD]
        value_cols = keys_window[:, (KV_HEADS + kv_group) * HEAD : (KV_HEADS + kv_group + 1) * HEAD]
        contexts.append(
            attend(
                queries[:, kv_group * per_group : (kv_group + 1) * per_group],
                key_cols,
                value_cols,
                allowed,
            )
        )
    context = jnp.concatenate(contexts, axis=1).reshape(tok_rows, query_width).astype(jnp.bfloat16)
    attn_out = jnp.dot(
        context,
        lax.all_gather(w_out, "tensor", axis=1, tiled=True),
        preferred_element_type=jnp.float32,
    )
    residual = (tokens.astype(jnp.float32) + attn_out).astype(jnp.bfloat16)
    expert_input = rms_scaled(residual, moe_gain)
    experts_all = w_gate.shape[0] * tensor_size
    capacity = max(2, 3 * tok_rows * TOP // (2 * experts_all))
    flat_routes = route_ids.reshape(-1)
    expert_hits = (
        flat_routes[:, None] == jnp.arange(experts_all, dtype=jnp.int32)[None, :]
    ).astype(jnp.int32)
    earlier_hits = jnp.cumsum(expert_hits, axis=0) - expert_hits
    slot_rank = jnp.sum(earlier_hits * expert_hits, axis=1)
    dest_slot = flat_routes * capacity + slot_rank
    slot_table = (
        jnp.arange(experts_all * capacity, dtype=jnp.int32)[:, None, None]
        == dest_slot.reshape(tok_rows, TOP)[None]
    )
    dispatch = jnp.any(slot_table, axis=2).astype(jnp.bfloat16)
    outgoing = jnp.dot(dispatch, expert_input, preferred_element_type=jnp.float32).astype(
        jnp.bfloat16
    )
    outgoing = outgoing.reshape(experts_all, capacity, expert_input.shape[1])
    arrived = lax.all_to_all(outgoing, "tensor", split_axis=0, concat_axis=0, tiled=True)
    rows_flat = arrived.reshape(-1, arrived.shape[-1])
    gate_out = jnp.dot(rows_flat, w_gate[0], preferred_element_type=jnp.float32)
    up_out = jnp.dot(rows_flat, w_up[0], preferred_element_type=jnp.float32)
    hidden = (jnp.maximum(gate_out, 0.0) * up_out).astype(jnp.bfloat16)
    produced = jnp.dot(hidden, w_down[0], preferred_element_type=jnp.float32).astype(jnp.bfloat16)
    returned = lax.all_to_all(
        produced.reshape(arrived.shape), "tensor", split_axis=0, concat_axis=0, tiled=True
    )
    picked = returned.reshape(-1, returned.shape[-1])[dest_slot].reshape(
        tok_rows, TOP, returned.shape[-1]
    )
    routed_sum = jnp.einsum("tk,tkd->td", route_weight, picked.astype(jnp.float32))
    mixed = (residual.astype(jnp.float32) + routed_sum).astype(jnp.bfloat16)
    return (mixed, cache_pages)


def by_chips(mesh):
    size = mesh.shape["tensor"]
    return size == CORES * CHIPS and (HEADS + 2 * KV_HEADS) % size == 0


def solution(mesh):
    return jax.shard_map(
        chip_body if by_chips(mesh) else block_body,
        mesh=mesh,
        in_specs=(
            P(("seq", "tensor"), None),
            P(("seq", "tensor")),
            P("seq", None),
            P(),
            P(None, "tensor"),
            P(None, "tensor"),
            P(),
            P(("seq", "tensor"), None),
            P(("seq", "tensor"), None),
            P("tensor", None, None),
            P("tensor", None, None),
            P("tensor", None, None),
        ),
        out_specs=(P(("seq", "tensor"), None), P(("seq", "tensor"), None, None)),
        check_vma=False,
    )
```

```python
import functools
import math

import jax
import jax.numpy as jnp
from jax import lax
from jax.experimental import pallas as pl
from jax.experimental.pallas import tpu as pltpu
from jax.sharding import PartitionSpec as P

HEADS = 12
KV_HEADS = 2
HEAD = 128
TOP = 4
PAGE = 16
CORES = 2
CHIPS = 4


epsilon = 1e-06
MIB = 1024 * 1024


LONG = pl.CostEstimate(flops=20 * 10**9, bytes_accessed=1, transcendentals=0)


ORDER = (0, 3, 1, 2)


def vmem():
    return pl.BlockSpec(memory_space=pltpu.VMEM)


def anywhere():
    return pl.BlockSpec(memory_space=pl.ANY)


def params(mib):
    return pltpu.CompilerParams(vmem_limit_bytes=mib * MIB)


def place():
    index = lax.axis_index("tensor")
    return index // CORES, lax.rem(index, CORES)


def hop(value, by):
    length = lax.axis_size("tensor")
    return lax.ppermute(value, "tensor", [(i, i ^ by) for i in range(length)])


def rms_rows(wide, gain_ref):
    mean_sq = jnp.mean(wide * wide, axis=-1, keepdims=True)
    return (wide * lax.rsqrt(mean_sq + epsilon) * gain_ref[...]).astype(jnp.bfloat16)


def project_kernel(count, *refs):
    pieces, (gain_ref, w_own, w_other) = refs[:count], refs[count : count + 3]
    out_ref, rows_ref = refs[-2:]
    core = place()[1]
    cols = w_own.shape[1]
    at = 0
    for piece in pieces:
        span = slice(at, at + piece.shape[0])
        rows_ref[span, :] = rms_rows(piece[...].astype(jnp.float32), gain_ref)
        at += piece.shape[0]
    for which, weights in ((core, w_own), (1 - core, w_other)):
        span = pl.ds(pl.multiple_of(which * cols, cols), cols)
        out_ref[:, span] = jnp.dot(
            rows_ref[...], weights[...], preferred_element_type=jnp.float32
        ).astype(jnp.bfloat16)


def project_call(pieces, gain, w_own, w_other, *earlier):
    rows, width = sum(p.shape[0] for p in pieces), pieces[0].shape[1]
    return pl.pallas_call(
        functools.partial(project_kernel, len(pieces)),
        out_shape=jax.ShapeDtypeStruct((rows, CORES * w_own.shape[1]), jnp.bfloat16),
        in_specs=[vmem()] * (len(pieces) + 3) + [anywhere()] * len(earlier),
        out_specs=vmem(),
        scratch_shapes=[pltpu.VMEM((rows, width), jnp.bfloat16)],
        cost_estimate=LONG,
        compiler_params=params(16),
        name="project",
    )(*pieces, gain, w_own, w_other, *earlier)


def pack_kernel(own, by_x, by_y, by_xy, segs_ref, routes_ref, shares_ref, out_ref):
    chip = place()[0]
    rows, width = own.shape
    for hop_by, piece in enumerate((own, by_x, by_y, by_xy)):

        @pl.when(chip ^ hop_by == CHIPS - 1)
        def _(piece=piece):
            out_ref[:rows, :] = piece[...]

    experts = PAGE // 2
    named = lax.broadcasted_iota(jnp.int32, (experts, rows), 0)
    table = jnp.zeros((experts, rows), jnp.float32)
    for k in range(TOP):
        routed = jnp.broadcast_to(routes_ref[k : k + 1, :], (experts, rows)) == named
        table = table + jnp.where(routed, shares_ref[k : k + 1, :], 0.0)
    segs = jnp.broadcast_to(segs_ref[...].astype(jnp.float32), (experts, rows))
    out_ref[rows:, :rows] = jnp.concatenate([segs, table], axis=0).astype(jnp.bfloat16)
    for part in (1, 2):
        table = table - table.astype(jnp.bfloat16).astype(jnp.float32)
        out_ref[rows:, part * rows : (part + 1) * rows] = jnp.concatenate(
            [segs, table], axis=0
        ).astype(jnp.bfloat16)
    out_ref[rows:, 3 * rows :] = jnp.zeros((PAGE, width - 3 * rows), jnp.bfloat16)


def pack_call(pieces, segment_ids, routes, shares):
    rows, width = pieces[0].shape
    return pl.pallas_call(
        pack_kernel,
        out_shape=jax.ShapeDtypeStruct((rows + PAGE, width), jnp.bfloat16),
        in_specs=[vmem()] * (CHIPS + 3),
        out_specs=vmem(),
        compiler_params=params(16),
        name="pack_kv",
    )(*pieces, segment_ids.reshape(1, rows), routes.T, shares.T)


def choose_kernel(own, prev, *out_refs):
    chip = place()[0]
    rows = own.shape[0] - PAGE
    row_id = lax.broadcasted_iota(jnp.int32, (PAGE, own.shape[1]), 0)
    for hop_by, out_ref in enumerate(out_refs, 1):
        later = (chip ^ hop_by) > chip

        @pl.when(later)
        def _(out_ref=out_ref):
            out_ref[...] = own[...]

        @pl.when(jnp.logical_not(later))
        def _(out_ref=out_ref):
            out_ref[:rows, :] = prev[:rows, :]
            below, mine = prev[rows:, :].astype(jnp.float32), own[rows:, :].astype(jnp.float32)
            out_ref[rows:, :] = jnp.where(row_id < PAGE // 2, below, mine).astype(jnp.bfloat16)


def choose_call(own, prev):
    return pl.pallas_call(
        choose_kernel,
        out_shape=(jax.ShapeDtypeStruct(own.shape, own.dtype),) * (CHIPS - 1),
        in_specs=[vmem()] * 2,
        out_specs=(vmem(),) * (CHIPS - 1),
        compiler_params=params(16),
        name="choose_kv",
    )(own, prev)


def attend_kernel(*refs):
    projected, refs = refs[:CHIPS], refs[CHIPS:]
    windows, refs = refs[: 2 * (CHIPS + 1)], refs[2 * (CHIPS + 1) :]
    out_ref, q_ref, s_ref, top_ref, sum_ref, acc_ref = refs
    chip, core = place()
    seq = lax.axis_index("seq")
    rows = out_ref.shape[0]
    per_group = HEADS // KV_HEADS
    per_chip = HEADS // (CHIPS - 1)
    block_rows = rows * CORES * CHIPS
    own_first = seq * block_rows + (chip * CORES + core) * rows

    def segs_of(ref):
        return ref[rows : rows + 1, :rows].astype(jnp.float32)

    own_segs = segs_of(windows[0])
    query_seg = jnp.broadcast_to(own_segs, (rows, rows)).T
    query_pos = lax.broadcasted_iota(jnp.int32, (rows, rows), 0) + own_first
    lane = lax.broadcasted_iota(jnp.int32, (rows, rows), 1)
    lowest = jnp.min(own_segs)

    for hop_by, piece in enumerate(projected):
        source = chip ^ hop_by

        @pl.when(source < CHIPS - 1)
        def _(source=source, piece=piece):
            for i in range(per_chip):
                start = pl.multiple_of((source * per_chip + i) * rows, rows)
                q_ref[pl.ds(start, rows), :] = piece[:, i * HEAD : (i + 1) * HEAD]

    pairs = []
    for n in range(CHIPS + 1):
        if n == 0:
            base, source = seq, chip
        elif n == CHIPS:
            base, source = seq - 1, chip
        else:
            source = chip ^ n
            base = jnp.where(source < chip, seq, seq - 1)
        first = base * block_rows + source * CORES * rows
        refs = (windows[n], windows[n + CHIPS + 1])
        pairs.append((refs, (first + core * rows, first + (1 - core) * rows)))

    scale = math.log2(math.e) / math.sqrt(HEAD)
    group_rows = per_group * rows
    used = []
    for n, (refs, firsts) in enumerate(pairs):
        use = (firsts[0] >= 0) & (firsts[0] <= own_first)
        last_seg = jnp.max(jnp.maximum(segs_of(refs[0]), segs_of(refs[1])))
        used.append(use & (last_seg >= lowest))

        def scores_of(n=n, refs=refs, firsts=firsts):
            bias = []
            for ref, first in zip(refs, firsts):
                allowed = (segs_of(ref) == query_seg) & (first + lane <= query_pos)
                bias.append(jnp.where(allowed, 0.0, -jnp.inf))
            bias = jnp.concatenate(bias, axis=1)
            for g in range(KV_HEADS):
                span = slice(g * HEAD, (g + 1) * HEAD)
                keys = jnp.concatenate([ref[:rows, span] for ref in refs], axis=0)
                part = slice(g * group_rows, (g + 1) * group_rows)
                scores = lax.dot_general(
                    q_ref[part, :], keys, (((1,), (1,)), ((), ())),
                    preferred_element_type=jnp.float32,
                )
                scores = scores.reshape(per_group, rows, 2 * rows) * scale + bias[None]
                scores = scores.reshape(group_rows, 2 * rows)
                s_ref[n, part, :] = scores
                high = jnp.maximum(scores[:, :rows], scores[:, rows:])
                top_ref[part, :] = high if n == 0 else jnp.maximum(top_ref[part, :], high)

        if n == 0:
            scores_of()
        else:
            pl.when(used[n])(scores_of)

    top_ref[...] = jnp.broadcast_to(jnp.max(top_ref[...], axis=1, keepdims=True), top_ref.shape)
    for n, (refs, firsts) in enumerate(pairs):

        def weigh(n=n, refs=refs):
            for g in range(KV_HEADS):
                part = slice(g * group_rows, (g + 1) * group_rows)
                top = top_ref[part, :]
                weights = jnp.exp2(s_ref[n, part, :] - jnp.concatenate([top, top], axis=1))
                span = slice((KV_HEADS + g) * HEAD, (KV_HEADS + g + 1) * HEAD)
                values = jnp.concatenate([ref[:rows, span] for ref in refs], axis=0)
                made = jnp.dot(
                    weights.astype(jnp.bfloat16), values, preferred_element_type=jnp.float32
                )
                sums = weights[:, :rows] + weights[:, rows:]
                if n == 0:
                    sum_ref[part, :] = sums
                    acc_ref[part, :] = made
                else:
                    sum_ref[part, :] += sums
                    acc_ref[part, :] += made

        if n == 0:
            weigh()
        else:
            pl.when(used[n])(weigh)

    for head in range(HEADS):
        part = slice(head * rows, (head + 1) * rows)
        total = jnp.sum(sum_ref[part, :], axis=1, keepdims=True)
        out_ref[:, head * HEAD : (head + 1) * HEAD] = (acc_ref[part, :] / total).astype(
            jnp.bfloat16
        )


def attend_call(projected, windows):
    rows = projected[0].shape[0]
    wide = HEADS * rows
    return pl.pallas_call(
        attend_kernel,
        out_shape=jax.ShapeDtypeStruct((rows, HEADS * HEAD), jnp.bfloat16),
        in_specs=[vmem()] * (len(projected) + len(windows)),
        out_specs=vmem(),
        scratch_shapes=[
            pltpu.VMEM((wide, HEAD), jnp.bfloat16),
            pltpu.VMEM((CHIPS + 1, wide, 2 * rows), jnp.float32),
            pltpu.VMEM((wide, rows), jnp.float32),
            pltpu.VMEM((wide, rows), jnp.float32),
            pltpu.VMEM((wide, HEAD), jnp.float32),
        ],
        compiler_params=params(32),
        name="attend",
    )(*projected, *windows)


def assemble_kernel(same, other, out_ref):
    chip, core = place()
    cols = same[0].shape[0]
    for pieces, which in ((same, core), (other, 1 - core)):
        done = 0
        for piece in pieces:
            count = piece.shape[0]
            start = ((chip ^ (done // cols)) * CORES + which) * cols + done % cols
            out_ref[pl.ds(pl.multiple_of(start, PAGE), count), :] = piece[...]
            done += count


def assemble_call(same, other):
    shape = (CORES * CHIPS * same[0].shape[0], same[0].shape[1])
    count = len(same)
    return pl.pallas_call(
        lambda *refs: assemble_kernel(refs[:count], refs[count:-1], refs[-1]),
        out_shape=jax.ShapeDtypeStruct(shape, jnp.bfloat16),
        in_specs=[vmem()] * (2 * count),
        out_specs=vmem(),
        compiler_params=params(16),
        name="assemble_w_out",
    )(*same, *other)


def expert_kernel(tile, pieces, count, *refs):
    tables, (w_ref, gain_ref), held = refs[:2], refs[2:4], refs[4:10]
    context, tokens = refs[10 : 10 + pieces], refs[10 + pieces : 10 + pieces + count]
    outs, (rows_ref, hidden_ref, total_ref) = refs[-5:-3], refs[-3:]
    chip, core = place()
    rows, width = outs[0].shape
    hidden = hidden_ref.shape[1]
    spans = [slice(i * rows, (i + 1) * rows) for i in range(2)]
    at = 0
    for piece in context:
        rows_ref[at : at + piece.shape[0], :] = piece[...]
        at += piece.shape[0]
    added = lax.dot_general(
        rows_ref[...], w_ref[...], (((1,), (1,)), ((), ())), preferred_element_type=jnp.float32
    )
    at = 0
    for piece in tokens:
        span = slice(at, at + piece.shape[0])
        at += piece.shape[0]
        residual = (piece[...].astype(jnp.float32) + added[span]).astype(jnp.bfloat16)
        wide = residual.astype(jnp.float32)
        if outs[0].dtype == jnp.float32 and span.start == 0:
            total_ref[span, :] = wide
        else:
            total_ref[span, :] = jnp.zeros_like(wide)
        rows_ref[span, :] = rms_rows(wide, gain_ref)

    for which in range(CORES):
        expert = chip * CORES + (core if which == 0 else 1 - core)
        gate, up, down = held[3 * which : 3 * which + 3]
        shares = []
        for table in tables:
            below = table[rows:, :].astype(jnp.float32)
            row_id = lax.broadcasted_iota(jnp.int32, below.shape, 0)
            row = jnp.sum(
                jnp.where(row_id == PAGE // 2 + expert, below, 0.0), axis=0, keepdims=True
            )
            row = row[:, :rows] + row[:, rows : 2 * rows] + row[:, 2 * rows : 3 * rows]
            shares.append(jnp.broadcast_to(row, (rows, rows)).T[:, :1])
        for column in range(0, hidden, tile):
            span = slice(column, column + tile)
            gate_out = jnp.dot(rows_ref[...], gate[:, span], preferred_element_type=jnp.float32)
            up_out = jnp.dot(rows_ref[...], up[:, span], preferred_element_type=jnp.float32)
            hidden_ref[:, span] = (jnp.maximum(gate_out, 0.0) * up_out).astype(jnp.bfloat16)
        for column in range(0, width, 2 * tile):
            cols = slice(column, column + 2 * tile)
            made = jnp.dot(hidden_ref[...], down[:, cols], preferred_element_type=jnp.float32)
            made = made.astype(jnp.bfloat16).astype(jnp.float32)
            for span, share, out_ref in zip(spans, shares, outs):
                total = total_ref[span, cols] + share * made[span]
                if which == 0:
                    total_ref[span, cols] = total
                else:
                    out_ref[:, cols] = total.astype(out_ref.dtype)


def expert_call(context, tokens, tables, w_all, gain, weights, kinds, *earlier):
    rows, width = tokens[0].shape
    hidden = weights[0].shape[1]
    return pl.pallas_call(
        functools.partial(expert_kernel, 256, len(context), len(tokens)),
        out_shape=tuple(jax.ShapeDtypeStruct((rows, width), kind) for kind in kinds),
        in_specs=[vmem()] * (10 + len(context) + len(tokens)) + [anywhere()] * len(earlier),
        out_specs=(vmem(), vmem()),
        scratch_shapes=[
            pltpu.VMEM((2 * rows, width), jnp.bfloat16),
            pltpu.VMEM((2 * rows, hidden), jnp.bfloat16),
            pltpu.VMEM((2 * rows, width), jnp.float32),
        ],
        cost_estimate=LONG,
        compiler_params=params(32),
        name="experts",
    )(*tables, w_all, gain, *weights, *context, *tokens, *earlier)


def mix_kernel(own, by_x, by_y, by_xy, out_ref):
    total = by_x[...].astype(jnp.float32) + by_y[...].astype(jnp.float32)
    total = total + by_xy[...].astype(jnp.float32)
    out_ref[...] = (own[...] + total).astype(jnp.bfloat16)


def mix_call(pieces):
    return pl.pallas_call(
        mix_kernel,
        out_shape=jax.ShapeDtypeStruct(pieces[0].shape, jnp.bfloat16),
        in_specs=[vmem()] * CHIPS,
        out_specs=vmem(),
        compiler_params=params(16),
        name="mix",
    )(*pieces)


def cache_kernel(table_ref, *refs):
    same, other, (out_ref, held) = refs[:2], refs[2:4], refs[4:]
    core = place()[1]
    page_rows = held.shape[1]
    pages = page_rows // PAGE
    for i, hop_by in enumerate(ORDER):
        source = (CHIPS - 1 ^ hop_by) * CORES
        span = slice(i % 2 * page_rows, (i % 2 + 1) * page_rows)
        held[source + core] = same[i // 2][span, :]
        held[source + 1 - core] = other[i // 2][span, :]

    def one(logical, carry):
        slot = table_ref[0, logical]
        to = slot // pages

        @pl.when(lax.rem(to, CORES) == core)
        def _():
            from_row = pl.multiple_of(lax.rem(logical, pages) * PAGE, PAGE)
            to_row = pl.multiple_of(lax.rem(slot, pages) * PAGE, PAGE)
            out_ref[to // CORES, pl.ds(to_row, PAGE), :] = held[
                logical // pages, pl.ds(from_row, PAGE), :
            ]

        return carry

    lax.fori_loop(0, table_ref.shape[1], one, 0, unroll=8)


def cache_call(page_table, same, other):
    rows, width = same[0].shape[0] // 2, same[0].shape[1]
    return pl.pallas_call(
        cache_kernel,
        out_shape=jax.ShapeDtypeStruct((CHIPS, rows, width), jnp.bfloat16),
        in_specs=[pl.BlockSpec(memory_space=pltpu.SMEM)] + [vmem()] * 4,
        out_specs=vmem(),
        scratch_shapes=[pltpu.VMEM((CORES * CHIPS, rows, width), jnp.bfloat16)],
        compiler_params=params(16),
        name="cache_pages",
    )(page_table, *same, *other)


def join_kernel(*refs):
    pieces, out_ref = refs[:CHIPS], refs[CHIPS]
    for hop_by, piece in enumerate(pieces):

        @pl.when(place()[0] ^ hop_by == CHIPS - 1)
        def _(piece=piece):
            out_ref[...] = piece[...]


def join_call(pieces):
    return pl.pallas_call(
        join_kernel,
        out_shape=jax.ShapeDtypeStruct(pieces[0].shape, pieces[0].dtype),
        in_specs=[vmem()] * CHIPS,
        out_specs=vmem(),
        compiler_params=params(16),
        name="join_pages",
    )(*pieces)


def hold_kernel(in_ref, *refs):
    refs[-1][...] = in_ref[...]


def hold_call(value, *earlier):
    return pl.pallas_call(
        hold_kernel,
        out_shape=jax.ShapeDtypeStruct(value.shape, value.dtype),
        in_specs=[vmem()] + [anywhere()] * len(earlier),
        out_specs=vmem(),
        cost_estimate=LONG,
        compiler_params=params(16),
        name="hold",
    )(value, *earlier)


def after(value, other):
    return lax.optimization_barrier((value, other))[0]


def chip_body(
    tokens, segment_ids, page_table, attn_gain, w_qkv, w_out, moe_gain,
    route_ids, route_weight, w_gate, w_up, w_down,
):
    rows = tokens.shape[0]
    seq_size = lax.axis_size("seq")

    def chips(value, by):
        return hop(value, CORES * by)

    gate, up, down = w_gate[0], w_up[0], w_down[0]
    w_own = w_out.T

    tokens_x, tokens_y = chips(tokens, 1), chips(tokens, 2)
    w_qkv_other, gate_other = hop(w_qkv, 1), hop(gate, 1)
    tokens_xy = [chips(tokens_y[: rows // 2], 1), chips(tokens_x[rows // 2 :], 2)]
    late = project_call((tokens_x, tokens_y), attn_gain, w_qkv, w_qkv_other)
    made = project_call((tokens, *tokens_xy), attn_gain, w_qkv, w_qkv_other, late)
    projected = [
        made[:rows],
        hold_call(chips(late[:rows], 1)),
        hold_call(chips(late[rows:], 2)),
        chips(made[rows:], 3),
    ]
    up_other = hop(after(up, tokens_x), 1)

    own_kv = pack_call(
        after(projected, (gate_other, up_other)), segment_ids, route_ids, route_weight
    )
    prev_kv = lax.ppermute(own_kv, "seq", [(i, i + 1) for i in range(seq_size - 1)])
    w_going, down_going = after((w_own, down), own_kv)
    mine = after((made, late), own_kv)
    paged = cache_call(page_table, mine, [hop(kv, 1) for kv in mine])
    w_x, w_y = chips(w_going, 1), chips(w_going, 2)
    down_other, w_own_other = hop(down_going, 1), hop(w_going, 1)

    sent = choose_call(own_kv, after(prev_kv, (w_x, w_y, down_other, w_own_other)))
    kv_xy, kv_x, kv_y = chips(sent[2], 3), chips(sent[0], 1), chips(sent[1], 2)
    kv_xy = hold_call(kv_xy)
    half = w_own.shape[0] // 2
    w_relayed = [hold_call(w_y[:half], *sent), hold_call(w_x[half:], *sent)]
    w_diagonal = [chips(w_relayed[0], 1), chips(w_relayed[1], 2)]
    windows = [own_kv, kv_x, kv_y, kv_xy, prev_kv]
    windows_other = [hop(w, 1) for w in windows]
    w_other = [w_own_other] + [hop(after(w, sent), 1) for w in (w_x, w_y)]
    windows_other = after(windows_other, (w_other, w_relayed))
    context = after(attend_call(projected, windows + windows_other), w_diagonal)
    context_x, context_y = chips(context, 1), chips(context, 2)
    context_xy = [chips(context_y[: rows // 2], 1), chips(context_x[rows // 2 :], 2)]
    last = CHIPS - 1
    paged = after(paged, (context_x, context_y))
    pages = [paged[last]]
    for by in (1, 2, 3):
        pairs = [(last * CORES + k, (last ^ by) * CORES + k) for k in range(CORES)]
        pages.append(lax.ppermute(paged[last ^ by], "tensor", pairs))
    w_other += [hop(w, 1) for w in w_diagonal]
    w_all = assemble_call([w_own, w_x, w_y] + w_diagonal, w_other)

    weights = [gate, up, down, gate_other, up_other, down_other]
    out_x, out_y = expert_call(
        (context_x, context_y), (tokens_x, tokens_y), (kv_x, kv_y), w_all, moe_gain, weights,
        (jnp.bfloat16, jnp.bfloat16),
    )
    back_x, back_y = hold_call(chips(out_x, 1)), hold_call(chips(out_y, 2))
    out, out_xy = expert_call(
        (context, *context_xy), (tokens, *tokens_xy), (own_kv, kv_xy), w_all, moe_gain, weights,
        (jnp.float32, jnp.bfloat16), out_x, *pages[1:3],
    )
    back_xy = chips(out_xy, 3)
    pages = join_call(pages)
    mixed = mix_call((out, back_x, back_y, back_xy))
    return (mixed, pages.reshape(rows // PAGE, PAGE, pages.shape[1]))


def from_behind(value, axis, by):
    length = lax.axis_size(axis)
    pairs = [(i, i + by) for i in range(length) if 0 <= i + by < length]
    return lax.ppermute(value, axis, pairs)


def rms_scaled(values, scales):
    wide = values.astype(jnp.float32)
    mean_sq = jnp.mean(wide * wide, axis=-1, keepdims=True)
    return (wide * lax.rsqrt(mean_sq + epsilon) * scales).astype(jnp.bfloat16)


def attend(queries, keys_window, values_window, allowed):
    scores = jnp.einsum(
        "qhd,kd->hqk", queries, keys_window, preferred_element_type=jnp.float32
    ) / math.sqrt(queries.shape[-1])
    scores = jnp.where(allowed[None], scores, -jnp.inf)
    highest = jnp.max(scores, axis=-1, keepdims=True)
    weights = jnp.exp(scores - highest)
    totals = jnp.sum(weights, axis=-1, keepdims=True)
    shares = (weights / totals).astype(jnp.bfloat16)
    return jnp.einsum("hqk,kd->qhd", shares, values_window, preferred_element_type=jnp.float32)


def block_body(
    tokens,
    segment_ids,
    page_table,
    attn_gain,
    w_qkv,
    w_out,
    moe_gain,
    route_ids,
    route_weight,
    w_gate,
    w_up,
    w_down,
):
    tok_rows = tokens.shape[0]
    tensor_size = lax.axis_size("tensor")
    tensor_index = lax.axis_index("tensor")
    seq_index = lax.axis_index("seq")
    block_rows = tok_rows * tensor_size
    normed = rms_scaled(tokens, attn_gain)
    block_normed = lax.all_gather(normed, "tensor", axis=0, tiled=True)
    own_columns = jnp.dot(block_normed, w_qkv, preferred_element_type=jnp.float32).astype(
        jnp.bfloat16
    )
    projected = lax.all_to_all(own_columns, "tensor", split_axis=0, concat_axis=1, tiled=True)
    query_width = HEADS * HEAD
    queries = projected[:, :query_width].reshape(tok_rows, HEADS, HEAD)
    own_kv = projected[:, query_width:]
    block_kv, block_segs = (
        lax.all_gather(own_kv, "tensor", axis=0, tiled=True),
        lax.all_gather(segment_ids, "tensor", axis=0, tiled=True),
    )
    earlier_kv, earlier_seg_block = from_behind((block_kv, block_segs), "seq", 1)
    pages_here = tok_rows // PAGE
    pages_block = block_rows // PAGE
    slot_ids = tensor_index * pages_here + jnp.arange(pages_here, dtype=jnp.int32)
    matches = page_table[0][None, :] == slot_ids[:, None]
    logical = jnp.sum(
        jnp.where(matches, jnp.arange(pages_block, dtype=jnp.int32)[None, :], 0), axis=1
    )
    cache_pages = block_kv.reshape(pages_block, PAGE, block_kv.shape[1])[logical]
    all_kv = jnp.concatenate([earlier_kv, block_kv], axis=0)
    all_segs = jnp.concatenate([earlier_seg_block, block_segs], axis=0)
    window = block_rows + tok_rows
    first_key = tensor_index * tok_rows
    keys_window = lax.dynamic_slice_in_dim(all_kv, first_key, window, 0)
    segs_window = lax.dynamic_slice_in_dim(all_segs, first_key, window, 0)
    key_pos = (seq_index - 1) * block_rows + first_key + jnp.arange(window, dtype=jnp.int32)
    query_pos = seq_index * block_rows + first_key + jnp.arange(tok_rows, dtype=jnp.int32)
    allowed = (
        (segs_window[None, :] == segment_ids[:, None])
        & (key_pos[None, :] <= query_pos[:, None])
        & (key_pos[None, :] >= 0)
    )
    per_group = HEADS // KV_HEADS
    contexts = []
    for kv_group in range(KV_HEADS):
        key_cols = keys_window[:, kv_group * HEAD : (kv_group + 1) * HEAD]
        value_cols = keys_window[:, (KV_HEADS + kv_group) * HEAD : (KV_HEADS + kv_group + 1) * HEAD]
        contexts.append(
            attend(
                queries[:, kv_group * per_group : (kv_group + 1) * per_group],
                key_cols,
                value_cols,
                allowed,
            )
        )
    context = jnp.concatenate(contexts, axis=1).reshape(tok_rows, query_width).astype(jnp.bfloat16)
    attn_out = jnp.dot(
        context,
        lax.all_gather(w_out, "tensor", axis=1, tiled=True),
        preferred_element_type=jnp.float32,
    )
    residual = (tokens.astype(jnp.float32) + attn_out).astype(jnp.bfloat16)
    expert_input = rms_scaled(residual, moe_gain)
    experts_all = w_gate.shape[0] * tensor_size
    capacity = max(2, 3 * tok_rows * TOP // (2 * experts_all))
    flat_routes = route_ids.reshape(-1)
    expert_hits = (
        flat_routes[:, None] == jnp.arange(experts_all, dtype=jnp.int32)[None, :]
    ).astype(jnp.int32)
    earlier_hits = jnp.cumsum(expert_hits, axis=0) - expert_hits
    slot_rank = jnp.sum(earlier_hits * expert_hits, axis=1)
    dest_slot = flat_routes * capacity + slot_rank
    slot_table = (
        jnp.arange(experts_all * capacity, dtype=jnp.int32)[:, None, None]
        == dest_slot.reshape(tok_rows, TOP)[None]
    )
    dispatch = jnp.any(slot_table, axis=2).astype(jnp.bfloat16)
    outgoing = jnp.dot(dispatch, expert_input, preferred_element_type=jnp.float32).astype(
        jnp.bfloat16
    )
    outgoing = outgoing.reshape(experts_all, capacity, expert_input.shape[1])
    arrived = lax.all_to_all(outgoing, "tensor", split_axis=0, concat_axis=0, tiled=True)
    rows_flat = arrived.reshape(-1, arrived.shape[-1])
    gate_out = jnp.dot(rows_flat, w_gate[0], preferred_element_type=jnp.float32)
    up_out = jnp.dot(rows_flat, w_up[0], preferred_element_type=jnp.float32)
    hidden = (jnp.maximum(gate_out, 0.0) * up_out).astype(jnp.bfloat16)
    produced = jnp.dot(hidden, w_down[0], preferred_element_type=jnp.float32).astype(jnp.bfloat16)
    returned = lax.all_to_all(
        produced.reshape(arrived.shape), "tensor", split_axis=0, concat_axis=0, tiled=True
    )
    picked = returned.reshape(-1, returned.shape[-1])[dest_slot].reshape(
        tok_rows, TOP, returned.shape[-1]
    )
    routed_sum = jnp.einsum("tk,tkd->td", route_weight, picked.astype(jnp.float32))
    mixed = (residual.astype(jnp.float32) + routed_sum).astype(jnp.bfloat16)
    return (mixed, cache_pages)


def by_chips(mesh):
    size = mesh.shape["tensor"]
    return size == CORES * CHIPS and (HEADS + 2 * KV_HEADS) % size == 0


def solution(mesh):
    return jax.shard_map(
        chip_body if by_chips(mesh) else block_body,
        mesh=mesh,
        in_specs=(
            P(("seq", "tensor"), None),
            P(("seq", "tensor")),
            P("seq", None),
            P(),
            P(None, "tensor"),
            P(None, "tensor"),
            P(),
            P(("seq", "tensor"), None),
            P(("seq", "tensor"), None),
            P("tensor", None, None),
            P("tensor", None, None),
            P("tensor", None, None),
        ),
        out_specs=(P(("seq", "tensor"), None), P(("seq", "tensor"), None, None)),
        check_vma=False,
    )
```
